32 devices in a mesh: dp: 16 (over z, y, x), tensor: 2 (over core).
Axes of the slice: x: 2, y: 2, z: 4, core: 2. Of those that a mesh axis runs over, the one named last changes fastest.
Arguments:
- tokens: bfloat16 [8192, 2048], P(('dp', 'tensor')), may hold values from -6 to 6
- lengths: int32 [16], P('dp'), may hold values from 257 to 512, as said below
- w_query: bfloat16 [2048, 2048], P('dp', 'tensor'), may hold values from -0.125 to 0.125
- w_key: bfloat16 [2048, 2048], P('dp', 'tensor'), may hold values from -0.125 to 0.125
- w_value: bfloat16 [2048, 4096], P('dp', 'tensor'), may hold values from -0.125 to 0.125
- w_gate: bfloat16 [2048, 4096], P('dp', 'tensor'), may hold values from -0.125 to 0.125
- w_out: bfloat16 [4096, 2048], P('tensor', 'dp'), may hold values from -0.125 to 0.125
- w_ffgate: bfloat16 [2048, 4096], P('dp', 'tensor'), may hold values from -0.125 to 0.125
- w_ffup: bfloat16 [2048, 4096], P('dp', 'tensor'), may hold values from -0.125 to 0.125
- w_ffdown: bfloat16 [4096, 2048], P('tensor', 'dp'), may hold values from -0.125 to 0.125
- gain_attn: bfloat16 [2048], P('dp'), may hold values from 0.099609375 to 1.8984375
- gain_mlp: bfloat16 [2048], P('dp'), may hold values from 0.099609375 to 1.8984375
- cotangent: bfloat16 [8192, 2048], P(('dp', 'tensor')), may hold values from -6 to 6
Outputs:
- output: bfloat16 [8192, 2048], P(('dp', 'tensor'))
- tokens_grad: bfloat16 [8192, 2048], P(('dp', 'tensor'))
- grad_query: float32 [2048, 2048], P('dp', 'tensor')
- grad_key: float32 [2048, 2048], P('dp', 'tensor')
- grad_value: float32 [2048, 4096], P('dp', 'tensor')
- gate_weight_gradient: float32 [2048, 4096], P('dp', 'tensor')
- grad_out: float32 [4096, 2048], P('tensor', 'dp')
- grad_ffgate: float32 [2048, 4096], P('dp', 'tensor')
- grad_ffup: float32 [2048, 4096], P('dp', 'tensor')
- grad_ffdown: float32 [4096, 2048], P('tensor', 'dp')
- grad_gain_attn: float32 [2048], P(('dp', 'tensor'))
- grad_gain_mlp: float32 [2048], P(('dp', 'tensor'))
The draws below stay inside these ranges and needn't reach their ends.
Inputs may be any that keep to these rules, and one draw needn't show every extreme that they name: `lengths`: one slot of every draw is full; each slot is used past its middle.
All inputs are finite; a program needn't handle non-finite values.
Results may differ from the reference program's by a relative error of at most 0.015.
The reference program's roundings to bfloat16 on the way count: a program that leaves them out, or rounds other values in their place, can miss the bound.
Values may be sent and summed in bfloat16 or wider, within the bound.
No kernel may reach another device: no remote copies, remote signals or barrier semaphores. Data moves between devices by JAX's collectives and lax.ppermute only.
A program may use at most 256 MiB of HBM per device.

```python
import math
import jax
import jax.numpy as jnp
from jax import lax

D = 2048
HEADS = 8
DK = 256
DV = 512
FF = 4096
SLOT = 512
SLOTS = 16
TOKENS = 8192
QK = 2048
VD = 4096


def draw_lengths(key, part):
    key = jax.random.fold_in(key, 7)
    first_key, second_key = jax.random.split(key)
    drawn = jax.random.randint(first_key, (SLOTS,), SLOT // 2 + 1, SLOT + 1)
    chosen = jax.random.randint(second_key, (), 0, SLOTS)
    return jnp.where(jnp.arange(SLOTS) == chosen, SLOT, drawn).astype(jnp.int32)


def steps_of(rng, extent, cuts, smallest, high):
    level = 1.0
    for axis_at, parts in cuts:
        draws = jax.random.uniform(jax.random.fold_in(jax.random.fold_in(rng, 6), axis_at), (parts,), jnp.float32, smallest / len(cuts), high / len(cuts))
        level = level * jnp.repeat(jnp.exp(draws), extent[axis_at] // parts).reshape((-1,) + (1,) * (len(extent) - 1 - axis_at))
    return level


def centred(stream_key, shape, width, reach, cuts=(), kind=jnp.bfloat16):
    factor_of = steps_of(stream_key, shape, cuts, -0.22, 0.18) if cuts else 1.0
    values = jax.random.normal(stream_key, shape, jnp.float32) * width * factor_of
    return jnp.minimum(jnp.maximum(values, -reach), reach).astype(kind)


def setup_inputs(seed: int = 0) -> dict:
    keys = jax.random.split(jax.random.key(seed), 14)
    tokens = centred(keys[0], (TOKENS, D), 1.0, 6.0, ((0, 32),))
    lengths = draw_lengths(jax.random.fold_in(keys[13], 71), 0)
    w_query = centred(keys[2], (D, QK), D ** -0.5, 0.125, ((0, 16), (1, 2)))
    w_key = centred(keys[3], (D, QK), D ** -0.5, 0.125, ((0, 16), (1, 2)))
    w_value = centred(keys[4], (D, VD), D ** -0.5, 0.125, ((0, 16), (1, 2)))
    w_gate = centred(keys[5], (D, VD), D ** -0.5, 0.125, ((0, 16), (1, 2)))
    w_out = centred(keys[6], (VD, D), (VD // 2) ** -0.5, 0.125, ((0, 2), (1, 16)))
    w_ffgate = centred(keys[7], (D, FF), D ** -0.5, 0.125, ((0, 16), (1, 2)))
    w_ffup = centred(keys[8], (D, FF), D ** -0.5, 0.125, ((0, 16), (1, 2)))
    w_ffdown = centred(keys[9], (FF, D), (FF // 2) ** -0.5, 0.125, ((0, 2), (1, 16)))
    gain_attn = jnp.clip(1.0 + 0.18 * jax.random.normal(keys[10], (D,), jnp.float32), 0.099609375, 1.8984375).astype(jnp.bfloat16)
    gain_mlp = jnp.clip(1.0 + 0.18 * jax.random.normal(keys[11], (D,), jnp.float32), 0.099609375, 1.8984375).astype(jnp.bfloat16)
    cotangent = centred(keys[12], (TOKENS, D), 1.0, 6.0, ((0, 32),))
    return {"tokens": tokens, "lengths": lengths, "w_query": w_query, "w_key": w_key, "w_value": w_value, "w_gate": w_gate, "w_out": w_out, "w_ffgate": w_ffgate, "w_ffup": w_ffup, "w_ffdown": w_ffdown, "gain_attn": gain_attn, "gain_mlp": gain_mlp, "cotangent": cotangent}


@jax.custom_vjp
def low(v):
    return lax.optimization_barrier(v.astype(jnp.bfloat16)).astype(jnp.float32)

@jax.custom_vjp
def low_back(v):
    return v

def low_keep(v):
    return (low(v), None)

def low_pass(kept, grad):
    return (grad,)

def back_keep(v):
    return (v, None)

def back_low(kept, grad):
    return (low(grad),)
low.defvjp(low_keep, low_pass)
low_back.defvjp(back_keep, back_low)
norm_eps = 1e-06
group_floor = 1.0
exact_mode = lax.Precision.HIGHEST

def rms_scale(rows, gain):
    factor = lax.rsqrt(lax.optimization_barrier(jnp.mean(rows * rows, axis=-1, keepdims=True)) + norm_eps)
    return rows * factor * gain

def decay_table(count, heads, first_head):
    positions = jnp.arange(count, dtype=jnp.int32)
    spacing = (positions[:, None] - positions[None, :]).astype(jnp.int32)
    head_ids = (jnp.arange(heads, dtype=jnp.int32) + first_head).astype(jnp.float32)
    log_rates = jnp.log1p(-jnp.exp2(-5.0 - head_ids))
    kept_spacing = jnp.where(spacing >= 0, spacing, jnp.zeros_like(spacing)).astype(jnp.float32)
    powers = jnp.exp(kept_spacing[None] * log_rates[:, None, None])
    return jnp.where(spacing[None] >= 0, powers, jnp.zeros_like(powers))

def matmul(left, right):
    return jnp.dot(left, right, precision=exact_mode)

def layer_rows(rows, params, valid_rows, decays):
    w_query, w_key, w_value, w_gate, w_out, w_ffgate, w_ffup, w_ffdown, gain_attn, gain_mlp = params
    group = valid_rows.shape[0]
    normed_attn = low(rms_scale(rows, gain_attn))
    query_matrix = low(low_back(matmul(normed_attn, w_query))).reshape(group, SLOT, HEADS, DK)
    key_matrix_rows = low(low_back(matmul(normed_attn, w_key))).reshape(group, SLOT, HEADS, DK)
    value_rows = low(low_back(matmul(normed_attn, w_value))).reshape(group, SLOT, HEADS, DV)
    gate_pre = low_back(matmul(normed_attn, w_gate))
    unscaled_scores = low_back(jnp.einsum('snhd,smhd->shnm', query_matrix, key_matrix_rows, precision=exact_mode))
    scores = low(unscaled_scores * decays[None])
    retained = low_back(jnp.einsum('shnm,smhe->snhe', scores, value_rows, precision=exact_mode))
    normed = retained * lax.rsqrt(lax.optimization_barrier(jnp.mean(retained * retained, axis=-1, keepdims=True)) + group_floor)
    gated_rows = low(jax.nn.silu(gate_pre) * normed.reshape(group * SLOT, VD))
    hidden = rows + low_back(matmul(gated_rows, w_out))
    normed_mlp = low(rms_scale(hidden, gain_mlp))
    gate_up = low_back(matmul(normed_mlp, w_ffgate))
    value_up = low_back(matmul(normed_mlp, w_ffup))
    inner_act = low(jax.nn.gelu(gate_up, approximate=True) * value_up)
    mlp_rows = low_back(matmul(inner_act, w_ffdown))
    return valid_rows.reshape(group * SLOT, 1) * (hidden + mlp_rows)

def reference(tokens, lengths, w_query, w_key, w_value, w_gate, w_out, w_ffgate, w_ffup, w_ffdown, gain_attn, gain_mlp, cotangent):
    weights = tuple((weight.astype(jnp.float32) for weight in (w_query, w_key, w_value, w_gate, w_out, w_ffgate, w_ffup, w_ffdown, gain_attn, gain_mlp)))
    group = math.gcd(SLOTS, max(1, 4096 // SLOT))
    blocks = SLOTS // group
    positions = jnp.arange(SLOT, dtype=jnp.int32)
    valid = (positions[None, :] < lengths.astype(jnp.int32)[:, None]).astype(jnp.float32)
    decays = decay_table(SLOT, HEADS, 0)
    token_blocks = tokens.astype(jnp.float32).reshape(blocks, group * SLOT, D)
    cot_blocks = cotangent.astype(jnp.float32).reshape(blocks, group * SLOT, D)
    valid_blocks = valid.reshape(blocks, group, SLOT)

    def one_block(totals, block):
        token_block, valid_block, cot_block = block

        def forward(rows, params):
            return layer_rows(rows, params, valid_block, decays)
        result, pullback = jax.vjp(forward, token_block, weights)
        grad_rows, grad_params = pullback(cot_block)
        totals = tuple((left + right for left, right in zip(totals, grad_params)))
        return (totals, (result.astype(jnp.bfloat16), grad_rows.astype(jnp.bfloat16)))
    zeros = tuple((jnp.zeros_like(weight) for weight in weights))
    totals, (results, grads) = lax.scan(one_block, zeros, (token_blocks, valid_blocks, cot_blocks))
    return (results.reshape(TOKENS, D), grads.reshape(TOKENS, D), totals[0], totals[1], totals[2], totals[3], totals[4], totals[5], totals[6], totals[7], totals[8], totals[9])
```

```python
import jax
import jax.numpy as jnp
from jax import lax
from jax.sharding import PartitionSpec as P

DK = 256
DV = 512
PLANE = 4

norm_eps = 1e-06
group_floor = 1.0

bf16 = jnp.bfloat16
f32 = jnp.float32


def decay_table(positions, head):
    spacing = positions[:, None] - positions[None, :]
    log_rate = jnp.log1p(-jnp.exp2(-5.0 - head.astype(f32)))
    kept_spacing = jnp.where(spacing >= 0, spacing, jnp.zeros_like(spacing)).astype(f32)
    powers = jnp.exp(kept_spacing * log_rate)
    return jnp.where(spacing >= 0, powers, jnp.zeros_like(powers))


def dot(left, right):
    return jnp.dot(left, right, preferred_element_type=f32)


def dot_nt(left, right):
    return lax.dot_general(left, right, (((1,), (1,)), ((), ())), preferred_element_type=f32)


def dot_tn(left, right):
    return lax.dot_general(left, right, (((0,), (0,)), ((), ())), preferred_element_type=f32)


def hop(value, bits, count):
    return lax.ppermute(value, "dp", [(i, i ^ bits) for i in range(count)])


def swap(value):
    return lax.ppermute(value, "tensor", [(0, 1), (1, 0)])


def natural(blocks, me):
    stacked = jnp.stack(blocks)
    return [lax.dynamic_index_in_dim(stacked, me ^ j, 0, keepdims=False) for j in range(PLANE)]


def plane_gather(mine, count):
    half = mine.shape[0] // 2
    from_x = hop(mine, 1, count)
    from_y = hop(mine, 2, count)
    far_a = hop(from_x[:half], 2, count)
    far_b = hop(from_y[half:], 1, count)
    return [mine, from_x, from_y, jnp.concatenate([far_a, far_b])]


def spread(mine, count):
    blocks = plane_gather(mine, count)
    near = jnp.stack(blocks)
    other = swap(near)
    return jnp.stack([near, other], axis=1).reshape(8 * mine.shape[0], mine.shape[1])


def fold(terms, rows, count):
    parts = terms.reshape(PLANE, 2, rows, terms.shape[1])
    arrived = swap(parts[:, 1].astype(bf16))
    mine = parts[:, 0] + arrived.astype(f32)
    half = rows // 2
    first, second = mine[:, :half], mine[:, half:]
    from_x = hop(jnp.stack([first[1], first[3]]).astype(bf16), 1, count).astype(f32)
    from_y = hop(jnp.stack([second[2], second[3]]).astype(bf16), 2, count).astype(f32)
    last_y = hop((first[2] + from_x[1]).astype(bf16), 2, count).astype(f32)
    last_x = hop((second[1] + from_y[1]).astype(bf16), 1, count).astype(f32)
    return jnp.concatenate([first[0] + from_x[0] + last_y, second[0] + from_y[0] + last_x])


def on_device(
    tokens,
    lengths,
    w_query,
    w_key,
    w_value,
    w_gate,
    w_out,
    w_ffgate,
    w_ffup,
    w_ffdown,
    gain_attn,
    gain_mlp,
    cotangent,
):
    count = lax.axis_size("dp")
    depth = count // PLANE
    columns = [[q + PLANE * z for z in range(depth)] for q in range(PLANE)]
    place = lax.axis_index("dp")
    me = place % PLANE
    core = lax.axis_index("tensor")
    rows, width = tokens.shape
    shard = w_query.shape[0]

    gains = jnp.stack([gain_attn, gain_mlp])[None]
    step = 1
    while step < count:
        gains = jnp.concatenate([gains, hop(gains, step, count)])
        step *= 2
    order = place ^ jnp.arange(count)
    gains = jnp.take(gains, order, axis=0).astype(f32)
    gain_first = gains[:, 0].reshape(1, width)
    gain_second = gains[:, 1].reshape(1, width)

    def cut_columns(weight):
        part = weight.shape[1] // PLANE
        return [lax.dynamic_slice_in_dim(weight, (me ^ k) * part, part, 1) for k in range(PLANE)]

    def cut_rows(weight):
        part = weight.shape[0] // PLANE
        return [lax.dynamic_slice_in_dim(weight, (me ^ k) * part, part, 0) for k in range(PLANE)]

    def gather_depth(block):
        return lax.all_gather(block, "dp", axis=0, tiled=False, axis_index_groups=columns)

    wide = [cut_columns(w) for w in (w_query, w_key, w_value, w_gate)]
    wide_cuts = [jnp.concatenate([w[k] for w in wide], axis=1) for k in range(PLANE)]
    wide_blocks = [wide_cuts[0]] + [hop(wide_cuts[k], k, count) for k in range(1, PLANE)]
    out_cuts = cut_rows(w_out)
    out_blocks = [out_cuts[0]] + [hop(out_cuts[k], k, count) for k in range(1, PLANE)]
    ff = [cut_columns(w) for w in (w_ffgate, w_ffup)]
    ff_cuts = [jnp.concatenate([w[k] for w in ff], axis=1) for k in range(PLANE)]
    ff_blocks = [ff_cuts[0]] + [hop(ff_cuts[k], k, count) for k in range(1, PLANE)]
    down_cuts = cut_rows(w_ffdown)
    down_blocks = [down_cuts[0]] + [hop(down_cuts[k], k, count) for k in range(1, PLANE)]

    def full_columns(blocks):
        block = jnp.concatenate(natural(blocks, me), axis=0)
        return gather_depth(block).reshape(width, block.shape[1])

    def full_rows(blocks):
        block = jnp.concatenate(natural(blocks, me), axis=1)
        gathered = gather_depth(block)
        return jnp.moveaxis(gathered, 0, 1).reshape(block.shape[0], width)

    wide_full = full_columns(wide_blocks)
    out_full = full_rows(out_blocks)
    ff_full = full_columns(ff_blocks)
    down_full = full_rows(down_blocks)
    key_cols = w_query.shape[1] // PLANE
    value_cols = w_value.shape[1] // PLANE
    heads = key_cols // DK
    assert heads == 1
    inner = w_ffgate.shape[1] // PLANE

    input_rows = tokens.astype(f32)
    first_scale = lax.rsqrt(jnp.mean(input_rows * input_rows, axis=-1, keepdims=True) + norm_eps)
    normed_attn = (input_rows * first_scale * gain_first).astype(bf16)
    attn_all = spread(normed_attn, count)
    total = attn_all.shape[0]
    slot_len = 2 * rows

    query_key = dot(attn_all, wide_full[:, : 2 * key_cols]).astype(bf16)
    query = query_key[:, :key_cols].reshape(PLANE, slot_len, key_cols)
    key = query_key[:, key_cols:].reshape(PLANE, slot_len, key_cols)
    value = dot(attn_all, wide_full[:, 2 * key_cols : 2 * key_cols + value_cols]).astype(bf16)
    value = value.reshape(PLANE, slot_len, value_cols)
    gate_pre = dot(attn_all, wide_full[:, 2 * key_cols + value_cols :])

    local = jnp.arange(rows, dtype=jnp.int32)
    positions = jnp.concatenate([core * rows + local, (1 - core) * rows + local])
    decays = decay_table(positions, core * PLANE + me)
    scores = jnp.einsum("snd,smd->snm", query, key, preferred_element_type=f32)
    scores = (scores * decays).astype(bf16)
    retained = jnp.einsum("snm,sme->sne", scores, value, preferred_element_type=f32)
    retained = retained.reshape(total, value_cols)
    group_scale = lax.rsqrt(jnp.mean(retained * retained, axis=-1, keepdims=True) + group_floor)
    normed = retained * group_scale
    sigma = jax.nn.sigmoid(gate_pre)
    gated = (gate_pre * sigma * normed).astype(bf16)
    hidden = input_rows + fold(dot(gated, out_full), rows, count)

    second_scale = lax.rsqrt(jnp.mean(hidden * hidden, axis=-1, keepdims=True) + norm_eps)
    normed_mlp = (hidden * second_scale * gain_second).astype(bf16)
    mlp_all = spread(normed_mlp, count)
    up = dot(mlp_all, ff_full)
    gate_up, value_up = up[:, :inner], up[:, inner:]
    gelu, gelu_back = jax.vjp(lambda u: jax.nn.gelu(u, approximate=True), gate_up)
    inner_act = (gelu * value_up).astype(bf16)
    valid_rows = ((core * rows + local) < lengths[0]).astype(f32)[:, None]
    mlp_rows = fold(dot(inner_act, down_full), rows, count)
    output = (valid_rows * (hidden + mlp_rows)).astype(bf16)

    back_rows = valid_rows * cotangent.astype(f32)
    back_all = spread(back_rows.astype(bf16), count)
    grad_down = dot_tn(inner_act, back_all).astype(bf16)
    grad_inner = dot_nt(back_all, down_full)
    grad_gate_up = gelu_back(grad_inner * value_up)[0].astype(bf16)
    grad_value_up = (grad_inner * gelu).astype(bf16)
    grad_up = jnp.concatenate([grad_gate_up, grad_value_up], axis=1)
    grad_ff = dot_tn(mlp_all, grad_up).astype(bf16)
    grad_normed = fold(dot_nt(grad_up, ff_full), rows, count)
    gain_term_mlp = jnp.sum(grad_normed * hidden * second_scale, axis=0)
    scaled = grad_normed * gain_second
    grad_hidden = back_rows + second_scale * (
        scaled
        - hidden * (second_scale * second_scale) * jnp.mean(hidden * scaled, axis=-1, keepdims=True)
    )

    attn_grad_all = spread(grad_hidden.astype(bf16), count)
    grad_out = dot_tn(gated, attn_grad_all).astype(bf16)
    grad_gated = dot_nt(attn_grad_all, out_full)
    grad_gate_pre = (
        grad_gated * normed * (sigma * (1.0 + gate_pre * (1.0 - sigma)))
    ).astype(bf16)
    grad_normed_head = grad_gated * (gate_pre * sigma)
    grad_retained = (
        group_scale
        * (
            grad_normed_head
            - normed * group_scale * jnp.mean(retained * grad_normed_head, axis=-1, keepdims=True)
        )
    ).astype(bf16)
    grad_retained = grad_retained.reshape(PLANE, slot_len, value_cols)
    grad_scores = jnp.einsum("sne,sme->snm", grad_retained, value, preferred_element_type=f32)
    grad_scores = (grad_scores * decays).astype(bf16)
    grad_query = jnp.einsum("snm,smd->snd", grad_scores, key, preferred_element_type=f32)
    grad_key = jnp.einsum("snm,snd->smd", grad_scores, query, preferred_element_type=f32)
    grad_value = jnp.einsum("snm,sne->sme", scores, grad_retained, preferred_element_type=f32)
    grad_wide = jnp.concatenate(
        [
            grad_query.astype(bf16).reshape(total, key_cols),
            grad_key.astype(bf16).reshape(total, key_cols),
            grad_value.astype(bf16).reshape(total, value_cols),
            grad_gate_pre,
        ],
        axis=1,
    )
    grad_wide_weights = dot_tn(attn_all, grad_wide).astype(bf16)
    grad_normed_attn = fold(dot_nt(grad_wide, wide_full), rows, count)
    gain_term_attn = jnp.sum(grad_normed_attn * input_rows * first_scale, axis=0)
    scaled_first = grad_normed_attn * gain_first
    tokens_grad = grad_hidden + first_scale * (
        scaled_first
        - input_rows
        * (first_scale * first_scale)
        * jnp.mean(input_rows * scaled_first, axis=-1, keepdims=True)
    )
    tokens_grad = tokens_grad.astype(bf16)

    def sum_depth(block):
        return lax.psum_scatter(
            block, "dp", scatter_dimension=0, tiled=True, axis_index_groups=columns
        )

    def back_columns(block):
        cuts = [lax.dynamic_slice_in_dim(block, (me ^ k) * shard, shard, 0) for k in range(PLANE)]
        blocks = [cuts[0]] + [hop(cuts[k], k, count) for k in range(1, PLANE)]
        return natural(blocks, me)

    def back_rows_of(block):
        cuts = [lax.dynamic_slice_in_dim(block, (me ^ k) * shard, shard, 1) for k in range(PLANE)]
        blocks = [cuts[0]] + [hop(cuts[k], k, count) for k in range(1, PLANE)]
        return jnp.concatenate(natural(blocks, me), axis=0).astype(f32)

    def depth_first(block):
        cut = block.reshape(block.shape[0], depth, width // depth)
        return jnp.moveaxis(cut, 1, 0).reshape(depth * block.shape[0], width // depth)

    down_sum = back_rows_of(sum_depth(depth_first(grad_down)))
    ff_sums = back_columns(sum_depth(grad_ff))
    ffgate_sum = jnp.concatenate([b[:, :inner] for b in ff_sums], axis=1).astype(f32)
    ffup_sum = jnp.concatenate([b[:, inner:] for b in ff_sums], axis=1).astype(f32)
    out_sum = back_rows_of(sum_depth(depth_first(grad_out)))
    wide_sums = back_columns(sum_depth(grad_wide_weights))
    edges = (0, key_cols, 2 * key_cols, 2 * key_cols + value_cols, 2 * key_cols + 2 * value_cols)
    wide_out = [
        jnp.concatenate([b[:, lo:hi] for b in wide_sums], axis=1).astype(f32)
        for lo, hi in zip(edges[:-1], edges[1:])
    ]

    gain_terms = jnp.stack([gain_term_attn, gain_term_mlp])
    bit = count // 2
    while bit >= 1:
        side = (place // bit) % 2
        cut = gain_terms.reshape(2, 2, -1)
        kept = lax.dynamic_index_in_dim(cut, side, 1, keepdims=False)
        sent = lax.dynamic_index_in_dim(cut, 1 - side, 1, keepdims=False)
        gain_terms = kept + hop(sent, bit, count)
        bit //= 2
    cut = gain_terms.reshape(2, 2, -1)
    kept = lax.dynamic_index_in_dim(cut, core, 1, keepdims=False)
    sent = lax.dynamic_index_in_dim(cut, 1 - core, 1, keepdims=False)
    gain_terms = kept + swap(sent)

    return (
        output,
        tokens_grad,
        wide_out[0],
        wide_out[1],
        wide_out[2],
        wide_out[3],
        out_sum,
        ffgate_sum,
        ffup_sum,
        down_sum,
        gain_terms[0],
        gain_terms[1],
    )


def solution(mesh):
    return jax.shard_map(
        on_device,
        mesh=mesh,
        in_specs=(
            P(("dp", "tensor"), None),
            P("dp"),
            P("dp", "tensor"),
            P("dp", "tensor"),
            P("dp", "tensor"),
            P("dp", "tensor"),
            P("tensor", "dp"),
            P("dp", "tensor"),
            P("dp", "tensor"),
            P("tensor", "dp"),
            P("dp"),
            P("dp"),
            P(("dp", "tensor"), None),
        ),
        out_specs=(
            P(("dp", "tensor"), None),
            P(("dp", "tensor"), None),
            P("dp", "tensor"),
            P("dp", "tensor"),
            P("dp", "tensor"),
            P("dp", "tensor"),
            P("tensor", "dp"),
            P("dp", "tensor"),
            P("dp", "tensor"),
            P("tensor", "dp"),
            P(("dp", "tensor")),
            P(("dp", "tensor")),
        ),
        check_vma=False,
    )
```

```python
import functools

import jax
import jax.numpy as jnp
from jax import lax
from jax.experimental import pallas as pl
from jax.experimental.pallas import tpu as pltpu
from jax.sharding import PartitionSpec as P

DK = 256
DV = 512
PLANE = 4
VMEM_BYTES = 56 * 1024 * 1024

norm_eps = 1e-06
group_floor = 1.0
tanh_scale = 0.7978845608028654
tanh_cubic = 0.044715

bf16 = jnp.bfloat16
f32 = jnp.float32


def shaped(shape, kind):
    return jax.ShapeDtypeStruct(shape, kind)


def cost(flops, bytes_accessed):
    return pl.CostEstimate(flops=int(flops), bytes_accessed=int(bytes_accessed), transcendentals=0)


def params():
    return pltpu.CompilerParams(vmem_limit_bytes=VMEM_BYTES)


ANY = pl.BlockSpec(memory_space=pl.ANY)


def whole(shape):
    return pl.BlockSpec(shape, lambda i: (0,) * len(shape), pipeline_mode=pl.Buffered(1))


def by_slot(*shape):
    return pl.BlockSpec(shape, lambda i: (i,) + (0,) * (len(shape) - 1))


def dot(left, right):
    return jnp.dot(left, right, preferred_element_type=f32)


def dot_nt(left, right):
    return lax.dot_general(left, right, (((1,), (1,)), ((), ())), preferred_element_type=f32)


def dot_tn(left, right):
    return lax.dot_general(left, right, (((0,), (0,)), ((), ())), preferred_element_type=f32)


def decay_table(positions, head):
    spacing = positions[:, None] - positions[None, :]
    log_rate = jnp.log1p(-jnp.exp2(-5.0 - head.astype(f32)))
    kept_spacing = jnp.where(spacing >= 0, spacing, jnp.zeros_like(spacing)).astype(f32)
    powers = jnp.exp(kept_spacing * log_rate)
    return jnp.where(spacing >= 0, powers, jnp.zeros_like(powers))


def copy_kernel(plan, n_in, me_ref, *refs):
    ins, outs, sem = refs[:n_in], refs[n_in:-1], refs[-1]
    copies = [
        pltpu.make_async_copy(source, target, sem.at[i])
        for i, (source, target) in enumerate(plan(me_ref[0], ins, outs))
    ]
    for one in copies:
        one.start()
    for one in copies:
        one.wait()


def place_copies(plan, n_copies, me, ins, out_shapes):
    moved = 2 * sum(2 * s.size for s in out_shapes)
    return pl.pallas_call(
        functools.partial(copy_kernel, plan, len(ins)),
        in_specs=[pl.BlockSpec(memory_space=pltpu.SMEM)] + [pl.BlockSpec(memory_space=pltpu.VMEM)] * len(ins),
        out_specs=[ANY] * len(out_shapes),
        out_shape=out_shapes,
        scratch_shapes=[pltpu.SemaphoreType.DMA((n_copies,))],
        compiler_params=params(),
        cost_estimate=cost(0, moved),
    )(me, *ins)


def lanes(index, size):
    return pl.ds(pl.multiple_of(index * size, size), size)


def cut_columns(me, weights):
    rows = weights[0].shape[0]
    parts = [w.shape[1] // PLANE for w in weights]

    def plan(place, ins, outs):
        copies = []
        for k in range(PLANE):
            at = 0
            for w, part in zip(ins, parts):
                copies.append((w.at[:, lanes(place ^ k, part)], outs[k].at[:, pl.ds(at, part)]))
                at += part
        return copies

    shapes = [shaped((rows, sum(parts)), bf16)] * PLANE
    return place_copies(plan, PLANE * len(parts), me, weights, shapes)


def cut_rows(me, weight):
    depth = weight.shape[0] // PLANE
    place = me[0]
    return [lax.dynamic_slice_in_dim(weight, (place ^ k) * depth, depth, 0) for k in range(PLANE)]


def in_order(blocks, place, axis):
    stacked = jnp.stack(blocks)
    return jnp.concatenate(
        [lax.dynamic_index_in_dim(stacked, place ^ j, 0, keepdims=False) for j in range(PLANE)], axis
    )


def join_weights(me, column_blocks, row_blocks):
    rows, width = column_blocks[0].shape if column_blocks else (row_blocks[0].shape[1], 0)
    tall = PLANE * rows
    if not row_blocks:
        groups, extra = 0, []
    else:
        inner, cols = row_blocks[0].shape
        groups = inner // tall
        aligned = cols % 128 == 0
        extra = row_blocks if aligned else [in_order(row_blocks, me[0], 1)]

    def plan(place, ins, outs):
        copies = []
        for k in range(PLANE):
            if column_blocks:
                copies.append((ins[k], outs[0].at[lanes(place ^ k, rows), pl.ds(0, width)]))
        for k, block in enumerate(ins[len(column_blocks) :]):
            for g in range(groups):
                at = width + g * tall
                if aligned:
                    spot = pl.ds(pl.multiple_of(at + (place ^ k) * cols, cols), cols)
                else:
                    spot = pl.ds(at, tall)
                copies.append((block.at[pl.ds(g * tall, tall)], outs[0].at[:, spot]))
        return copies

    n_copies = len(column_blocks) + len(extra) * groups
    shape = shaped((tall, width + groups * tall), bf16)
    return place_copies(plan, n_copies, me, [*column_blocks, *extra], [shape])[0]


def load_pieces(pieces, held, sem):
    step = pl.program_id(0)
    rows = pieces[0].shape[0]
    copies = [
        pltpu.make_async_copy(piece, held.at[i // 2, pl.ds((i % 2) * rows, rows)], sem.at[i])
        for i, piece in enumerate(pieces)
    ]

    @pl.when(step == 0)
    def start():
        for one in copies:
            one.start()

    for s in range(len(pieces) // 2):

        @pl.when(step == s)
        def arrive(s=s):
            copies[2 * s].wait()
            copies[2 * s + 1].wait()

    return held[step]


def retain_kernel(*refs):
    pieces, (weights, decays) = refs[:8], refs[8:10]
    query_ref, key_ref, value_ref, scores_ref, retained_ref, rows_ref = refs[10:16]
    held, sem, out_sem = refs[16:]
    rows = load_pieces(pieces, held, sem)
    step = pl.program_id(0)
    slot_len = rows.shape[0]
    keep = pltpu.make_async_copy(held.at[step], rows_ref.at[pl.ds(step * slot_len, slot_len)], out_sem)
    keep.start()
    dk, dv = query_ref.shape[1], value_ref.shape[1]
    query_key = dot(rows, weights[:, : 2 * dk]).astype(bf16)
    query, key = query_key[:, :dk], query_key[:, dk:]
    query_ref[...] = query
    key_ref[...] = key
    scores = (dot_nt(query, key) * decays[...]).astype(bf16)
    scores_ref[...] = scores[None]
    value = dot(rows, weights[:, 2 * dk : 2 * dk + dv]).astype(bf16)
    value_ref[...] = value
    retained_ref[...] = dot(scores, value)
    keep.wait()


def retain(pieces, weights, decays, dk, dv):
    rows, width = pieces[0].shape
    slot_len = 2 * rows
    total = PLANE * slot_len
    return pl.pallas_call(
        retain_kernel,
        grid=(PLANE,),
        in_specs=[ANY] * 8 + [whole((width, 2 * dk + dv)), whole((slot_len, slot_len))],
        out_specs=[
            by_slot(slot_len, dk),
            by_slot(slot_len, dk),
            by_slot(slot_len, dv),
            by_slot(1, slot_len, slot_len),
            by_slot(slot_len, dv),
            ANY,
        ],
        out_shape=[
            shaped((total, dk), bf16),
            shaped((total, dk), bf16),
            shaped((total, dv), bf16),
            shaped((PLANE, slot_len, slot_len), bf16),
            shaped((total, dv), f32),
            shaped((total, width), bf16),
        ],
        scratch_shapes=[
            pltpu.VMEM((PLANE, slot_len, width), bf16),
            pltpu.SemaphoreType.DMA((8,)),
            pltpu.SemaphoreType.DMA,
        ],
        compiler_params=params(),
        cost_estimate=cost(2.2 * total * width * (2 * dk + dv), 30e6),
    )(*pieces, weights, decays)


def times_rows(left, right, wide):
    groups = right.shape[1] // wide
    for z in range(right.shape[0] // wide):
        terms = dot(left[:, :wide], right[z * wide : (z + 1) * wide, :wide])
        for g in range(1, groups):
            terms += dot(
                left[:, g * wide : (g + 1) * wide],
                right[z * wide : (z + 1) * wide, g * wide : (g + 1) * wide],
            )
        yield slice(z * wide, (z + 1) * wide), terms


def times_rows_back(left, right, wide):
    made = []
    for g in range(right.shape[1] // wide):
        group = slice(g * wide, (g + 1) * wide)
        terms = dot_nt(left[:, :wide], right[:wide, group])
        for z in range(1, right.shape[0] // wide):
            block = slice(z * wide, (z + 1) * wide)
            terms += dot_nt(left[:, block], right[block, group])
        made.append(terms)
    return made[0] if len(made) == 1 else jnp.concatenate(made, axis=1)


def split_out(terms, near_ref, far_ref, columns):
    rows = near_ref.shape[1]
    near_ref[0, :, columns] = terms[:rows]
    far_ref[0, :, columns] = terms[rows:].astype(bf16)


def gate_out_kernel(wide, rows_ref, weights, out_weights, retained_ref, gate_ref, gated_ref, near_ref, far_ref):
    retained = retained_ref[...]
    scale = lax.rsqrt(jnp.mean(retained * retained, axis=-1, keepdims=True) + group_floor)
    gate = dot(rows_ref[...], weights[...])
    gate_ref[...] = gate
    gated_ref[...] = (gate * jax.nn.sigmoid(gate) * (retained * scale)).astype(bf16)
    for columns, terms in times_rows(gated_ref[...], out_weights[...], wide):
        split_out(terms, near_ref, far_ref, columns)


def gate_out(rows_all, joined, retained, wide):
    total, width = rows_all.shape
    dv = retained.shape[1]
    slot_len = total // PLANE
    rows = slot_len // 2
    return pl.pallas_call(
        functools.partial(gate_out_kernel, wide),
        grid=(PLANE,),
        in_specs=[
            by_slot(slot_len, width),
            pl.BlockSpec((width, dv), lambda i: (0, 2), pipeline_mode=pl.Buffered(1)),
            pl.BlockSpec((width, dv), lambda i: (0, 3), pipeline_mode=pl.Buffered(1)),
            by_slot(slot_len, dv),
        ],
        out_specs=[by_slot(slot_len, dv), by_slot(slot_len, dv), by_slot(1, rows, width), by_slot(1, rows, width)],
        out_shape=[
            shaped((total, dv), f32),
            shaped((total, dv), bf16),
            shaped((PLANE, rows, width), f32),
            shaped((PLANE, rows, width), bf16),
        ],
        compiler_params=params(),
        cost_estimate=cost(4 * total * width * dv, 40e6),
    )(rows_all, joined, joined, retained)


def project_kernel(wide, left, right, near_ref, far_ref):
    for columns, terms in times_rows(left[...], right[...], wide):
        split_out(terms, near_ref, far_ref, columns)


def project(left, right, wide):
    total, inner = left.shape
    width = right.shape[0]
    slot_len = total // PLANE
    rows = slot_len // 2
    return pl.pallas_call(
        functools.partial(project_kernel, wide),
        grid=(PLANE,),
        in_specs=[by_slot(slot_len, inner), whole(right.shape)],
        out_specs=[by_slot(1, rows, width)] * 2,
        out_shape=[shaped((PLANE, rows, width), f32), shaped((PLANE, rows, width), bf16)],
        compiler_params=params(),
        cost_estimate=cost(2 * total * inner * width, 20e6),
    )(left, right)


def back_kernel(left, first, second, near_ref, far_ref):
    dv = second.shape[1]
    narrow = first.shape[1] - dv
    terms = dot_nt(left[:, :dv], first[:, narrow:]) + dot_nt(left[:, dv : 2 * dv], second[...])
    terms += dot_nt(left[:, 2 * dv :], first[:, :narrow])
    split_out(terms, near_ref, far_ref, slice(None))


def project_back(left, joined, dk, dv):
    total, inner = left.shape
    width = joined.shape[0]
    slot_len = total // PLANE
    rows = slot_len // 2
    return pl.pallas_call(
        back_kernel,
        grid=(PLANE,),
        in_specs=[
            by_slot(slot_len, inner),
            whole((width, 2 * dk + dv)),
            pl.BlockSpec((width, dv), lambda i: (0, 2), pipeline_mode=pl.Buffered(1)),
        ],
        out_specs=[by_slot(1, rows, width)] * 2,
        out_shape=[shaped((PLANE, rows, width), f32), shaped((PLANE, rows, width), bf16)],
        compiler_params=params(),
        cost_estimate=cost(2 * total * inner * width, 20e6),
    )(left, joined, joined)


def fold_kernel(spots, n, *refs):
    nears, arriveds = refs[:n], refs[n : 2 * n]
    x_ref, y_ref, keep_x_ref, keep_y_ref = refs[2 * n :]
    half = x_ref.shape[1]

    def summed(k, lo):
        i, j = spots[k]
        return nears[i][j, lo : lo + half] + arriveds[i][j, lo : lo + half].astype(f32)

    x_ref[0] = summed(1, 0).astype(bf16)
    x_ref[1] = summed(3, 0).astype(bf16)
    y_ref[0] = summed(2, half).astype(bf16)
    y_ref[1] = summed(3, half).astype(bf16)
    keep_x_ref[...] = summed(1, half)
    keep_y_ref[...] = summed(2, 0)


def fold_cut(nears, arriveds):
    spots = [(i, j) for i, near in enumerate(nears) for j in range(near.shape[0])]
    _, rows, width = nears[0].shape
    half = rows // 2
    part = width // 4

    def cols(*shape):
        return pl.BlockSpec((*shape, part), lambda i: (0,) * len(shape) + (i,))

    given = [cols(near.shape[0], rows) for near in nears]
    return pl.pallas_call(
        functools.partial(fold_kernel, spots, len(nears)),
        grid=(width // part,),
        in_specs=given + given,
        out_specs=[cols(2, half), cols(2, half), cols(half), cols(half)],
        out_shape=[
            shaped((2, half, width), bf16),
            shaped((2, half, width), bf16),
            shaped((half, width), f32),
            shaped((half, width), f32),
        ],
        compiler_params=params(),
        cost_estimate=cost(1e6, 20e6),
    )(*nears, *arriveds)


def dot_back_kernel(wide, back, right, out_ref):
    out_ref[...] = times_rows_back(back[...], right[...], wide)


def dot_back(back, joined, inner, start, wide):
    total, width = back.shape
    slot_len = total // PLANE
    return pl.pallas_call(
        functools.partial(dot_back_kernel, wide),
        grid=(PLANE,),
        in_specs=[
            by_slot(slot_len, width),
            pl.BlockSpec((width, inner), lambda i: (0, start // inner), pipeline_mode=pl.Buffered(1)),
        ],
        out_specs=by_slot(slot_len, inner),
        out_shape=shaped((total, inner), f32),
        compiler_params=params(),
        cost_estimate=cost(2 * total * width * inner, 20e6),
    )(back, joined)


def hidden_kernel(first, n, n_kept, *refs):
    pieces, (weights, grad_in) = refs[: 2 * n], refs[2 * n : 2 * n + 2]
    act_ref, grad_ref, rows_ref, near_ref, far_ref = refs[2 * n + 2 + n_kept : 2 * n + 7 + n_kept]
    held, sem, out_sem = refs[2 * n + 7 + n_kept :]
    rows = load_pieces(pieces, held, sem)
    step = pl.program_id(0)
    slot_len = rows.shape[0]
    inner = act_ref.shape[1]
    keep = pltpu.make_async_copy(
        held.at[step], rows_ref.at[pl.ds((step + first) * slot_len, slot_len)], out_sem
    )
    keep.start()
    weights = weights[...]
    up = dot(rows, weights[:, :inner])
    value = dot(rows, weights[:, inner:])
    slope = jnp.tanh(tanh_scale * (up + tanh_cubic * (up * up * up)))
    gelu = 0.5 * up * (1.0 + slope)
    act_ref[...] = (gelu * value).astype(bf16)
    rise = 0.5 * (1.0 + slope) + 0.5 * up * (1.0 - slope * slope) * (
        tanh_scale * (1.0 + 3.0 * tanh_cubic * (up * up))
    )
    grad = grad_in[...]
    grad_ref[:, :inner] = (grad * value * rise).astype(bf16)
    grad_ref[:, inner:] = (grad * gelu).astype(bf16)
    split_out(dot_nt(grad_ref[...], weights), near_ref, far_ref, slice(None))
    keep.wait()


def hidden_units(first, pieces, joined, grad_in, kept):
    n = len(pieces) // 2
    rows, width = pieces[0].shape
    slot_len = 2 * rows
    total, inner = grad_in.shape

    def at(cols):
        return pl.BlockSpec((slot_len, cols), lambda i: (i + first, 0))

    return pl.pallas_call(
        functools.partial(hidden_kernel, first, n, len(kept)),
        grid=(n,),
        in_specs=[ANY] * (2 * n)
        + [pl.BlockSpec((width, 2 * inner), lambda i: (0, 0), pipeline_mode=pl.Buffered(1)), at(inner)]
        + [ANY] * len(kept),
        out_specs=[at(inner), at(2 * inner), ANY, by_slot(1, rows, width), by_slot(1, rows, width)],
        out_shape=[
            shaped((total, inner), bf16),
            shaped((total, 2 * inner), bf16),
            shaped((total, width), bf16),
            shaped((n, rows, width), f32),
            shaped((n, rows, width), bf16),
        ],
        scratch_shapes=[
            pltpu.VMEM((n, slot_len, width), bf16),
            pltpu.SemaphoreType.DMA((2 * n,)),
            pltpu.SemaphoreType.DMA,
        ],
        input_output_aliases={2 * n + 2 + i: i for i in range(len(kept))},
        compiler_params=params(),
        cost_estimate=cost(8 * n * slot_len * width * inner, 15e6),
    )(*pieces, joined, grad_in, *kept)


def retain_back_kernel(first, wide, n, n_kept, *refs):
    pieces = refs[: 2 * n]
    out_weights, decays, query, key, value, gate_ref, scores, retained_ref = refs[2 * n : 2 * n + 8]
    grad_ref, rows_ref = refs[2 * n + 8 + n_kept : 2 * n + 10 + n_kept]
    held, sem, out_sem = refs[2 * n + 10 + n_kept :]
    rows = load_pieces(pieces, held, sem)
    step = pl.program_id(0)
    slot_len = rows.shape[0]
    keep = pltpu.make_async_copy(
        held.at[step], rows_ref.at[pl.ds((step + first) * slot_len, slot_len)], out_sem
    )
    keep.start()
    dk, dv = query.shape[1], value.shape[1]
    grad = times_rows_back(rows, out_weights[...], wide)
    retained, gate = retained_ref[...], gate_ref[...]
    scale = lax.rsqrt(jnp.mean(retained * retained, axis=-1, keepdims=True) + group_floor)
    sigma = jax.nn.sigmoid(gate)
    normed = retained * scale
    grad_ref[:, dv : 2 * dv] = (grad * normed * (sigma * (1.0 + gate * (1.0 - sigma)))).astype(bf16)
    grad = grad * (gate * sigma)
    mean = jnp.mean(normed * grad, axis=-1, keepdims=True)
    grad_retained = (scale * (grad - normed * mean)).astype(bf16)
    grad_scores = (dot_nt(grad_retained, value[...]) * decays[...]).astype(bf16)
    grad_ref[:, :dv] = dot_tn(scores[0], grad_retained).astype(bf16)
    grad_ref[:, 2 * dv : 2 * dv + dk] = dot(grad_scores, key[...]).astype(bf16)
    grad_ref[:, 2 * dv + dk :] = dot_tn(grad_scores, query[...]).astype(bf16)
    keep.wait()


def retain_back(first, pieces, joined, decays, query, key, value, gate, scores, retained, kept, wide):
    n = len(pieces) // 2
    rows, width = pieces[0].shape
    slot_len = 2 * rows
    total, dk = query.shape
    dv = value.shape[1]

    def at(cols):
        return pl.BlockSpec((slot_len, cols), lambda i: (i + first, 0))

    return pl.pallas_call(
        functools.partial(retain_back_kernel, first, wide, n, len(kept)),
        grid=(n,),
        in_specs=[ANY] * (2 * n)
        + [
            pl.BlockSpec((width, dv), lambda i: (0, 3), pipeline_mode=pl.Buffered(1)),
            whole((slot_len, slot_len)),
            at(dk),
            at(dk),
            at(dv),
            at(dv),
            pl.BlockSpec((1, slot_len, slot_len), lambda i: (i + first, 0, 0)),
            at(dv),
        ]
        + [ANY] * len(kept),
        out_specs=[at(2 * dk + 2 * dv), ANY],
        out_shape=[shaped((total, 2 * dk + 2 * dv), bf16), shaped((total, width), bf16)],
        scratch_shapes=[
            pltpu.VMEM((n, slot_len, width), bf16),
            pltpu.SemaphoreType.DMA((2 * n,)),
            pltpu.SemaphoreType.DMA,
        ],
        input_output_aliases={2 * n + 8 + i: i for i in range(len(kept))},
        compiler_params=params(),
        cost_estimate=cost(4 * n * slot_len * width * dv, 15e6),
    )(*pieces, joined, decays, query, key, value, gate, scores, retained, *kept)


def grad_kernel(left, right, grad_ref):
    grad_ref[...] = dot_tn(left[...], right[...]).astype(bf16)


def columns_grad(left, right, block, cols):
    total, width = left.shape
    part = width // 4
    return pl.pallas_call(
        grad_kernel,
        grid=(width // part,),
        in_specs=[
            pl.BlockSpec((total, part), lambda i: (0, i)),
            pl.BlockSpec((total, cols), lambda i: (0, block), pipeline_mode=pl.Buffered(1)),
        ],
        out_specs=by_slot(part, cols),
        out_shape=shaped((width, cols), bf16),
        compiler_params=params(),
        cost_estimate=cost(2 * total * width * cols, 20e6),
    )(left, right)


def rows_grad(left, right, wide):
    total, inner = left.shape
    blocks = right.shape[1] // wide
    return pl.pallas_call(
        grad_kernel,
        grid=(blocks,),
        in_specs=[whole((total, inner)), pl.BlockSpec((total, wide), lambda i: (0, i))],
        out_specs=by_slot(inner, wide),
        out_shape=shaped((blocks * inner, wide), bf16),
        compiler_params=params(),
        cost_estimate=cost(2 * total * inner * wide * blocks, 20e6),
    )(left, right)


def place_grads_kernel(n, me_ref, *refs):
    ins, outs, held, sem = refs[:PLANE], refs[PLANE : PLANE + n], refs[-2], refs[-1]
    place = me_ref[0]
    copies = []
    for k in range(PLANE):
        held[k] = ins[k][...].astype(f32)
        at = 0
        for i, out in enumerate(outs):
            part = out.shape[1] // PLANE
            one = pltpu.make_async_copy(
                held.at[k, :, pl.ds(at, part)], out.at[:, lanes(place ^ k, part)], sem.at[k * n + i]
            )
            one.start()
            copies.append(one)
            at += part
    for one in copies:
        one.wait()


def place_columns(me, blocks, widths):
    rows = blocks[0].shape[0]
    n = len(widths)
    return pl.pallas_call(
        functools.partial(place_grads_kernel, n),
        in_specs=[pl.BlockSpec(memory_space=pltpu.SMEM)]
        + [pl.BlockSpec(memory_space=pltpu.VMEM)] * PLANE,
        out_specs=[ANY] * n,
        out_shape=[shaped((rows, PLANE * w), f32) for w in widths],
        scratch_shapes=[
            pltpu.VMEM((PLANE, *blocks[0].shape), f32),
            pltpu.SemaphoreType.DMA((PLANE * n,)),
        ],
        compiler_params=params(),
        cost_estimate=cost(0, 8e6),
    )(me, *blocks)


def place_rows_kernel(me_ref, *refs):
    ins, out, held, sem = refs[:PLANE], refs[PLANE], refs[-2], refs[-1]
    rows = ins[0].shape[0]
    copies = []
    for k in range(PLANE):
        held[k] = ins[k][...].astype(f32)
        one = pltpu.make_async_copy(held.at[k], out.at[lanes(me_ref[0] ^ k, rows), :], sem.at[k])
        one.start()
        copies.append(one)
    for one in copies:
        one.wait()


def place_rows(me, blocks):
    rows, cols = blocks[0].shape
    return pl.pallas_call(
        place_rows_kernel,
        in_specs=[pl.BlockSpec(memory_space=pltpu.SMEM)]
        + [pl.BlockSpec(memory_space=pltpu.VMEM)] * PLANE,
        out_specs=ANY,
        out_shape=shaped((PLANE * rows, cols), f32),
        scratch_shapes=[pltpu.VMEM((PLANE, rows, cols), f32), pltpu.SemaphoreType.DMA((PLANE,))],
        compiler_params=params(),
        cost_estimate=cost(0, 4e6),
    )(me, *blocks)


def hop(value, bits, count):
    return lax.ppermute(value, "dp", [(i, i ^ bits) for i in range(count)])


def swap(value):
    return lax.ppermute(value, "tensor", [(0, 1), (1, 0)])


def trade(blocks, count):
    return [blocks[0]] + [hop(blocks[k], k, count) for k in range(1, PLANE)]


def spread(mine, count, beside=None):
    half = mine.shape[0] // 2
    from_x = hop(mine, 1, count)
    from_y = hop(mine, 2, count)
    pieces = [mine, swap(mine)]
    if beside:
        from_x, from_y = after((from_x, from_y), beside(0, 1, pieces))
    far_a = hop(from_x[:half], 2, count)
    far_b = hop(from_y[half:], 1, count)
    nearer = [from_x, swap(from_x), from_y, swap(from_y)]
    if beside:
        far_a, far_b = after((far_a, far_b), beside(1, 3, nearer))
    far = jnp.concatenate([far_a, far_b])
    far = [far, swap(far)]
    if beside:
        return beside(3, 4, far)
    return pieces + nearer + far


def fold(nears, fars, count, beside=None):
    arriveds = [swap(far) for far in fars]
    to_x, to_y, keep_x, keep_y = fold_cut(nears, arriveds)
    from_x = hop(to_x, 1, count)
    from_y = hop(to_y, 2, count)
    made = None
    if beside:
        made = beside((to_x, to_y))
        from_x, from_y = after((from_x, from_y), made)
    last_y = hop((keep_y + from_x[1].astype(f32)).astype(bf16), 2, count)
    last_x = hop((keep_x + from_y[1].astype(f32)).astype(bf16), 1, count)
    added = jnp.concatenate(
        [from_x[0].astype(f32) + last_y.astype(f32), from_y[0].astype(f32) + last_x.astype(f32)]
    )
    summed = nears[0][0] + arriveds[0][0].astype(f32) + added
    return (summed, made) if beside else summed


def after(values, done):
    return lax.optimization_barrier((values, done))[0]


def on_device(
    tokens,
    lengths,
    w_query,
    w_key,
    w_value,
    w_gate,
    w_out,
    w_ffgate,
    w_ffup,
    w_ffdown,
    gain_attn,
    gain_mlp,
    cotangent,
):
    count = lax.axis_size("dp")
    depth = count // PLANE
    columns = [[q + PLANE * z for z in range(depth)] for q in range(PLANE)]
    place = lax.axis_index("dp")
    me = place % PLANE
    me_scalar = me.reshape(1).astype(jnp.int32)
    core = lax.axis_index("tensor")
    rows, width = tokens.shape
    wide = width // depth
    shard = w_query.shape[0]
    dk = w_query.shape[1] // PLANE
    dv = w_value.shape[1] // PLANE
    inner = w_ffgate.shape[1] // PLANE
    assert dk == DK and dv == DV

    def gather_depth(block):
        return lax.all_gather(block, "dp", axis=0, tiled=True, axis_index_groups=columns)

    def sum_depth(block):
        return lax.psum_scatter(block, "dp", scatter_dimension=0, tiled=True, axis_index_groups=columns)

    attn_cuts = cut_columns(me_scalar, (w_query, w_key, w_value, w_gate)), cut_rows(me_scalar, w_out)
    attn_blocks = [trade(cuts, count) for cuts in attn_cuts]
    attn_own = join_weights(me_scalar, *attn_blocks)
    attn_joined = gather_depth(attn_own)

    gains = jnp.stack([gain_attn, gain_mlp])[None]
    step = 1
    while step < count:
        gains = jnp.concatenate([gains, hop(gains, step, count)])
        step *= 2
    gains = jnp.take(gains, place ^ jnp.arange(count), axis=0).astype(f32)
    gain_first = gains[:, 0].reshape(1, width)
    gain_second = gains[:, 1].reshape(1, width)

    input_rows = tokens.astype(f32)
    first_scale = lax.rsqrt(jnp.mean(input_rows * input_rows, axis=-1, keepdims=True) + norm_eps)
    normed_attn = (input_rows * first_scale * gain_first).astype(bf16)
    attn_pieces = spread(after(normed_attn, attn_own), count)

    ff_cuts = after((cut_columns(me_scalar, (w_ffgate, w_ffup)), cut_rows(me_scalar, w_ffdown)), attn_pieces)
    ff_blocks = [trade(cuts, count) for cuts in ff_cuts]
    ff_own = join_weights(me_scalar, *ff_blocks)
    ff_joined = gather_depth(ff_own)

    local = jnp.arange(rows, dtype=jnp.int32)
    valid_rows = ((core * rows + local) < lengths[0]).astype(f32)[:, None]
    back_rows = valid_rows * cotangent.astype(f32)
    back_all = jnp.concatenate(spread(after(back_rows.astype(bf16), ff_own), count))

    positions = jnp.concatenate([core * rows + local, (1 - core) * rows + local])
    decays = decay_table(positions, core * PLANE + me)
    attn_pieces = after(attn_pieces, back_all)
    query, key, value, scores, retained, attn_all = retain(attn_pieces, attn_joined, decays, dk, dv)
    gate, gated, near, far = gate_out(attn_all, attn_joined, retained, wide)
    hidden = input_rows + fold([near], [far], count)

    second_scale = lax.rsqrt(jnp.mean(hidden * hidden, axis=-1, keepdims=True) + norm_eps)
    normed_mlp = (hidden * second_scale * gain_second).astype(bf16)

    grad_inner = dot_back(back_all, ff_joined, inner, 2 * inner, wide)
    state = {"kept": (), "nears": [], "fars": []}

    def units(lo, hi, pieces):
        *state["kept"], near, far = hidden_units(lo, pieces, ff_joined, grad_inner, state["kept"])
        state["nears"].append(near)
        state["fars"].append(far)
        return state["kept"]

    inner_act, grad_up, mlp_all = spread(normed_mlp, count, units)

    def ff_grads(done):
        act, back, left, right = after((inner_act, back_all, mlp_all, grad_up), done)
        return rows_grad(act, back, wide), columns_grad(left, right, 0, 2 * inner)

    grad_normed, (grad_down, grad_ff) = fold(state["nears"], state["fars"], count, ff_grads)
    down_part = sum_depth(grad_down)
    ff_part = sum_depth(grad_ff)
    scaled = grad_normed * gain_second
    grad_hidden = back_rows + second_scale * (
        scaled
        - hidden * (second_scale * second_scale) * jnp.mean(hidden * scaled, axis=-1, keepdims=True)
    )
    gain_term_mlp = jnp.sum(grad_normed * hidden * second_scale, axis=0)

    state["kept"] = ()

    def heads(lo, hi, pieces):
        state["kept"] = retain_back(
            lo, pieces, attn_joined, decays, query, key, value, gate, scores, retained, state["kept"], wide
        )
        return state["kept"]

    grad_wide, attn_grad_all = spread(grad_hidden.astype(bf16), count, heads)
    out_part = sum_depth(rows_grad(gated, attn_grad_all, wide))
    wide_part = sum_depth(columns_grad(attn_all, grad_wide, 0, 2 * dv + 2 * dk))

    near, far = project_back(grad_wide, attn_joined, dk, dv)
    grad_normed_attn = fold([near], [far], count)
    gain_term_attn = jnp.sum(grad_normed_attn * input_rows * first_scale, axis=0)
    scaled_first = grad_normed_attn * gain_first
    tokens_grad = grad_hidden + first_scale * (
        scaled_first
        - input_rows
        * (first_scale * first_scale)
        * jnp.mean(input_rows * scaled_first, axis=-1, keepdims=True)
    )
    tokens_grad = tokens_grad.astype(bf16)

    down_weights = ff_joined[:, 2 * inner :]
    near, far = project(after(inner_act, attn_grad_all), down_weights, wide)
    output = (valid_rows * (hidden + fold([near], [far], count))).astype(bf16)

    gain_terms = jnp.stack([gain_term_attn, gain_term_mlp])
    bit = count // 2
    while bit >= 1:
        side = (place // bit) % 2
        cut = gain_terms.reshape(2, 2, -1)
        kept = lax.dynamic_index_in_dim(cut, side, 1, keepdims=False)
        sent = lax.dynamic_index_in_dim(cut, 1 - side, 1, keepdims=False)
        gain_terms = kept + hop(sent, bit, count)
        bit //= 2
    cut = gain_terms.reshape(2, 2, -1)
    kept = lax.dynamic_index_in_dim(cut, core, 1, keepdims=False)
    sent = lax.dynamic_index_in_dim(cut, 1 - core, 1, keepdims=False)
    gain_terms = kept + swap(sent)
    wide_part = after(wide_part, (output, tokens_grad, gain_terms))

    def back_columns(block, widths):
        cuts = [lax.dynamic_slice_in_dim(block, (me ^ k) * shard, shard, 0).astype(bf16) for k in range(PLANE)]
        return place_columns(me_scalar, trade(cuts, count), widths)

    def back_rows_of(block):
        cuts = [lax.dynamic_slice_in_dim(block, (me ^ k) * shard, shard, 1).astype(bf16) for k in range(PLANE)]
        return place_rows(me_scalar, trade(cuts, count))

    down_sum = back_rows_of(down_part)
    ffgate_sum, ffup_sum = back_columns(ff_part, (inner, inner))
    out_sum = back_rows_of(out_part)
    value_sum, gate_sum, query_sum, key_sum = back_columns(wide_part, (dv, dv, dk, dk))

    return (
        output,
        tokens_grad,
        query_sum,
        key_sum,
        value_sum,
        gate_sum,
        out_sum,
        ffgate_sum,
        ffup_sum,
        down_sum,
        gain_terms[0],
        gain_terms[1],
    )


def solution(mesh):
    return jax.shard_map(
        on_device,
        mesh=mesh,
        in_specs=(
            P(("dp", "tensor"), None),
            P("dp"),
            P("dp", "tensor"),
            P("dp", "tensor"),
            P("dp", "tensor"),
            P("dp", "tensor"),
            P("tensor", "dp"),
            P("dp", "tensor"),
            P("dp", "tensor"),
            P("tensor", "dp"),
            P("dp"),
            P("dp"),
            P(("dp", "tensor"), None),
        ),
        out_specs=(
            P(("dp", "tensor"), None),
            P(("dp", "tensor"), None),
            P("dp", "tensor"),
            P("dp", "tensor"),
            P("dp", "tensor"),
            P("dp", "tensor"),
            P("tensor", "dp"),
            P("dp", "tensor"),
            P("dp", "tensor"),
            P("tensor", "dp"),
            P(("dp", "tensor")),
            P(("dp", "tensor")),
        ),
        check_vma=False,
    )
```

```python
import functools

import jax
import jax.numpy as jnp
from jax import lax
from jax.experimental import pallas as pl
from jax.experimental.pallas import tpu as pltpu
from jax.sharding import PartitionSpec as P

DK = 256
DV = 512
PLANE = 4
SLOTS = ((0, 1), (1, 3), (3, 4))
VMEM_BYTES = 62 * 1024 * 1024

norm_eps = 1e-06
group_floor = 1.0
tanh_scale = 0.7978845608028654
tanh_cubic = 0.044715

bf16 = jnp.bfloat16
f32 = jnp.float32


def shaped(shape, kind):
    return jax.ShapeDtypeStruct(shape, kind)


def cost(flops, bytes_accessed):
    return pl.CostEstimate(flops=int(flops), bytes_accessed=int(bytes_accessed), transcendentals=0)


def params():
    return pltpu.CompilerParams(vmem_limit_bytes=VMEM_BYTES)


ANY = pl.BlockSpec(memory_space=pl.ANY)


def whole(shape):
    return pl.BlockSpec(shape, lambda i: (0,) * len(shape), pipeline_mode=pl.Buffered(1))


def by_slot(*shape):
    return pl.BlockSpec(shape, lambda i: (i,) + (0,) * (len(shape) - 1))


def dot(left, right):
    return jnp.dot(left, right, preferred_element_type=f32)


def dot_nt(left, right):
    return lax.dot_general(left, right, (((1,), (1,)), ((), ())), preferred_element_type=f32)


def dot_tn(left, right):
    return lax.dot_general(left, right, (((0,), (0,)), ((), ())), preferred_element_type=f32)


def decay_table(positions, head):
    spacing = positions[:, None] - positions[None, :]
    log_rate = jnp.log1p(-jnp.exp2(-5.0 - head.astype(f32)))
    kept_spacing = jnp.where(spacing >= 0, spacing, jnp.zeros_like(spacing)).astype(f32)
    powers = jnp.exp(kept_spacing * log_rate)
    return jnp.where(spacing >= 0, powers, jnp.zeros_like(powers))


def copy_kernel(plan, n_in, me_ref, *refs):
    ins, outs, sem = refs[:n_in], refs[n_in:-1], refs[-1]
    copies = [
        pltpu.make_async_copy(source, target, sem.at[i])
        for i, (source, target) in enumerate(plan(me_ref[0], ins, outs))
    ]
    for one in copies:
        one.start()
    for one in copies:
        one.wait()


def place_copies(plan, n_copies, me, ins, out_shapes):
    moved = 2 * sum(2 * s.size for s in out_shapes)
    return pl.pallas_call(
        functools.partial(copy_kernel, plan, len(ins)),
        in_specs=[pl.BlockSpec(memory_space=pltpu.SMEM)] + [pl.BlockSpec(memory_space=pltpu.VMEM)] * len(ins),
        out_specs=[ANY] * len(out_shapes),
        out_shape=out_shapes,
        scratch_shapes=[pltpu.SemaphoreType.DMA((n_copies,))],
        compiler_params=params(),
        cost_estimate=cost(0, moved),
    )(me, *ins)


def lanes(index, size):
    return pl.ds(pl.multiple_of(index * size, size), size)


def cut_weights(me, by_columns, by_rows):
    rows, cols = by_columns[0].shape[0], by_rows.shape[1]
    parts = [w.shape[1] // PLANE for w in by_columns]
    inner = by_rows.shape[0] // PLANE
    width = sum(parts)
    aligned = cols % 128 == 0
    if not aligned:
        by_rows = jnp.moveaxis(by_rows.reshape(PLANE, inner // rows, rows, cols), 1, 2)
        by_rows = jnp.moveaxis(by_rows.reshape(PLANE, rows, -1), 0, 1).reshape(rows, -1)

    def plan(place, ins, outs):
        copies = []
        for k in range(PLANE):
            at = 0
            for w, part in zip(ins, parts):
                copies.append((w.at[:, lanes(place ^ k, part)], outs[k].at[:, pl.ds(at, part)]))
                at += part
            if not aligned:
                copies.append((ins[-1].at[:, lanes(place ^ k, inner)], outs[k].at[:, pl.ds(width, inner)]))
                continue
            for block in range(inner // rows):
                source = pl.ds(pl.multiple_of((place ^ k) * inner + block * rows, rows), rows)
                copies.append((ins[-1].at[source, :], outs[k].at[:, pl.ds(width + block * cols, cols)]))
        return copies

    shapes = [shaped((rows, width + inner), bf16)] * PLANE
    n_copies = PLANE * (len(parts) + (inner // rows if aligned else 1))
    return place_copies(plan, n_copies, me, [*by_columns, by_rows], shapes)


def join_weights(me, blocks, width):
    rows, inner = blocks[0].shape[0], blocks[0].shape[1] - width
    tall = PLANE * rows
    aligned = rows % 128 == 0
    extra = []
    if not aligned:
        parts = jnp.stack([lax.dynamic_index_in_dim(jnp.stack(blocks), me[0] ^ j, 0, keepdims=False) for j in range(PLANE)])
        parts = parts[:, :, width:].reshape(PLANE, rows, inner // tall, PLANE, rows)
        extra = [jnp.transpose(parts, (3, 1, 2, 0, 4)).reshape(tall, inner)]

    def plan(place, ins, outs):
        copies = []
        for k in range(PLANE):
            copies.append((ins[k].at[:, pl.ds(0, width)], outs[0].at[lanes(place ^ k, rows), pl.ds(0, width)]))
            for block in range(inner // rows if aligned else 0):
                spot = pl.ds(pl.multiple_of(width + (place ^ k) * rows, rows), rows)
                if block >= PLANE:
                    spot = pl.ds(pl.multiple_of(width + (block // PLANE) * tall + (place ^ k) * rows, rows), rows)
                source = ins[k].at[:, pl.ds(width + block * rows, rows)]
                copies.append((source, outs[0].at[pl.ds((block % PLANE) * rows, rows), spot]))
        if not aligned:
            copies.append((ins[PLANE], outs[0].at[:, pl.ds(width, inner)]))
        return copies

    n_copies = PLANE * (1 + inner // rows) if aligned else PLANE + 1
    return place_copies(plan, n_copies, me, [*blocks, *extra], [shaped((tall, width + inner), bf16)])[0]


def load_pieces(pieces, held, sem):
    step = pl.program_id(0)
    rows = pieces[0].shape[0]
    copies = [
        pltpu.make_async_copy(piece, held.at[i // 2, pl.ds((i % 2) * rows, rows)], sem.at[i])
        for i, piece in enumerate(pieces)
    ]

    @pl.when(step == 0)
    def start():
        for one in copies:
            one.start()

    for s in range(len(pieces) // 2):

        @pl.when(step == s)
        def arrive(s=s):
            copies[2 * s].wait()
            copies[2 * s + 1].wait()

    return held[step]


def retain_kernel(*refs):
    pieces, (weights, decays) = refs[:8], refs[8:10]
    query_ref, key_ref, value_ref, scores_ref, retained_ref, rows_ref = refs[10:16]
    held, sem, out_sem = refs[16:]
    rows = load_pieces(pieces, held, sem)
    step = pl.program_id(0)
    slot_len = rows.shape[0]
    keep = pltpu.make_async_copy(held.at[step], rows_ref.at[pl.ds(step * slot_len, slot_len)], out_sem)
    keep.start()
    dk, dv = query_ref.shape[1], value_ref.shape[1]
    query_key = dot(rows, weights[:, : 2 * dk]).astype(bf16)
    query, key = query_key[:, :dk], query_key[:, dk:]
    query_ref[...] = query
    key_ref[...] = key
    scores = (dot_nt(query, key) * decays[...]).astype(bf16)
    scores_ref[...] = scores[None]
    value = dot(rows, weights[:, 2 * dk : 2 * dk + dv]).astype(bf16)
    value_ref[...] = value
    retained_ref[...] = dot(scores, value)
    keep.wait()


def retain(pieces, weights, decays, dk, dv):
    rows, width = pieces[0].shape
    slot_len = 2 * rows
    total = PLANE * slot_len
    return pl.pallas_call(
        retain_kernel,
        grid=(PLANE,),
        in_specs=[ANY] * 8 + [whole((width, 2 * dk + dv)), whole((slot_len, slot_len))],
        out_specs=[
            by_slot(slot_len, dk),
            by_slot(slot_len, dk),
            by_slot(slot_len, dv),
            by_slot(1, slot_len, slot_len),
            by_slot(slot_len, dv),
            ANY,
        ],
        out_shape=[
            shaped((total, dk), bf16),
            shaped((total, dk), bf16),
            shaped((total, dv), bf16),
            shaped((PLANE, slot_len, slot_len), bf16),
            shaped((total, dv), f32),
            shaped((total, width), bf16),
        ],
        scratch_shapes=[
            pltpu.VMEM((PLANE, slot_len, width), bf16),
            pltpu.SemaphoreType.DMA((8,)),
            pltpu.SemaphoreType.DMA,
        ],
        compiler_params=params(),
        cost_estimate=cost(2.2 * total * width * (2 * dk + dv), 30e6),
    )(*pieces, weights, decays)


def times_rows(left, right, wide):
    groups = right.shape[1] // wide
    for z in range(right.shape[0] // wide):
        terms = dot(left[:, :wide], right[z * wide : (z + 1) * wide, :wide])
        for g in range(1, groups):
            terms += dot(
                left[:, g * wide : (g + 1) * wide],
                right[z * wide : (z + 1) * wide, g * wide : (g + 1) * wide],
            )
        yield slice(z * wide, (z + 1) * wide), terms


def times_rows_back(left, right, wide):
    made = []
    for g in range(right.shape[1] // wide):
        group = slice(g * wide, (g + 1) * wide)
        terms = dot_nt(left[:, :wide], right[:wide, group])
        for z in range(1, right.shape[0] // wide):
            block = slice(z * wide, (z + 1) * wide)
            terms += dot_nt(left[:, block], right[block, group])
        made.append(terms)
    return made[0] if len(made) == 1 else jnp.concatenate(made, axis=1)


def split_out(terms, near_ref, far_ref, columns):
    rows = near_ref.shape[1]
    near_ref[0, :, columns] = terms[:rows]
    far_ref[0, :, columns] = terms[rows:].astype(bf16)


def gate_out_kernel(wide, n_kept, rows_ref, weights, out_weights, retained_ref, *refs):
    gate_ref, gated_ref, near_ref, far_ref = refs[n_kept:]
    retained = retained_ref[...]
    scale = lax.rsqrt(jnp.mean(retained * retained, axis=-1, keepdims=True) + group_floor)
    gate = dot(rows_ref[...], weights[...])
    gate_ref[...] = gate
    gated_ref[...] = (gate * jax.nn.sigmoid(gate) * (retained * scale)).astype(bf16)
    for columns, terms in times_rows(gated_ref[...], out_weights[...], wide):
        split_out(terms, near_ref, far_ref, columns)


def gate_out(lo, hi, rows_all, joined, retained, kept, wide):
    total, width = rows_all.shape
    dv = retained.shape[1]
    slot_len = total // PLANE
    rows = slot_len // 2

    def at(cols):
        return pl.BlockSpec((slot_len, cols), lambda i: (i + lo, 0))

    return pl.pallas_call(
        functools.partial(gate_out_kernel, wide, len(kept)),
        grid=(hi - lo,),
        in_specs=[
            at(width),
            pl.BlockSpec((width, dv), lambda i: (0, 2), pipeline_mode=pl.Buffered(1)),
            pl.BlockSpec((width, dv), lambda i: (0, 3), pipeline_mode=pl.Buffered(1)),
            at(dv),
        ]
        + [ANY] * len(kept),
        out_specs=[at(dv), at(dv), by_slot(1, rows, width), by_slot(1, rows, width)],
        out_shape=[
            shaped((total, dv), f32),
            shaped((total, dv), bf16),
            shaped((hi - lo, rows, width), f32),
            shaped((hi - lo, rows, width), bf16),
        ],
        input_output_aliases={4 + i: i for i in range(len(kept))},
        compiler_params=params(),
        cost_estimate=cost((hi - lo) * total * width * dv, (hi - lo) * 10e6),
    )(rows_all, joined, joined, retained, *kept)


def project_kernel(wide, left, right, near_ref, far_ref):
    for columns, terms in times_rows(left[...], right[...], wide):
        split_out(terms, near_ref, far_ref, columns)


def project(left, right, wide):
    total, inner = left.shape
    width = right.shape[0]
    slot_len = total // PLANE
    rows = slot_len // 2
    return pl.pallas_call(
        functools.partial(project_kernel, wide),
        grid=(PLANE,),
        in_specs=[by_slot(slot_len, inner), whole(right.shape)],
        out_specs=[by_slot(1, rows, width)] * 2,
        out_shape=[shaped((PLANE, rows, width), f32), shaped((PLANE, rows, width), bf16)],
        compiler_params=params(),
        cost_estimate=cost(2 * total * inner * width, 20e6),
    )(left, right)


def back_kernel(left, first, second, near_ref, far_ref):
    dv = second.shape[1]
    narrow = first.shape[1] - dv
    terms = dot_nt(left[:, :dv], first[:, narrow:]) + dot_nt(left[:, dv : 2 * dv], second[...])
    terms += dot_nt(left[:, 2 * dv :], first[:, :narrow])
    split_out(terms, near_ref, far_ref, slice(None))


def project_back(left, joined, dk, dv):
    total, inner = left.shape
    width = joined.shape[0]
    slot_len = total // PLANE
    rows = slot_len // 2
    return pl.pallas_call(
        back_kernel,
        grid=(PLANE,),
        in_specs=[
            by_slot(slot_len, inner),
            whole((width, 2 * dk + dv)),
            pl.BlockSpec((width, dv), lambda i: (0, 2), pipeline_mode=pl.Buffered(1)),
        ],
        out_specs=[by_slot(1, rows, width)] * 2,
        out_shape=[shaped((PLANE, rows, width), f32), shaped((PLANE, rows, width), bf16)],
        compiler_params=params(),
        cost_estimate=cost(2 * total * inner * width, 20e6),
    )(left, joined, joined)


def fold_kernel(*refs):
    nears, arriveds = refs[:3], refs[3:6]
    x1_ref, y2_ref, x3_ref, y3_ref, keep_x_ref, keep_y_ref = refs[6:]
    half = x1_ref.shape[0]
    targets = ((x1_ref, keep_x_ref), (keep_y_ref, y2_ref), (x3_ref, y3_ref))
    for near, arrived, (first, second) in zip(nears, arriveds, targets):
        first[...] = (near[0, :half] + arrived[0, :half].astype(f32)).astype(first.dtype)
        second[...] = (near[0, half:] + arrived[0, half:].astype(f32)).astype(second.dtype)


def fold_cut(slots):
    nears, arriveds, spots = zip(*slots)
    _, rows, width = nears[0].shape
    half = rows // 2
    part = width // 4
    kinds = (bf16, bf16, bf16, bf16, f32, f32)
    given = [pl.BlockSpec((1, rows, part), lambda i, spot=spot: (spot, 0, i)) for spot in spots]
    return pl.pallas_call(
        fold_kernel,
        grid=(width // part,),
        in_specs=given + given,
        out_specs=[pl.BlockSpec((half, part), lambda i: (0, i))] * len(kinds),
        out_shape=[shaped((half, width), kind) for kind in kinds],
        compiler_params=params(),
        cost_estimate=cost(1e6, 12e6),
    )(*nears, *arriveds)


def hidden_kernel(first, wide, n, n_kept, *refs):
    pieces, (weights, down_weights, back) = refs[: 2 * n], refs[2 * n : 2 * n + 3]
    act_ref, grad_ref, rows_ref, near_ref, far_ref = refs[2 * n + 3 + n_kept : 2 * n + 8 + n_kept]
    held, sem, out_sem = refs[2 * n + 8 + n_kept :]
    rows = load_pieces(pieces, held, sem)
    step = pl.program_id(0)
    slot_len = rows.shape[0]
    inner = act_ref.shape[1]
    keep = pltpu.make_async_copy(
        held.at[step], rows_ref.at[pl.ds((step + first) * slot_len, slot_len)], out_sem
    )
    keep.start()
    weights = weights[...]
    up = dot(rows, weights[:, :inner])
    value = dot(rows, weights[:, inner:])
    slope = jnp.tanh(tanh_scale * (up + tanh_cubic * (up * up * up)))
    gelu = 0.5 * up * (1.0 + slope)
    act_ref[...] = (gelu * value).astype(bf16)
    rise = 0.5 * (1.0 + slope) + 0.5 * up * (1.0 - slope * slope) * (
        tanh_scale * (1.0 + 3.0 * tanh_cubic * (up * up))
    )
    grad = times_rows_back(back[...], down_weights[...], wide)
    grad_ref[:, :inner] = (grad * value * rise).astype(bf16)
    grad_ref[:, inner:] = (grad * gelu).astype(bf16)
    split_out(dot_nt(grad_ref[...], weights), near_ref, far_ref, slice(None))
    keep.wait()


def hidden_units(first, pieces, joined, back, kept, inner, wide):
    n = len(pieces) // 2
    rows, width = pieces[0].shape
    slot_len = 2 * rows
    total = back.shape[0]

    def at(cols):
        return pl.BlockSpec((slot_len, cols), lambda i: (i + first, 0))

    return pl.pallas_call(
        functools.partial(hidden_kernel, first, wide, n, len(kept)),
        grid=(n,),
        in_specs=[ANY] * (2 * n)
        + [
            pl.BlockSpec((width, 2 * inner), lambda i: (0, 0), pipeline_mode=pl.Buffered(1)),
            pl.BlockSpec((width, inner), lambda i: (0, 2), pipeline_mode=pl.Buffered(1)),
            at(width),
        ]
        + [ANY] * len(kept),
        out_specs=[at(inner), at(2 * inner), ANY, by_slot(1, rows, width), by_slot(1, rows, width)],
        out_shape=[
            shaped((total, inner), bf16),
            shaped((total, 2 * inner), bf16),
            shaped((total, width), bf16),
            shaped((n, rows, width), f32),
            shaped((n, rows, width), bf16),
        ],
        scratch_shapes=[
            pltpu.VMEM((n, slot_len, width), bf16),
            pltpu.SemaphoreType.DMA((2 * n,)),
            pltpu.SemaphoreType.DMA,
        ],
        input_output_aliases={2 * n + 3 + i: i for i in range(len(kept))},
        compiler_params=params(),
        cost_estimate=cost(10 * n * slot_len * width * inner, 15e6),
    )(*pieces, joined, joined, back, *kept)


def retain_back_kernel(first, wide, n, n_kept, *refs):
    pieces = refs[: 2 * n]
    out_weights, decays, query, key, value, gate_ref, scores, retained_ref = refs[2 * n : 2 * n + 8]
    grad_ref, rows_ref = refs[2 * n + 8 + n_kept : 2 * n + 10 + n_kept]
    held, sem, out_sem = refs[2 * n + 10 + n_kept :]
    rows = load_pieces(pieces, held, sem)
    step = pl.program_id(0)
    slot_len = rows.shape[0]
    keep = pltpu.make_async_copy(
        held.at[step], rows_ref.at[pl.ds((step + first) * slot_len, slot_len)], out_sem
    )
    keep.start()
    dk, dv = query.shape[1], value.shape[1]
    grad = times_rows_back(rows, out_weights[...], wide)
    retained, gate = retained_ref[...], gate_ref[...]
    scale = lax.rsqrt(jnp.mean(retained * retained, axis=-1, keepdims=True) + group_floor)
    sigma = jax.nn.sigmoid(gate)
    normed = retained * scale
    grad_ref[:, dv : 2 * dv] = (grad * normed * (sigma * (1.0 + gate * (1.0 - sigma)))).astype(bf16)
    grad = grad * (gate * sigma)
    mean = jnp.mean(normed * grad, axis=-1, keepdims=True)
    grad_retained = (scale * (grad - normed * mean)).astype(bf16)
    grad_scores = (dot_nt(grad_retained, value[...]) * decays[...]).astype(bf16)
    grad_ref[:, :dv] = dot_tn(scores[0], grad_retained).astype(bf16)
    grad_ref[:, 2 * dv : 2 * dv + dk] = dot(grad_scores, key[...]).astype(bf16)
    grad_ref[:, 2 * dv + dk :] = dot_tn(grad_scores, query[...]).astype(bf16)
    keep.wait()


def retain_back(first, pieces, joined, decays, query, key, value, gate, scores, retained, kept, wide):
    n = len(pieces) // 2
    rows, width = pieces[0].shape
    slot_len = 2 * rows
    total, dk = query.shape
    dv = value.shape[1]

    def at(cols):
        return pl.BlockSpec((slot_len, cols), lambda i: (i + first, 0))

    return pl.pallas_call(
        functools.partial(retain_back_kernel, first, wide, n, len(kept)),
        grid=(n,),
        in_specs=[ANY] * (2 * n)
        + [
            pl.BlockSpec((width, dv), lambda i: (0, 3), pipeline_mode=pl.Buffered(1)),
            whole((slot_len, slot_len)),
            at(dk),
            at(dk),
            at(dv),
            at(dv),
            pl.BlockSpec((1, slot_len, slot_len), lambda i: (i + first, 0, 0)),
            at(dv),
        ]
        + [ANY] * len(kept),
        out_specs=[at(2 * dk + 2 * dv), ANY],
        out_shape=[shaped((total, 2 * dk + 2 * dv), bf16), shaped((total, width), bf16)],
        scratch_shapes=[
            pltpu.VMEM((n, slot_len, width), bf16),
            pltpu.SemaphoreType.DMA((2 * n,)),
            pltpu.SemaphoreType.DMA,
        ],
        input_output_aliases={2 * n + 8 + i: i for i in range(len(kept))},
        compiler_params=params(),
        cost_estimate=cost(4 * n * slot_len * width * dv, 15e6),
    )(*pieces, joined, decays, query, key, value, gate, scores, retained, *kept)


def grad_kernel(left, right, grad_ref):
    grad_ref[...] = dot_tn(left[...], right[...]).astype(bf16)


def columns_grad(left, right, block, cols):
    total, width = left.shape
    part = width // 4
    return pl.pallas_call(
        grad_kernel,
        grid=(width // part,),
        in_specs=[
            pl.BlockSpec((total, part), lambda i: (0, i)),
            pl.BlockSpec((total, cols), lambda i: (0, block), pipeline_mode=pl.Buffered(1)),
        ],
        out_specs=by_slot(part, cols),
        out_shape=shaped((width, cols), bf16),
        compiler_params=params(),
        cost_estimate=cost(2 * total * width * cols, 20e6),
    )(left, right)


def rows_grad(left, right, wide):
    total, inner = left.shape
    blocks = right.shape[1] // wide
    return pl.pallas_call(
        grad_kernel,
        grid=(blocks,),
        in_specs=[whole((total, inner)), pl.BlockSpec((total, wide), lambda i: (0, i))],
        out_specs=by_slot(inner, wide),
        out_shape=shaped((blocks * inner, wide), bf16),
        compiler_params=params(),
        cost_estimate=cost(2 * total * inner * wide * blocks, 20e6),
    )(left, right)


def place_grads_kernel(n, me_ref, *refs):
    ins, outs, held, sem = refs[:PLANE], refs[PLANE : PLANE + n], refs[-2], refs[-1]
    place = me_ref[0]
    copies = []
    for k in range(PLANE):
        held[k] = ins[k][...].astype(f32)
        at = 0
        for i, out in enumerate(outs):
            part = out.shape[1] // PLANE
            one = pltpu.make_async_copy(
                held.at[k, :, pl.ds(at, part)], out.at[:, lanes(place ^ k, part)], sem.at[k * n + i]
            )
            one.start()
            copies.append(one)
            at += part
    for one in copies:
        one.wait()


def place_columns(me, blocks, widths):
    rows = blocks[0].shape[0]
    n = len(widths)
    return pl.pallas_call(
        functools.partial(place_grads_kernel, n),
        in_specs=[pl.BlockSpec(memory_space=pltpu.SMEM)]
        + [pl.BlockSpec(memory_space=pltpu.VMEM)] * PLANE,
        out_specs=[ANY] * n,
        out_shape=[shaped((rows, PLANE * w), f32) for w in widths],
        scratch_shapes=[
            pltpu.VMEM((PLANE, *blocks[0].shape), f32),
            pltpu.SemaphoreType.DMA((PLANE * n,)),
        ],
        compiler_params=params(),
        cost_estimate=cost(0, 8e6),
    )(me, *blocks)


def place_rows_kernel(me_ref, *refs):
    ins, out, held, sem = refs[:PLANE], refs[PLANE], refs[-2], refs[-1]
    rows = ins[0].shape[0]
    copies = []
    for k in range(PLANE):
        held[k] = ins[k][...].astype(f32)
        one = pltpu.make_async_copy(held.at[k], out.at[lanes(me_ref[0] ^ k, rows), :], sem.at[k])
        one.start()
        copies.append(one)
    for one in copies:
        one.wait()


def place_rows(me, blocks):
    rows, cols = blocks[0].shape
    return pl.pallas_call(
        place_rows_kernel,
        in_specs=[pl.BlockSpec(memory_space=pltpu.SMEM)]
        + [pl.BlockSpec(memory_space=pltpu.VMEM)] * PLANE,
        out_specs=ANY,
        out_shape=shaped((PLANE * rows, cols), f32),
        scratch_shapes=[pltpu.VMEM((PLANE, rows, cols), f32), pltpu.SemaphoreType.DMA((PLANE,))],
        compiler_params=params(),
        cost_estimate=cost(0, 4e6),
    )(me, *blocks)


def hop(value, bits, count):
    return lax.ppermute(value, "dp", [(i, i ^ bits) for i in range(count)])


def swap(value):
    return lax.ppermute(value, "tensor", [(0, 1), (1, 0)])


def trade(blocks, count):
    return [blocks[0]] + [hop(blocks[k], k, count) for k in range(1, PLANE)]


def spread(mine, count, beside=None):
    half = mine.shape[0] // 2
    from_x = hop(mine, 1, count)
    from_y = hop(mine, 2, count)
    pieces = [mine, swap(mine)]
    if beside:
        from_x, from_y = after((from_x, from_y), beside(0, 1, pieces))
    far_a = hop(from_x[:half], 2, count)
    far_b = hop(from_y[half:], 1, count)
    nearer = [from_x, swap(from_x), from_y, swap(from_y)]
    if beside:
        far_a, far_b = after((far_a, far_b), beside(1, 3, nearer))
    far = jnp.concatenate([far_a, far_b])
    far = [far, swap(far)]
    if beside:
        return beside(3, 4, far)
    return pieces + nearer + far


def fold(groups, count, before=(), first=None, second=None):
    slots = {}

    def take(lo, near, far):
        arrived = swap(far)
        for k in range(near.shape[0]):
            slots[lo + k] = near, arrived, k

    for group in groups:
        take(*group)
    given = after([(near, arrived) for near, arrived, _ in (slots[k] for k in (1, 2, 3))], before)
    cut = fold_cut([(*pair, slots[k][2]) for k, pair in zip((1, 2, 3), given)])
    to_x1, to_y2, to_x3, to_y3, keep_x, keep_y = cut
    half, width = to_x1.shape
    x1, y2 = hop(to_x1, 1, count), hop(to_y2, 2, count)
    x3, y3 = hop(to_x3, 1, count), hop(to_y3, 2, count)
    made = []
    if first:
        made.append(first((to_x3, to_y3)))
        x3, y3 = after((x3, y3), made)
    if 0 not in slots:
        take(*made[0][0])
    near_0, arrived_0, spot = slots[0]
    to_y, to_x = (keep_y + x3.astype(f32)).astype(bf16), (keep_x + y3.astype(f32)).astype(bf16)
    last_y, last_x = hop(to_y, 2, count), hop(to_x, 1, count)
    if second:
        made.append(second((to_x, to_y), made))
        last_y, last_x = after((last_y, last_x), made[-1])
    near_0, arrived_0 = near_0[spot], arrived_0[spot].astype(f32)
    summed = [
        near_0[:half] + arrived_0[:half] + (x1.astype(f32) + last_y.astype(f32)),
        near_0[half:] + arrived_0[half:] + (y2.astype(f32) + last_x.astype(f32)),
    ]
    return jnp.concatenate(summed), *made


def after(values, done):
    return lax.optimization_barrier((values, done))[0]


def on_device(
    tokens,
    lengths,
    w_query,
    w_key,
    w_value,
    w_gate,
    w_out,
    w_ffgate,
    w_ffup,
    w_ffdown,
    gain_attn,
    gain_mlp,
    cotangent,
):
    count = lax.axis_size("dp")
    depth = count // PLANE
    columns = [[q + PLANE * z for z in range(depth)] for q in range(PLANE)]
    place = lax.axis_index("dp")
    me = place % PLANE
    me_scalar = me.reshape(1).astype(jnp.int32)
    core = lax.axis_index("tensor")
    rows, width = tokens.shape
    wide = width // depth
    shard = w_query.shape[0]
    dk = w_query.shape[1] // PLANE
    dv = w_value.shape[1] // PLANE
    inner = w_ffgate.shape[1] // PLANE
    assert dk == DK and dv == DV

    def gather_depth(block):
        return lax.all_gather(block, "dp", axis=0, tiled=True, axis_index_groups=columns)

    def sum_depth(block):
        return lax.psum_scatter(block, "dp", scatter_dimension=0, tiled=True, axis_index_groups=columns)

    attn_cuts = cut_weights(me_scalar, (w_query, w_key, w_value, w_gate), w_out)
    attn_own = join_weights(me_scalar, trade(attn_cuts, count), 2 * dk + 2 * dv)
    attn_joined = gather_depth(attn_own)

    gains = jnp.stack([gain_attn, gain_mlp])[None]
    step = 1
    while step < count:
        gains = jnp.concatenate([gains, hop(gains, step, count)])
        step *= 2
    gains = jnp.take(gains, place ^ jnp.arange(count), axis=0).astype(f32)
    gain_first = gains[:, 0].reshape(1, width)
    gain_second = gains[:, 1].reshape(1, width)

    input_rows = tokens.astype(f32)
    first_scale = lax.rsqrt(jnp.mean(input_rows * input_rows, axis=-1, keepdims=True) + norm_eps)
    normed_attn = (input_rows * first_scale * gain_first).astype(bf16)
    attn_pieces = spread(after(normed_attn, attn_own), count)

    ff_cuts = after(cut_weights(me_scalar, (w_ffgate, w_ffup), w_ffdown), attn_pieces)
    ff_own = join_weights(me_scalar, trade(ff_cuts, count), 2 * inner)
    ff_joined = gather_depth(ff_own)

    local = jnp.arange(rows, dtype=jnp.int32)
    valid_rows = ((core * rows + local) < lengths[0]).astype(f32)[:, None]
    back_rows = valid_rows * cotangent.astype(f32)
    back_pieces = spread(after(back_rows.astype(bf16), ff_own), count)
    back_all = jnp.concatenate(back_pieces)

    positions = jnp.concatenate([core * rows + local, (1 - core) * rows + local])
    decays = decay_table(positions, core * PLANE + me)
    attn_pieces = after(attn_pieces, back_all)
    query, key, value, scores, retained, attn_all = retain(attn_pieces, attn_joined, decays, dk, dv)
    kept, groups = [], []
    for lo, hi in (SLOTS[1], SLOTS[2]):
        *kept, near, far = gate_out(lo, hi, attn_all, attn_joined, retained, kept, wide)
        groups.append((lo, near, far))

    def gate_own(done):
        lo, hi = SLOTS[0]
        *made, near, far = gate_out(lo, hi, after(attn_all, done), attn_joined, retained, kept, wide)
        return (lo, near, far), made

    added, (_, (gate, gated)) = fold(groups, count, first=gate_own)
    hidden = input_rows + added

    second_scale = lax.rsqrt(jnp.mean(hidden * hidden, axis=-1, keepdims=True) + norm_eps)
    normed_mlp = (hidden * second_scale * gain_second).astype(bf16)

    state = {"kept": (), "groups": []}

    def units(lo, hi, pieces):
        if lo == 0:
            state["own"] = pieces
            return ()
        if lo == 1:
            lo, pieces = 0, state["own"] + pieces
        *state["kept"], near, far = hidden_units(lo, pieces, ff_joined, back_all, state["kept"], inner, wide)
        state["groups"].append((lo, near, far))
        return state["kept"]

    inner_act, grad_up, mlp_all = spread(normed_mlp, count, units)
    grad_down = rows_grad(inner_act, back_all, wide)

    def up_grad(done):
        return columns_grad(*after((mlp_all, grad_up), done), 0, 2 * inner)

    grad_normed, grad_ff = fold(state["groups"], count, before=grad_down, first=up_grad)
    down_part = sum_depth(grad_down)
    ff_part = sum_depth(grad_ff)
    scaled = grad_normed * gain_second
    grad_hidden = back_rows + second_scale * (
        scaled
        - hidden * (second_scale * second_scale) * jnp.mean(hidden * scaled, axis=-1, keepdims=True)
    )
    gain_term_mlp = jnp.sum(grad_normed * hidden * second_scale, axis=0)

    state = {"kept": ()}

    def heads(lo, hi, pieces):
        if lo == 3:
            pieces = after(pieces, down_part)
        state["kept"] = retain_back(
            lo, pieces, attn_joined, decays, query, key, value, gate, scores, retained, state["kept"], wide
        )
        if lo > 0:
            return state["kept"]
        act = after(inner_act, pieces)
        state["mlp"] = project(act, ff_joined[:, 2 * inner :], wide)
        return state["kept"], state["mlp"]

    grad_wide, attn_grad_all = spread(grad_hidden.astype(bf16), count, heads)
    grad_out = rows_grad(gated, attn_grad_all, wide)
    out_part = sum_depth(grad_out)

    def wide_grad(done):
        return columns_grad(attn_all, after(grad_wide, done), 0, 2 * dv + 2 * dk)

    def back_terms(done, made):
        return project_back(after(grad_wide, (done, ff_part)), attn_joined, dk, dv)

    mlp_added, grad_wide_weights, (near, far) = fold(
        [(0, *state["mlp"])], count, before=grad_out, first=wide_grad, second=back_terms
    )
    wide_part = sum_depth(grad_wide_weights)
    output = (valid_rows * (hidden + mlp_added)).astype(bf16)
    grad_normed_attn, _ = fold([(0, near, far)], count, first=lambda done: out_part)
    gain_term_attn = jnp.sum(grad_normed_attn * input_rows * first_scale, axis=0)
    scaled_first = grad_normed_attn * gain_first
    tokens_grad = grad_hidden + first_scale * (
        scaled_first
        - input_rows
        * (first_scale * first_scale)
        * jnp.mean(input_rows * scaled_first, axis=-1, keepdims=True)
    )
    tokens_grad = tokens_grad.astype(bf16)

    gain_terms = jnp.stack([gain_term_attn, gain_term_mlp])
    bit = count // 2
    while bit >= 1:
        side = (place // bit) % 2
        cut = gain_terms.reshape(2, 2, -1)
        kept = lax.dynamic_index_in_dim(cut, side, 1, keepdims=False)
        sent = lax.dynamic_index_in_dim(cut, 1 - side, 1, keepdims=False)
        gain_terms = kept + hop(sent, bit, count)
        bit //= 2
    cut = gain_terms.reshape(2, 2, -1)
    kept = lax.dynamic_index_in_dim(cut, core, 1, keepdims=False)
    sent = lax.dynamic_index_in_dim(cut, 1 - core, 1, keepdims=False)
    gain_terms = kept + swap(sent)

    def back_columns(block, widths):
        cuts = [lax.dynamic_slice_in_dim(block, (me ^ k) * shard, shard, 0).astype(bf16) for k in range(PLANE)]
        return place_columns(me_scalar, trade(cuts, count), widths)

    def back_rows_of(block):
        cuts = [lax.dynamic_slice_in_dim(block, (me ^ k) * shard, shard, 1).astype(bf16) for k in range(PLANE)]
        return place_rows(me_scalar, trade(cuts, count))

    down_sum = back_rows_of(down_part)
    ffgate_sum, ffup_sum = back_columns(ff_part, (inner, inner))
    out_sum = back_rows_of(out_part)
    early = output, tokens_grad, gain_terms, down_sum, ffgate_sum, ffup_sum, out_sum
    value_sum, gate_sum, query_sum, key_sum = back_columns(after(wide_part, early), (dv, dv, dk, dk))

    return (
        output,
        tokens_grad,
        query_sum,
        key_sum,
        value_sum,
        gate_sum,
        out_sum,
        ffgate_sum,
        ffup_sum,
        down_sum,
        gain_terms[0],
        gain_terms[1],
    )


def solution(mesh):
    return jax.shard_map(
        on_device,
        mesh=mesh,
        in_specs=(
            P(("dp", "tensor"), None),
            P("dp"),
            P("dp", "tensor"),
            P("dp", "tensor"),
            P("dp", "tensor"),
            P("dp", "tensor"),
            P("tensor", "dp"),
            P("dp", "tensor"),
            P("dp", "tensor"),
            P("tensor", "dp"),
            P("dp"),
            P("dp"),
            P(("dp", "tensor"), None),
        ),
        out_specs=(
            P(("dp", "tensor"), None),
            P(("dp", "tensor"), None),
            P("dp", "tensor"),
            P("dp", "tensor"),
            P("dp", "tensor"),
            P("dp", "tensor"),
            P("tensor", "dp"),
            P("dp", "tensor"),
            P("dp", "tensor"),
            P("tensor", "dp"),
            P(("dp", "tensor")),
            P(("dp", "tensor")),
        ),
        check_vma=False,
    )
```

```python
import functools

import jax
import jax.numpy as jnp
from jax import lax
from jax.experimental import pallas as pl
from jax.experimental.pallas import tpu as pltpu
from jax.sharding import PartitionSpec as P

DK = 256
DV = 512
PLANE = 4
SLOTS = ((0, 1), (1, 3), (3, 4))
VMEM_BYTES = 62 * 1024 * 1024

norm_eps = 1e-06
group_floor = 1.0
tanh_scale = 0.7978845608028654
tanh_cubic = 0.044715

bf16 = jnp.bfloat16
f32 = jnp.float32


def shaped(shape, kind):
    return jax.ShapeDtypeStruct(shape, kind)


def cost(flops, bytes_accessed):
    return pl.CostEstimate(flops=int(flops), bytes_accessed=int(bytes_accessed), transcendentals=0)


def params():
    return pltpu.CompilerParams(vmem_limit_bytes=VMEM_BYTES)


ANY = pl.BlockSpec(memory_space=pl.ANY)


def whole(shape):
    return pl.BlockSpec(shape, lambda i: (0,) * len(shape), pipeline_mode=pl.Buffered(1))


def by_slot(*shape):
    return pl.BlockSpec(shape, lambda i: (i,) + (0,) * (len(shape) - 1))


def dot(left, right):
    return jnp.dot(left, right, preferred_element_type=f32)


def dot_nt(left, right):
    return lax.dot_general(left, right, (((1,), (1,)), ((), ())), preferred_element_type=f32)


def dot_tn(left, right):
    return lax.dot_general(left, right, (((0,), (0,)), ((), ())), preferred_element_type=f32)


def decay_table(positions, head):
    spacing = positions[:, None] - positions[None, :]
    log_rate = jnp.log1p(-jnp.exp2(-5.0 - head.astype(f32)))
    kept_spacing = jnp.where(spacing >= 0, spacing, jnp.zeros_like(spacing)).astype(f32)
    powers = jnp.exp(kept_spacing * log_rate)
    return jnp.where(spacing >= 0, powers, jnp.zeros_like(powers))


def copy_kernel(plan, n_in, me_ref, *refs):
    ins, outs, sem = refs[:n_in], refs[n_in:-1], refs[-1]
    copies = [
        pltpu.make_async_copy(source, target, sem.at[i])
        for i, (source, target) in enumerate(plan(me_ref[0], ins, outs))
    ]
    for one in copies:
        one.start()
    for one in copies:
        one.wait()


def place_copies(plan, n_copies, me, ins, out_shapes):
    moved = 2 * sum(2 * s.size for s in out_shapes)
    return pl.pallas_call(
        functools.partial(copy_kernel, plan, len(ins)),
        in_specs=[pl.BlockSpec(memory_space=pltpu.SMEM)] + [pl.BlockSpec(memory_space=pltpu.VMEM)] * len(ins),
        out_specs=[ANY] * len(out_shapes),
        out_shape=out_shapes,
        scratch_shapes=[pltpu.SemaphoreType.DMA((n_copies,))],
        compiler_params=params(),
        cost_estimate=cost(0, moved),
    )(me, *ins)


def lanes(index, size):
    return pl.ds(pl.multiple_of(index * size, size), size)


def cut_weights(me, by_columns, by_rows):
    rows, cols = by_columns[0].shape[0], by_rows.shape[1]
    parts = [w.shape[1] // PLANE for w in by_columns]
    inner = by_rows.shape[0] // PLANE
    width = sum(parts)
    aligned = cols % 128 == 0
    if not aligned:
        by_rows = jnp.moveaxis(by_rows.reshape(PLANE, inner // rows, rows, cols), 1, 2)
        by_rows = jnp.moveaxis(by_rows.reshape(PLANE, rows, -1), 0, 1).reshape(rows, -1)

    def plan(place, ins, outs):
        copies = []
        for k in range(PLANE):
            at = 0
            for w, part in zip(ins, parts):
                copies.append((w.at[:, lanes(place ^ k, part)], outs[k].at[:, pl.ds(at, part)]))
                at += part
            if not aligned:
                copies.append((ins[-1].at[:, lanes(place ^ k, inner)], outs[k].at[:, pl.ds(width, inner)]))
                continue
            for block in range(inner // rows):
                source = pl.ds(pl.multiple_of((place ^ k) * inner + block * rows, rows), rows)
                copies.append((ins[-1].at[source, :], outs[k].at[:, pl.ds(width + block * cols, cols)]))
        return copies

    shapes = [shaped((rows, width + inner), bf16)] * PLANE
    n_copies = PLANE * (len(parts) + (inner // rows if aligned else 1))
    return place_copies(plan, n_copies, me, [*by_columns, by_rows], shapes)


def join_weights(me, blocks, width):
    rows, inner = blocks[0].shape[0], blocks[0].shape[1] - width
    tall = PLANE * rows
    aligned = rows % 128 == 0
    extra = []
    if not aligned:
        parts = jnp.stack([lax.dynamic_index_in_dim(jnp.stack(blocks), me[0] ^ j, 0, keepdims=False) for j in range(PLANE)])
        parts = parts[:, :, width:].reshape(PLANE, rows, inner // tall, PLANE, rows)
        extra = [jnp.transpose(parts, (3, 1, 2, 0, 4)).reshape(tall, inner)]

    def plan(place, ins, outs):
        copies = []
        for k in range(PLANE):
            copies.append((ins[k].at[:, pl.ds(0, width)], outs[0].at[lanes(place ^ k, rows), pl.ds(0, width)]))
            for block in range(inner // rows if aligned else 0):
                spot = pl.ds(pl.multiple_of(width + (place ^ k) * rows, rows), rows)
                if block >= PLANE:
                    spot = pl.ds(pl.multiple_of(width + (block // PLANE) * tall + (place ^ k) * rows, rows), rows)
                source = ins[k].at[:, pl.ds(width + block * rows, rows)]
                copies.append((source, outs[0].at[pl.ds((block % PLANE) * rows, rows), spot]))
        if not aligned:
            copies.append((ins[PLANE], outs[0].at[:, pl.ds(width, inner)]))
        return copies

    n_copies = PLANE * (1 + inner // rows) if aligned else PLANE + 1
    return place_copies(plan, n_copies, me, [*blocks, *extra], [shaped((tall, width + inner), bf16)])[0]


def load_pieces(pieces, held, sem):
    step = pl.program_id(0)
    rows = pieces[0].shape[0]
    copies = [
        pltpu.make_async_copy(piece, held.at[i // 2, pl.ds((i % 2) * rows, rows)], sem.at[i])
        for i, piece in enumerate(pieces)
    ]

    @pl.when(step == 0)
    def start():
        for one in copies:
            one.start()

    for s in range(len(pieces) // 2):

        @pl.when(step == s)
        def arrive(s=s):
            copies[2 * s].wait()
            copies[2 * s + 1].wait()

    return held[step]


def times_rows(left, right, wide):
    groups = right.shape[1] // wide
    for z in range(right.shape[0] // wide):
        terms = dot(left[:, :wide], right[z * wide : (z + 1) * wide, :wide])
        for g in range(1, groups):
            terms += dot(
                left[:, g * wide : (g + 1) * wide],
                right[z * wide : (z + 1) * wide, g * wide : (g + 1) * wide],
            )
        yield slice(z * wide, (z + 1) * wide), terms


def times_rows_back(left, right, wide):
    made = []
    for g in range(right.shape[1] // wide):
        group = slice(g * wide, (g + 1) * wide)
        terms = dot_nt(left[:, :wide], right[:wide, group])
        for z in range(1, right.shape[0] // wide):
            block = slice(z * wide, (z + 1) * wide)
            terms += dot_nt(left[:, block], right[block, group])
        made.append(terms)
    return made[0] if len(made) == 1 else jnp.concatenate(made, axis=1)


def split_out(terms, near_ref, far_refs, columns):
    rows = near_ref.shape[1]
    near_ref[0, :, columns] = terms[:rows]
    far = terms[rows:].astype(bf16)
    for slot, far_ref in enumerate(far_refs):

        @pl.when(pl.program_id(0) == slot)
        def put(far_ref=far_ref):
            far_ref[:, columns] = far


def split_specs(n, rows, width):
    fars = [pl.BlockSpec((rows, width), lambda i: (0, 0), pipeline_mode=pl.Buffered(1))] * n
    return [by_slot(1, rows, width), *fars]


def split_shapes(n, rows, width):
    return [shaped((n, rows, width), f32)] + [shaped((rows, width), bf16)] * n


def weave(place, own, others, target, width, sem):
    planes, full = 4, own.shape[1]
    shard = own.shape[0] // planes
    copies = []
    for plane in range(planes):
        top = plane * PLANE * shard
        for k in range(PLANE):
            if k == 0:
                source = own.at[pl.ds(plane * shard, shard)]
            else:
                source = others.at[pl.ds((plane * (PLANE - 1) + k - 1) * shard, shard)]
            spot = pl.ds(pl.multiple_of(top + (place ^ k) * shard, shard), shard)
            moves = [(source.at[:, pl.ds(0, width)], target.at[spot, pl.ds(0, width)])]
            spot = pl.ds(pl.multiple_of(width + (place ^ k) * shard, shard), shard)
            for a in range((full - width) // shard):
                piece = source.at[:, pl.ds(width + a * shard, shard)]
                moves.append((piece, target.at[pl.ds(top + a * shard, shard), spot]))
            copies += [pltpu.make_async_copy(*move, sem.at[plane, k, n]) for n, move in enumerate(moves)]
    return copies


def retain_kernel(first, wide, n, n_kept, woven, *refs):
    pieces, refs = refs[: 2 * n], refs[2 * n :]
    if woven:
        place_ref, own, others, decays = refs[:4]
        refs = refs[4:]
    else:
        weights, decays = refs[:2]
        refs = refs[2 + n_kept :]
    query_ref, key_ref, value_ref, gate_ref, scores_ref, retained_ref, gated_ref, rows_ref = refs[:8]
    near_ref, *far_refs = refs[8 : 9 + n]
    if woven:
        joined_ref, held, sem, out_sem, weights, weights_sem, joined_sem = refs[9 + n :]
    else:
        held, sem, out_sem = refs[9 + n :]
    step = pl.program_id(0)
    dk, dv = query_ref.shape[1], value_ref.shape[1]
    if woven:
        copies = weave(place_ref[0], own, others, weights, 2 * dk + 2 * dv, weights_sem)
        keep_weights = pltpu.make_async_copy(weights, joined_ref, joined_sem)

        @pl.when(step == 0)
        def bring():
            for one in copies:
                one.start()

    rows = load_pieces(pieces, held, sem)
    slot_len = rows.shape[0]
    keep = pltpu.make_async_copy(
        held.at[step], rows_ref.at[pl.ds((step + first) * slot_len, slot_len)], out_sem
    )
    keep.start()
    if woven:

        @pl.when(step == 0)
        def brought():
            for one in copies:
                one.wait()
            keep_weights.start()

    query_key = dot(rows, weights[:, : 2 * dk]).astype(bf16)
    query, key = query_key[:, :dk], query_key[:, dk:]
    query_ref[...] = query
    key_ref[...] = key
    scores = (dot_nt(query, key) * decays[...]).astype(bf16)
    scores_ref[...] = scores[None]
    value = dot(rows, weights[:, 2 * dk : 2 * dk + dv]).astype(bf16)
    value_ref[...] = value
    retained = dot(scores, value)
    retained_ref[...] = retained
    scale = lax.rsqrt(jnp.mean(retained * retained, axis=-1, keepdims=True) + group_floor)
    gate = dot(rows, weights[:, 2 * dk + dv : 2 * dk + 2 * dv])
    gate_ref[...] = gate
    gated_ref[...] = (gate * jax.nn.sigmoid(gate) * (retained * scale)).astype(bf16)
    for columns, terms in times_rows(gated_ref[...], weights[:, 2 * dk + 2 * dv :], wide):
        split_out(terms, near_ref, far_refs, columns)
    keep.wait()
    if woven:

        @pl.when(step == n - 1)
        def kept():
            keep_weights.wait()


def retain(first, pieces, weights, decays, kept, dk, dv, wide, place=None):
    n = len(pieces) // 2
    rows, width = pieces[0].shape
    slot_len = 2 * rows
    total = PLANE * slot_len

    def at(cols):
        return pl.BlockSpec((slot_len, cols), lambda i: (i + first, 0))

    kept_specs = [at(dk), at(dk), at(dv), at(dv), None, at(dv), at(dv), ANY]
    kept_specs[4] = pl.BlockSpec((1, slot_len, slot_len), lambda i: (i + first, 0, 0))
    out_specs = kept_specs + split_specs(n, rows, width)
    out_shape = [
        shaped((total, dk), bf16),
        shaped((total, dk), bf16),
        shaped((total, dv), bf16),
        shaped((total, dv), f32),
        shaped((PLANE, slot_len, slot_len), bf16),
        shaped((total, dv), f32),
        shaped((total, dv), bf16),
        shaped((total, width), bf16),
        *split_shapes(n, rows, width),
    ]
    scratch_shapes = [
        pltpu.VMEM((n, slot_len, width), bf16),
        pltpu.SemaphoreType.DMA((2 * n,)),
        pltpu.SemaphoreType.DMA,
    ]
    if place is None:
        given = [weights, decays]
        in_specs = [whole(weights.shape), whole((slot_len, slot_len))]
    else:
        assert not kept
        given = [place, *weights, decays]
        in_specs = [pl.BlockSpec(memory_space=pltpu.SMEM), ANY, ANY, whole((slot_len, slot_len))]
        full = weights[0].shape[1]
        shard = weights[0].shape[0] // 4
        out_specs.append(ANY)
        out_shape.append(shaped((width, full), bf16))
        scratch_shapes += [
            pltpu.VMEM((width, full), bf16),
            pltpu.SemaphoreType.DMA((4, PLANE, 1 + (full - 2 * dk - 2 * dv) // shard)),
            pltpu.SemaphoreType.DMA,
        ]
    return pl.pallas_call(
        functools.partial(retain_kernel, first, wide, n, len(kept), place is not None),
        grid=(n,),
        in_specs=[ANY] * (2 * n) + in_specs + [ANY] * len(kept),
        out_specs=out_specs,
        out_shape=out_shape,
        scratch_shapes=scratch_shapes,
        input_output_aliases={2 * n + len(given) + i: i for i in range(len(kept))},
        compiler_params=params(),
        cost_estimate=cost(2.2 * n * slot_len * width * (2 * dk + 3 * dv), 15e6),
    )(*pieces, *given, *kept)


def project_kernel(wide, left, right, near_ref, *far_refs):
    for columns, terms in times_rows(left[...], right[...], wide):
        split_out(terms, near_ref, far_refs, columns)


def project(left, right, wide):
    total, inner = left.shape
    width = right.shape[0]
    slot_len = total // PLANE
    rows = slot_len // 2
    return pl.pallas_call(
        functools.partial(project_kernel, wide),
        grid=(PLANE,),
        in_specs=[by_slot(slot_len, inner), whole(right.shape)],
        out_specs=split_specs(PLANE, rows, width),
        out_shape=split_shapes(PLANE, rows, width),
        compiler_params=params(),
        cost_estimate=cost(2 * total * inner * width, 20e6),
    )(left, right)


def back_kernel(left, first, second, near_ref, *far_refs):
    dv = second.shape[1]
    narrow = first.shape[1] - dv
    terms = dot_nt(left[:, :dv], first[:, narrow:]) + dot_nt(left[:, dv : 2 * dv], second[...])
    terms += dot_nt(left[:, 2 * dv :], first[:, :narrow])
    split_out(terms, near_ref, far_refs, slice(None))


def project_back(left, joined, dk, dv):
    total, inner = left.shape
    width = joined.shape[0]
    slot_len = total // PLANE
    rows = slot_len // 2
    return pl.pallas_call(
        back_kernel,
        grid=(PLANE,),
        in_specs=[
            by_slot(slot_len, inner),
            whole((width, 2 * dk + dv)),
            pl.BlockSpec((width, dv), lambda i: (0, 2), pipeline_mode=pl.Buffered(1)),
        ],
        out_specs=split_specs(PLANE, rows, width),
        out_shape=split_shapes(PLANE, rows, width),
        compiler_params=params(),
        cost_estimate=cost(2 * total * inner * width, 20e6),
    )(left, joined, joined)


def fold_kernel(*refs):
    nears, arriveds = refs[:3], refs[3:6]
    x1_ref, y2_ref, x3_ref, y3_ref, keep_x_ref, keep_y_ref = refs[6:]
    half = x1_ref.shape[0]
    targets = ((x1_ref, keep_x_ref), (keep_y_ref, y2_ref), (x3_ref, y3_ref))
    for near, arrived, (first, second) in zip(nears, arriveds, targets):
        first[...] = (near[0, :half] + arrived[:half].astype(f32)).astype(first.dtype)
        second[...] = (near[0, half:] + arrived[half:].astype(f32)).astype(second.dtype)


def fold_cut(slots):
    nears, arriveds, spots = zip(*slots)
    _, rows, width = nears[0].shape
    half = rows // 2
    part = width // 4
    kinds = (bf16, bf16, bf16, bf16, f32, f32)
    given = [pl.BlockSpec((1, rows, part), lambda i, spot=spot: (spot, 0, i)) for spot in spots]
    given += [pl.BlockSpec((rows, part), lambda i: (0, i))] * len(spots)
    return pl.pallas_call(
        fold_kernel,
        grid=(width // part,),
        in_specs=given,
        out_specs=[pl.BlockSpec((half, part), lambda i: (0, i))] * len(kinds),
        out_shape=[shaped((half, width), kind) for kind in kinds],
        compiler_params=params(),
        cost_estimate=cost(1e6, 12e6),
    )(*nears, *arriveds)


def hidden_kernel(first, wide, n, n_kept, *refs):
    pieces, (weights, down_weights, back) = refs[: 2 * n], refs[2 * n : 2 * n + 3]
    act_ref, grad_ref, rows_ref, near_ref, *far_refs = refs[2 * n + 3 + n_kept : 3 * n + 7 + n_kept]
    held, sem, out_sem = refs[3 * n + 7 + n_kept :]
    rows = load_pieces(pieces, held, sem)
    step = pl.program_id(0)
    slot_len = rows.shape[0]
    inner = act_ref.shape[1]
    keep = pltpu.make_async_copy(
        held.at[step], rows_ref.at[pl.ds((step + first) * slot_len, slot_len)], out_sem
    )
    keep.start()
    weights = weights[...]
    up = dot(rows, weights[:, :inner])
    value = dot(rows, weights[:, inner:])
    slope = jnp.tanh(tanh_scale * (up + tanh_cubic * (up * up * up)))
    gelu = 0.5 * up * (1.0 + slope)
    act_ref[...] = (gelu * value).astype(bf16)
    rise = 0.5 * (1.0 + slope) + 0.5 * up * (1.0 - slope * slope) * (
        tanh_scale * (1.0 + 3.0 * tanh_cubic * (up * up))
    )
    grad = times_rows_back(back[...], down_weights[...], wide)
    grad_ref[:, :inner] = (grad * value * rise).astype(bf16)
    grad_ref[:, inner:] = (grad * gelu).astype(bf16)
    split_out(dot_nt(grad_ref[...], weights), near_ref, far_refs, slice(None))
    keep.wait()


def hidden_units(first, pieces, joined, back, kept, inner, wide):
    n = len(pieces) // 2
    rows, width = pieces[0].shape
    slot_len = 2 * rows
    total = back.shape[0]

    def at(cols):
        return pl.BlockSpec((slot_len, cols), lambda i: (i + first, 0))

    return pl.pallas_call(
        functools.partial(hidden_kernel, first, wide, n, len(kept)),
        grid=(n,),
        in_specs=[ANY] * (2 * n)
        + [
            pl.BlockSpec((width, 2 * inner), lambda i: (0, 0), pipeline_mode=pl.Buffered(1)),
            pl.BlockSpec((width, inner), lambda i: (0, 2), pipeline_mode=pl.Buffered(1)),
            at(width),
        ]
        + [ANY] * len(kept),
        out_specs=[at(inner), at(2 * inner), ANY, *split_specs(n, rows, width)],
        out_shape=[
            shaped((total, inner), bf16),
            shaped((total, 2 * inner), bf16),
            shaped((total, width), bf16),
            *split_shapes(n, rows, width),
        ],
        scratch_shapes=[
            pltpu.VMEM((n, slot_len, width), bf16),
            pltpu.SemaphoreType.DMA((2 * n,)),
            pltpu.SemaphoreType.DMA,
        ],
        input_output_aliases={2 * n + 3 + i: i for i in range(len(kept))},
        compiler_params=params(),
        cost_estimate=cost(10 * n * slot_len * width * inner, 15e6),
    )(*pieces, joined, joined, back, *kept)


def retain_back_kernel(first, wide, n, n_kept, *refs):
    pieces = refs[: 2 * n]
    out_weights, decays, query, key, value, gate_ref, scores, retained_ref = refs[2 * n : 2 * n + 8]
    grad_ref, rows_ref = refs[2 * n + 8 + n_kept : 2 * n + 10 + n_kept]
    held, sem, out_sem = refs[2 * n + 10 + n_kept :]
    rows = load_pieces(pieces, held, sem)
    step = pl.program_id(0)
    slot_len = rows.shape[0]
    keep = pltpu.make_async_copy(
        held.at[step], rows_ref.at[pl.ds((step + first) * slot_len, slot_len)], out_sem
    )
    keep.start()
    dk, dv = query.shape[1], value.shape[1]
    grad = times_rows_back(rows, out_weights[...], wide)
    retained, gate = retained_ref[...], gate_ref[...]
    scale = lax.rsqrt(jnp.mean(retained * retained, axis=-1, keepdims=True) + group_floor)
    sigma = jax.nn.sigmoid(gate)
    normed = retained * scale
    grad_ref[:, dv : 2 * dv] = (grad * normed * (sigma * (1.0 + gate * (1.0 - sigma)))).astype(bf16)
    grad = grad * (gate * sigma)
    mean = jnp.mean(normed * grad, axis=-1, keepdims=True)
    grad_retained = (scale * (grad - normed * mean)).astype(bf16)
    grad_scores = (dot_nt(grad_retained, value[...]) * decays[...]).astype(bf16)
    grad_ref[:, :dv] = dot_tn(scores[0], grad_retained).astype(bf16)
    grad_ref[:, 2 * dv : 2 * dv + dk] = dot(grad_scores, key[...]).astype(bf16)
    grad_ref[:, 2 * dv + dk :] = dot_tn(grad_scores, query[...]).astype(bf16)
    keep.wait()


def retain_back(first, pieces, joined, decays, query, key, value, gate, scores, retained, kept, wide):
    n = len(pieces) // 2
    rows, width = pieces[0].shape
    slot_len = 2 * rows
    total, dk = query.shape
    dv = value.shape[1]

    def at(cols):
        return pl.BlockSpec((slot_len, cols), lambda i: (i + first, 0))

    return pl.pallas_call(
        functools.partial(retain_back_kernel, first, wide, n, len(kept)),
        grid=(n,),
        in_specs=[ANY] * (2 * n)
        + [
            pl.BlockSpec((width, dv), lambda i: (0, 3), pipeline_mode=pl.Buffered(1)),
            whole((slot_len, slot_len)),
            at(dk),
            at(dk),
            at(dv),
            at(dv),
            pl.BlockSpec((1, slot_len, slot_len), lambda i: (i + first, 0, 0)),
            at(dv),
        ]
        + [ANY] * len(kept),
        out_specs=[at(2 * dk + 2 * dv), ANY],
        out_shape=[shaped((total, 2 * dk + 2 * dv), bf16), shaped((total, width), bf16)],
        scratch_shapes=[
            pltpu.VMEM((n, slot_len, width), bf16),
            pltpu.SemaphoreType.DMA((2 * n,)),
            pltpu.SemaphoreType.DMA,
        ],
        input_output_aliases={2 * n + 8 + i: i for i in range(len(kept))},
        compiler_params=params(),
        cost_estimate=cost(4 * n * slot_len * width * dv, 15e6),
    )(*pieces, joined, decays, query, key, value, gate, scores, retained, *kept)


def grad_kernel(left, right, grad_ref):
    grad_ref[...] = dot_tn(left[...], right[...]).astype(bf16)


def columns_grad(left, right, block, cols):
    total, width = left.shape
    part = width // 4
    return pl.pallas_call(
        grad_kernel,
        grid=(width // part,),
        in_specs=[
            pl.BlockSpec((total, part), lambda i: (0, i)),
            pl.BlockSpec((total, cols), lambda i: (0, block), pipeline_mode=pl.Buffered(1)),
        ],
        out_specs=by_slot(part, cols),
        out_shape=shaped((width, cols), bf16),
        compiler_params=params(),
        cost_estimate=cost(2 * total * width * cols, 20e6),
    )(left, right)


def places_grad_kernel(me_ref, left, right, own, others, held, sem):
    step = pl.program_id(0)
    slot = step % 2
    held[slot] = dot_tn(left[...], right[...]).astype(bf16)
    shard = held.shape[1] // PLANE

    def each(step, slot, act):
        def copy(j, target):
            return pltpu.make_async_copy(held.at[slot, pl.ds(j * shard, shard)], target, sem.at[slot, j])

        for j in range(PLANE):
            k = me_ref[0] ^ j

            @pl.when(k == 0)
            def here(j=j):
                act(copy(j, own.at[pl.ds(pl.multiple_of(step * shard, shard), shard)]))

            @pl.when(k != 0)
            def there(j=j, k=k):
                at = pl.multiple_of((step * (PLANE - 1) + k - 1) * shard, shard)
                act(copy(j, others.at[pl.ds(at, shard)]))

    each(step, slot, lambda one: one.start())

    @pl.when(step > 0)
    def before():
        each(step - 1, 1 - slot, lambda one: one.wait())

    @pl.when(step == pl.num_programs(0) - 1)
    def last():
        each(step, slot, lambda one: one.wait())


def places_grad(me, left, right, depth):
    total, width = left.shape
    cols = right.shape[1]
    part = width // depth
    return pl.pallas_call(
        places_grad_kernel,
        grid=(depth,),
        in_specs=[
            pl.BlockSpec(memory_space=pltpu.SMEM),
            pl.BlockSpec((total, part), lambda i: (0, i)),
            whole((total, cols)),
        ],
        out_specs=[ANY, ANY],
        out_shape=[
            shaped((width // PLANE, cols), bf16),
            shaped((width // PLANE * (PLANE - 1), cols), bf16),
        ],
        scratch_shapes=[pltpu.VMEM((2, part, cols), bf16), pltpu.SemaphoreType.DMA((2, PLANE))],
        compiler_params=params(),
        cost_estimate=cost(2 * total * width * cols, 20e6),
    )(me, left, right)


def rows_grad(left, right, wide):
    total, inner = left.shape
    blocks = right.shape[1] // wide
    return pl.pallas_call(
        grad_kernel,
        grid=(blocks,),
        in_specs=[whole((total, inner)), pl.BlockSpec((total, wide), lambda i: (0, i))],
        out_specs=by_slot(inner, wide),
        out_shape=shaped((blocks * inner, wide), bf16),
        compiler_params=params(),
        cost_estimate=cost(2 * total * inner * wide * blocks, 20e6),
    )(left, right)


def place_grads_kernel(n, me_ref, *refs):
    ins, outs, held, sem = refs[:PLANE], refs[PLANE : PLANE + n], refs[-2], refs[-1]
    place = me_ref[0]
    copies = []
    for k in range(PLANE):
        held[k] = ins[k][...].astype(f32)
        at = 0
        for i, out in enumerate(outs):
            part = out.shape[1] // PLANE
            one = pltpu.make_async_copy(
                held.at[k, :, pl.ds(at, part)], out.at[:, lanes(place ^ k, part)], sem.at[k * n + i]
            )
            one.start()
            copies.append(one)
            at += part
    for one in copies:
        one.wait()


def place_columns(me, blocks, widths):
    rows = blocks[0].shape[0]
    n = len(widths)
    return pl.pallas_call(
        functools.partial(place_grads_kernel, n),
        in_specs=[pl.BlockSpec(memory_space=pltpu.SMEM)]
        + [pl.BlockSpec(memory_space=pltpu.VMEM)] * PLANE,
        out_specs=[ANY] * n,
        out_shape=[shaped((rows, PLANE * w), f32) for w in widths],
        scratch_shapes=[
            pltpu.VMEM((PLANE, *blocks[0].shape), f32),
            pltpu.SemaphoreType.DMA((PLANE * n,)),
        ],
        compiler_params=params(),
        cost_estimate=cost(0, 8e6),
    )(me, *blocks)


def place_rows_kernel(me_ref, *refs):
    ins, out, held, sem = refs[:PLANE], refs[PLANE], refs[-2], refs[-1]
    rows = ins[0].shape[0]
    copies = []
    for k in range(PLANE):
        held[k] = ins[k][...].astype(f32)
        one = pltpu.make_async_copy(held.at[k], out.at[lanes(me_ref[0] ^ k, rows), :], sem.at[k])
        one.start()
        copies.append(one)
    for one in copies:
        one.wait()


def place_rows(me, blocks):
    rows, cols = blocks[0].shape
    return pl.pallas_call(
        place_rows_kernel,
        in_specs=[pl.BlockSpec(memory_space=pltpu.SMEM)]
        + [pl.BlockSpec(memory_space=pltpu.VMEM)] * PLANE,
        out_specs=ANY,
        out_shape=shaped((PLANE * rows, cols), f32),
        scratch_shapes=[pltpu.VMEM((PLANE, rows, cols), f32), pltpu.SemaphoreType.DMA((PLANE,))],
        compiler_params=params(),
        cost_estimate=cost(0, 4e6),
    )(me, *blocks)


def hop(value, bits, count):
    return lax.ppermute(value, "dp", [(i, i ^ bits) for i in range(count)])


def swap(value):
    return lax.ppermute(value, "tensor", [(0, 1), (1, 0)])


def trade(blocks, count):
    return [blocks[0]] + [hop(blocks[k], k, count) for k in range(1, PLANE)]


def spread(mine, count, beside=None):
    half = mine.shape[0] // 2
    from_x = hop(mine, 1, count)
    from_y = hop(mine, 2, count)
    pieces = [mine, swap(mine)]
    if beside:
        from_x, from_y = after((from_x, from_y), beside(0, 1, pieces))
    far_a = hop(from_x[:half], 2, count)
    far_b = hop(from_y[half:], 1, count)
    nearer = [from_x, swap(from_x), from_y, swap(from_y)]
    if beside:
        far_a, far_b = after((far_a, far_b), beside(1, 3, nearer))
    far = jnp.concatenate([far_a, far_b])
    far = [far, swap(far)]
    if beside:
        return beside(3, 4, far)
    return pieces + nearer + far


def fold(groups, count, before=None, first=None, second=None):
    slots = {}

    def take(lo, near, *fars):
        for k, far in enumerate(fars):
            slots[lo + k] = near, swap(far), k

    for group in groups:
        take(*group)
    given = [(near, arrived) for near, arrived, _ in (slots[k] for k in (1, 2, 3))]
    made = []
    if before:
        made.append(before(slots[1][1]))
        given = after(given, made)
    cut = fold_cut([(*pair, slots[k][2]) for k, pair in zip((1, 2, 3), given)])
    to_x1, to_y2, to_x3, to_y3, keep_x, keep_y = cut
    half, width = to_x1.shape
    x1, y2 = hop(to_x1, 1, count), hop(to_y2, 2, count)
    x3, y3 = hop(to_x3, 1, count), hop(to_y3, 2, count)
    if first:
        made.append(first((to_x3, to_y3)))
        x3, y3 = after((x3, y3), made)
    if 0 not in slots:
        take(*made[-1][0])
    near_0, arrived_0, spot = slots[0]
    to_y, to_x = (keep_y + x3.astype(f32)).astype(bf16), (keep_x + y3.astype(f32)).astype(bf16)
    last_y, last_x = hop(to_y, 2, count), hop(to_x, 1, count)
    if second:
        made.append(second((to_x, to_y)))
        last_y, last_x = after((last_y, last_x), made[-1])
    near_0, arrived_0 = near_0[spot], arrived_0.astype(f32)
    summed = [
        near_0[:half] + arrived_0[:half] + (x1.astype(f32) + last_y.astype(f32)),
        near_0[half:] + arrived_0[half:] + (y2.astype(f32) + last_x.astype(f32)),
    ]
    return jnp.concatenate(summed), *made


def after(values, done):
    return lax.optimization_barrier((values, done))[0]


def on_device(
    tokens,
    lengths,
    w_query,
    w_key,
    w_value,
    w_gate,
    w_out,
    w_ffgate,
    w_ffup,
    w_ffdown,
    gain_attn,
    gain_mlp,
    cotangent,
):
    count = lax.axis_size("dp")
    depth = count // PLANE
    columns = [[q + PLANE * z for z in range(depth)] for q in range(PLANE)]
    place = lax.axis_index("dp")
    me = place % PLANE
    me_scalar = me.reshape(1).astype(jnp.int32)
    core = lax.axis_index("tensor")
    rows, width = tokens.shape
    wide = width // depth
    shard = w_query.shape[0]
    dk = w_query.shape[1] // PLANE
    dv = w_value.shape[1] // PLANE
    inner = w_ffgate.shape[1] // PLANE
    assert dk == DK and dv == DV

    def gather_depth(block):
        return lax.all_gather(block, "dp", axis=0, tiled=True, axis_index_groups=columns)

    def sum_depth(block):
        return lax.psum_scatter(block, "dp", scatter_dimension=0, tiled=True, axis_index_groups=columns)

    attn_cuts = cut_weights(me_scalar, (w_query, w_key, w_value, w_gate), w_out)
    attn_blocks = trade(attn_cuts, count)
    attn_width = 2 * dk + 2 * dv
    if depth == 4:
        own_gathered = gather_depth(attn_cuts[0])
        attn_own = jnp.concatenate(attn_blocks[1:])
        attn_weights = own_gathered, gather_depth(attn_own)
    else:
        attn_own = join_weights(me_scalar, attn_blocks, attn_width)
        attn_joined = gather_depth(attn_own)

    gains = jnp.stack([gain_attn, gain_mlp])[None]
    step = 1
    while step < count:
        gains = jnp.concatenate([gains, hop(gains, step, count)])
        step *= 2
    gains = jnp.take(gains, place ^ jnp.arange(count), axis=0).astype(f32)
    gain_first = gains[:, 0].reshape(1, width)
    gain_second = gains[:, 1].reshape(1, width)

    input_rows = tokens.astype(f32)
    first_scale = lax.rsqrt(jnp.mean(input_rows * input_rows, axis=-1, keepdims=True) + norm_eps)
    normed_attn = (input_rows * first_scale * gain_first).astype(bf16)
    attn_pieces = spread(after(normed_attn, attn_own), count)

    ff_cuts = after(cut_weights(me_scalar, (w_ffgate, w_ffup), w_ffdown), attn_pieces)
    ff_own = join_weights(me_scalar, trade(ff_cuts, count), 2 * inner)
    ff_joined = gather_depth(ff_own)

    local = jnp.arange(rows, dtype=jnp.int32)
    valid_rows = ((core * rows + local) < lengths[0]).astype(f32)[:, None]
    back_rows = valid_rows * cotangent.astype(f32)
    back_pieces = spread(after(back_rows.astype(bf16), ff_own), count)
    back_all = jnp.concatenate(back_pieces)

    positions = jnp.concatenate([core * rows + local, (1 - core) * rows + local])
    decays = decay_table(positions, core * PLANE + me)
    attn_pieces = after(attn_pieces, back_all)
    kept, groups = [], []
    if depth == 4:
        *kept, attn_joined = retain(1, attn_pieces[2:], attn_weights, decays, kept, dk, dv, wide, me_scalar)
    else:
        kept = retain(1, attn_pieces[2:], attn_joined, decays, kept, dk, dv, wide)
    kept, terms = kept[:8], kept[8:]
    groups.append((1, *terms))

    def retain_own(done):
        pieces = after(attn_pieces[:2], done)
        made = retain(0, pieces, attn_joined, decays, kept, dk, dv, wide)
        return (0, *made[8:]), made[:8]

    added, (_, made) = fold(groups, count, first=retain_own)
    query, key, value, gate, scores, retained, gated, attn_all = made
    hidden = input_rows + added

    second_scale = lax.rsqrt(jnp.mean(hidden * hidden, axis=-1, keepdims=True) + norm_eps)
    normed_mlp = (hidden * second_scale * gain_second).astype(bf16)

    state = {"kept": (), "groups": []}

    def units(lo, hi, pieces):
        if lo == 0:
            state["own"] = pieces
            return ()
        if lo == 1:
            lo, pieces = 0, state["own"] + pieces
        made = hidden_units(lo, pieces, ff_joined, back_all, state["kept"], inner, wide)
        state["kept"] = made[:3]
        state["groups"].append((lo, *made[3:]))
        return state["kept"]

    inner_act, grad_up, mlp_all = spread(normed_mlp, count, units)

    def down_grad(_):
        return rows_grad(inner_act, back_all, wide)

    def up_grad(done):
        return columns_grad(*after((mlp_all, grad_up), done), 0, 2 * inner)

    grad_normed, grad_down, grad_ff = fold(state["groups"], count, down_grad, up_grad)
    down_part = sum_depth(grad_down)
    ff_part = sum_depth(grad_ff)
    scaled = grad_normed * gain_second
    grad_hidden = back_rows + second_scale * (
        scaled
        - hidden * (second_scale * second_scale) * jnp.mean(hidden * scaled, axis=-1, keepdims=True)
    )
    gain_term_mlp = jnp.sum(grad_normed * hidden * second_scale, axis=0)

    state = {"kept": ()}

    def heads(lo, hi, pieces):
        if lo == 3:
            pieces = after(pieces, down_part)
        state["kept"] = retain_back(
            lo, pieces, attn_joined, decays, query, key, value, gate, scores, retained, state["kept"], wide
        )
        if lo > 0:
            return state["kept"]
        act = after(inner_act, pieces)
        state["mlp"] = project(act, ff_joined[:, 2 * inner :], wide)
        return state["kept"], state["mlp"]

    grad_wide, attn_grad_all = spread(grad_hidden.astype(bf16), count, heads)
    grad_out = rows_grad(gated, attn_grad_all, wide)
    out_part = sum_depth(grad_out)

    own_grad, others_grad = places_grad(me_scalar, attn_all, after(grad_wide, grad_out), depth)

    def back_terms(done):
        return project_back(after(grad_wide, (done, ff_part)), attn_joined, dk, dv)

    mlp_added, _, attn_terms = fold([(0, *state["mlp"])], count, lambda _: others_grad, back_terms)
    others_part = sum_depth(others_grad)
    output = (valid_rows * (hidden + mlp_added)).astype(bf16)
    grad_normed_attn, *_ = fold([(0, *attn_terms)], count, lambda _: mlp_added, lambda _: out_part)
    own_grad = after(own_grad, grad_normed_attn)
    own_part = sum_depth(own_grad)
    gain_term_attn = jnp.sum(grad_normed_attn * input_rows * first_scale, axis=0)
    scaled_first = grad_normed_attn * gain_first
    tokens_grad = grad_hidden + first_scale * (
        scaled_first
        - input_rows
        * (first_scale * first_scale)
        * jnp.mean(input_rows * scaled_first, axis=-1, keepdims=True)
    )
    tokens_grad = tokens_grad.astype(bf16)

    def back_columns(block, widths):
        cuts = [lax.dynamic_slice_in_dim(block, (me ^ k) * shard, shard, 0).astype(bf16) for k in range(PLANE)]
        return place_columns(me_scalar, trade(cuts, count), widths)

    def back_rows_of(block):
        cuts = [lax.dynamic_slice_in_dim(block, (me ^ k) * shard, shard, 1).astype(bf16) for k in range(PLANE)]
        return place_rows(me_scalar, trade(cuts, count))

    down_sum = back_rows_of(down_part)
    ffgate_sum, ffup_sum = back_columns(ff_part, (inner, inner))
    out_sum = back_rows_of(out_part)
    blocks = [hop(others_part[k * shard : (k + 1) * shard], k + 1, count) for k in range(PLANE - 1)]
    gain_terms = jnp.stack([gain_term_attn, gain_term_mlp])
    bit = count // 2
    while bit >= 1:
        if bit == PLANE // 2:
            gain_terms = after(gain_terms, blocks)
        side = (place // bit) % 2
        cut = gain_terms.reshape(2, 2, -1)
        kept = lax.dynamic_index_in_dim(cut, side, 1, keepdims=False)
        sent = lax.dynamic_index_in_dim(cut, 1 - side, 1, keepdims=False)
        gain_terms = kept + hop(sent, bit, count)
        bit //= 2
    cut = gain_terms.reshape(2, 2, -1)
    kept = lax.dynamic_index_in_dim(cut, core, 1, keepdims=False)
    sent = lax.dynamic_index_in_dim(cut, 1 - core, 1, keepdims=False)
    gain_terms = kept + swap(sent)
    early = output, tokens_grad, gain_terms, down_sum, ffgate_sum, ffup_sum, out_sum
    value_sum, gate_sum, query_sum, key_sum = place_columns(
        me_scalar, [after(own_part, (blocks, early)), *blocks], (dv, dv, dk, dk)
    )

    return (
        output,
        tokens_grad,
        query_sum,
        key_sum,
        value_sum,
        gate_sum,
        out_sum,
        ffgate_sum,
        ffup_sum,
        down_sum,
        gain_terms[0],
        gain_terms[1],
    )


def solution(mesh):
    return jax.shard_map(
        on_device,
        mesh=mesh,
        in_specs=(
            P(("dp", "tensor"), None),
            P("dp"),
            P("dp", "tensor"),
            P("dp", "tensor"),
            P("dp", "tensor"),
            P("dp", "tensor"),
            P("tensor", "dp"),
            P("dp", "tensor"),
            P("dp", "tensor"),
            P("tensor", "dp"),
            P("dp"),
            P("dp"),
            P(("dp", "tensor"), None),
        ),
        out_specs=(
            P(("dp", "tensor"), None),
            P(("dp", "tensor"), None),
            P("dp", "tensor"),
            P("dp", "tensor"),
            P("dp", "tensor"),
            P("dp", "tensor"),
            P("tensor", "dp"),
            P("dp", "tensor"),
            P("dp", "tensor"),
            P("tensor", "dp"),
            P(("dp", "tensor")),
            P(("dp", "tensor")),
        ),
        check_vma=False,
    )
```

```python
import functools

import jax
import jax.numpy as jnp
from jax import lax
from jax.experimental import pallas as pl
from jax.experimental.pallas import tpu as pltpu
from jax.sharding import PartitionSpec as P

DK = 256
DV = 512
PLANE = 4
SLOTS = ((0, 1), (1, 3), (3, 4))

norm_eps = 1e-06
group_floor = 1.0
tanh_scale = 0.7978845608028654
tanh_cubic = 0.044715

bf16 = jnp.bfloat16
f32 = jnp.float32


def shaped(shape, kind):
    return jax.ShapeDtypeStruct(shape, kind)


def cost(flops, bytes_accessed):
    return pl.CostEstimate(flops=int(flops), bytes_accessed=int(bytes_accessed), transcendentals=0)


def params(mib=62):
    return pltpu.CompilerParams(vmem_limit_bytes=mib * 1024 * 1024)


ANY = pl.BlockSpec(memory_space=pl.ANY)


def whole(shape):
    return pl.BlockSpec(shape, lambda i: (0,) * len(shape), pipeline_mode=pl.Buffered(1))


def by_slot(*shape):
    return pl.BlockSpec(shape, lambda i: (i,) + (0,) * (len(shape) - 1))


def dot(left, right):
    return jnp.dot(left, right, preferred_element_type=f32)


def dot_nt(left, right):
    return lax.dot_general(left, right, (((1,), (1,)), ((), ())), preferred_element_type=f32)


def dot_tn(left, right):
    return lax.dot_general(left, right, (((0,), (0,)), ((), ())), preferred_element_type=f32)


def decay_table(positions, head):
    spacing = positions[:, None] - positions[None, :]
    log_rate = jnp.log1p(-jnp.exp2(-5.0 - head.astype(f32)))
    kept_spacing = jnp.where(spacing >= 0, spacing, jnp.zeros_like(spacing)).astype(f32)
    powers = jnp.exp(kept_spacing * log_rate)
    return jnp.where(spacing >= 0, powers, jnp.zeros_like(powers))


def copy_kernel(plan, n_in, me_ref, *refs):
    ins, outs, sem = refs[:n_in], refs[n_in:-1], refs[-1]
    copies = [
        pltpu.make_async_copy(source, target, sem.at[i])
        for i, (source, target) in enumerate(plan(me_ref[0], ins, outs))
    ]
    for one in copies:
        one.start()
    for one in copies:
        one.wait()


def place_copies(plan, n_copies, me, ins, out_shapes):
    moved = 2 * sum(2 * s.size for s in out_shapes)
    return pl.pallas_call(
        functools.partial(copy_kernel, plan, len(ins)),
        in_specs=[pl.BlockSpec(memory_space=pltpu.SMEM)] + [pl.BlockSpec(memory_space=pltpu.VMEM)] * len(ins),
        out_specs=[ANY] * len(out_shapes),
        out_shape=out_shapes,
        scratch_shapes=[pltpu.SemaphoreType.DMA((n_copies,))],
        compiler_params=params(),
        cost_estimate=cost(0, moved),
    )(me, *ins)


def lanes(index, size):
    return pl.ds(pl.multiple_of(index * size, size), size)


def cut_weights(me, by_columns, by_rows):
    rows, cols = by_columns[0].shape[0], by_rows.shape[1]
    parts = [w.shape[1] // PLANE for w in by_columns]
    inner = by_rows.shape[0] // PLANE
    width = sum(parts)
    aligned = cols % 128 == 0
    if not aligned:
        by_rows = jnp.moveaxis(by_rows.reshape(PLANE, inner // rows, rows, cols), 1, 2)
        by_rows = jnp.moveaxis(by_rows.reshape(PLANE, rows, -1), 0, 1).reshape(rows, -1)

    def plan(place, ins, outs):
        copies = []
        for k in range(PLANE):
            at = 0
            for w, part in zip(ins, parts):
                copies.append((w.at[:, lanes(place ^ k, part)], outs[k].at[:, pl.ds(at, part)]))
                at += part
            if not aligned:
                copies.append((ins[-1].at[:, lanes(place ^ k, inner)], outs[k].at[:, pl.ds(width, inner)]))
                continue
            for block in range(inner // rows):
                source = pl.ds(pl.multiple_of((place ^ k) * inner + block * rows, rows), rows)
                copies.append((ins[-1].at[source, :], outs[k].at[:, pl.ds(width + block * cols, cols)]))
        return copies

    shapes = [shaped((rows, width + inner), bf16)] * PLANE
    n_copies = PLANE * (len(parts) + (inner // rows if aligned else 1))
    return place_copies(plan, n_copies, me, [*by_columns, by_rows], shapes)


def join_weights(me, blocks, width):
    rows, inner = blocks[0].shape[0], blocks[0].shape[1] - width
    tall = PLANE * rows
    aligned = rows % 128 == 0
    extra = []
    if not aligned:
        parts = jnp.stack([lax.dynamic_index_in_dim(jnp.stack(blocks), me[0] ^ j, 0, keepdims=False) for j in range(PLANE)])
        parts = parts[:, :, width:].reshape(PLANE, rows, inner // tall, PLANE, rows)
        extra = [jnp.transpose(parts, (3, 1, 2, 0, 4)).reshape(tall, inner)]

    def plan(place, ins, outs):
        copies = []
        for k in range(PLANE):
            copies.append((ins[k].at[:, pl.ds(0, width)], outs[0].at[lanes(place ^ k, rows), pl.ds(0, width)]))
            for block in range(inner // rows if aligned else 0):
                spot = pl.ds(pl.multiple_of(width + (place ^ k) * rows, rows), rows)
                if block >= PLANE:
                    spot = pl.ds(pl.multiple_of(width + (block // PLANE) * tall + (place ^ k) * rows, rows), rows)
                source = ins[k].at[:, pl.ds(width + block * rows, rows)]
                copies.append((source, outs[0].at[pl.ds((block % PLANE) * rows, rows), spot]))
        if not aligned:
            copies.append((ins[PLANE], outs[0].at[:, pl.ds(width, inner)]))
        return copies

    n_copies = PLANE * (1 + inner // rows) if aligned else PLANE + 1
    return place_copies(plan, n_copies, me, [*blocks, *extra], [shaped((tall, width + inner), bf16)])[0]


def load_pieces(pieces, held, sem):
    step = pl.program_id(0)
    rows = pieces[0].shape[0]
    copies = [
        pltpu.make_async_copy(piece, held.at[i // 2, pl.ds((i % 2) * rows, rows)], sem.at[i])
        for i, piece in enumerate(pieces)
    ]

    @pl.when(step == 0)
    def start():
        for one in copies:
            one.start()

    for s in range(len(pieces) // 2):

        @pl.when(step == s)
        def arrive(s=s):
            copies[2 * s].wait()
            copies[2 * s + 1].wait()

    return held[step]


def times_rows(left, right, wide):
    groups = right.shape[1] // wide
    for z in range(right.shape[0] // wide):
        terms = dot(left[:, :wide], right[z * wide : (z + 1) * wide, :wide])
        for g in range(1, groups):
            terms += dot(
                left[:, g * wide : (g + 1) * wide],
                right[z * wide : (z + 1) * wide, g * wide : (g + 1) * wide],
            )
        yield slice(z * wide, (z + 1) * wide), terms


def times_rows_back(left, right, wide):
    made = []
    for g in range(right.shape[1] // wide):
        group = slice(g * wide, (g + 1) * wide)
        terms = dot_nt(left[:, :wide], right[:wide, group])
        for z in range(1, right.shape[0] // wide):
            block = slice(z * wide, (z + 1) * wide)
            terms += dot_nt(left[:, block], right[block, group])
        made.append(terms)
    return made[0] if len(made) == 1 else jnp.concatenate(made, axis=1)


def split_out(terms, near_ref, far_refs, columns):
    rows = near_ref.shape[1]
    near_ref[0, :, columns] = terms[:rows]
    far = terms[rows:].astype(bf16)
    for slot, far_ref in enumerate(far_refs):

        @pl.when(pl.program_id(0) == slot)
        def put(far_ref=far_ref):
            far_ref[:, columns] = far


def split_specs(n, rows, width):
    fars = [pl.BlockSpec((rows, width), lambda i: (0, 0), pipeline_mode=pl.Buffered(1))] * n
    return [by_slot(1, rows, width), *fars]


def split_shapes(n, rows, width, place=shaped):
    return [place((n, rows, width), f32)] + [place((rows, width), bf16)] * n


def weave(place, own, others, target, width, sem):
    planes, full = 4, own.shape[1]
    shard = own.shape[0] // planes
    copies = []
    for plane in range(planes):
        top = plane * PLANE * shard
        for k in range(PLANE):
            if k == 0:
                source = own.at[pl.ds(plane * shard, shard)]
            else:
                source = others.at[pl.ds((plane * (PLANE - 1) + k - 1) * shard, shard)]
            spot = pl.ds(pl.multiple_of(top + (place ^ k) * shard, shard), shard)
            moves = [(source.at[:, pl.ds(0, width)], target.at[spot, pl.ds(0, width)])]
            spot = pl.ds(pl.multiple_of(width + (place ^ k) * shard, shard), shard)
            for a in range((full - width) // shard):
                piece = source.at[:, pl.ds(width + a * shard, shard)]
                moves.append((piece, target.at[pl.ds(top + a * shard, shard), spot]))
            copies += [pltpu.make_async_copy(*move, sem.at[plane, k, n]) for n, move in enumerate(moves)]
    return copies


def retain_kernel(first, wide, n, n_kept, woven, *refs):
    pieces, refs = refs[: 2 * n], refs[2 * n :]
    if woven:
        place_ref, own, others, decays = refs[:4]
        refs = refs[4:]
    else:
        weights, decays = refs[:2]
        refs = refs[2 + n_kept :]
    query_ref, key_ref, value_ref, gate_ref, scores_ref, retained_ref, gated_ref, rows_ref = refs[:8]
    near_ref, *far_refs = refs[8 : 9 + n]
    if woven:
        joined_ref, held, sem, out_sem, weights, weights_sem, joined_sem = refs[9 + n :]
    else:
        held, sem, out_sem = refs[9 + n :]
    step = pl.program_id(0)
    dk, dv = query_ref.shape[1], value_ref.shape[1]
    if woven:
        copies = weave(place_ref[0], own, others, weights, 2 * dk + 2 * dv, weights_sem)
        keep_weights = pltpu.make_async_copy(weights, joined_ref, joined_sem)

        @pl.when(step == 0)
        def bring():
            for one in copies:
                one.start()

    rows = load_pieces(pieces, held, sem)
    slot_len = rows.shape[0]
    keep = pltpu.make_async_copy(
        held.at[step], rows_ref.at[pl.ds((step + first) * slot_len, slot_len)], out_sem
    )
    keep.start()
    if woven:

        @pl.when(step == 0)
        def brought():
            for one in copies:
                one.wait()
            keep_weights.start()

    query_key = dot(rows, weights[:, : 2 * dk]).astype(bf16)
    query, key = query_key[:, :dk], query_key[:, dk:]
    query_ref[...] = query
    key_ref[...] = key
    scores = (dot_nt(query, key) * decays[...]).astype(bf16)
    scores_ref[...] = scores[None]
    value = dot(rows, weights[:, 2 * dk : 2 * dk + dv]).astype(bf16)
    value_ref[...] = value
    retained = dot(scores, value)
    retained_ref[...] = retained
    scale = lax.rsqrt(jnp.mean(retained * retained, axis=-1, keepdims=True) + group_floor)
    gate = dot(rows, weights[:, 2 * dk + dv : 2 * dk + 2 * dv])
    gate_ref[...] = gate
    gated_ref[...] = (gate * jax.nn.sigmoid(gate) * (retained * scale)).astype(bf16)
    for columns, terms in times_rows(gated_ref[...], weights[:, 2 * dk + 2 * dv :], wide):
        split_out(terms, near_ref, far_refs, columns)
    keep.wait()
    if woven:

        @pl.when(step == n - 1)
        def kept():
            keep_weights.wait()


def retain(first, pieces, weights, decays, kept, dk, dv, wide, place=None):
    n = len(pieces) // 2
    rows, width = pieces[0].shape
    slot_len = 2 * rows
    total = PLANE * slot_len

    def at(cols):
        return pl.BlockSpec((slot_len, cols), lambda i: (i + first, 0))

    kept_specs = [at(dk), at(dk), at(dv), at(dv), None, at(dv), at(dv), ANY]
    kept_specs[4] = pl.BlockSpec((1, slot_len, slot_len), lambda i: (i + first, 0, 0))
    out_specs = kept_specs + split_specs(n, rows, width)
    out_shape = [
        shaped((total, dk), bf16),
        shaped((total, dk), bf16),
        shaped((total, dv), bf16),
        shaped((total, dv), f32),
        shaped((PLANE, slot_len, slot_len), bf16),
        shaped((total, dv), f32),
        shaped((total, dv), bf16),
        shaped((total, width), bf16),
        *split_shapes(n, rows, width),
    ]
    scratch_shapes = [
        pltpu.VMEM((n, slot_len, width), bf16),
        pltpu.SemaphoreType.DMA((2 * n,)),
        pltpu.SemaphoreType.DMA,
    ]
    if place is None:
        given = [weights, decays]
        in_specs = [whole(weights.shape), whole((slot_len, slot_len))]
    else:
        assert not kept
        given = [place, *weights, decays]
        in_specs = [pl.BlockSpec(memory_space=pltpu.SMEM), ANY, ANY, whole((slot_len, slot_len))]
        full = weights[0].shape[1]
        shard = weights[0].shape[0] // 4
        out_specs.append(ANY)
        out_shape.append(shaped((width, full), bf16))
        scratch_shapes += [
            pltpu.VMEM((width, full), bf16),
            pltpu.SemaphoreType.DMA((4, PLANE, 1 + (full - 2 * dk - 2 * dv) // shard)),
            pltpu.SemaphoreType.DMA,
        ]
    return pl.pallas_call(
        functools.partial(retain_kernel, first, wide, n, len(kept), place is not None),
        grid=(n,),
        in_specs=[ANY] * (2 * n) + in_specs + [ANY] * len(kept),
        out_specs=out_specs,
        out_shape=out_shape,
        scratch_shapes=scratch_shapes,
        input_output_aliases={2 * n + len(given) + i: i for i in range(len(kept))},
        compiler_params=params(),
        cost_estimate=cost(2.2 * n * slot_len * width * (2 * dk + 3 * dv), 15e6),
    )(*pieces, *given, *kept)


def project_kernel(wide, left, right, near_ref, *far_refs):
    for columns, terms in times_rows(left[...], right[...], wide):
        split_out(terms, near_ref, far_refs, columns)


def project(left, right, block, wide):
    total, inner = left.shape
    width = right.shape[0]
    slot_len = total // PLANE
    rows = slot_len // 2
    return pl.pallas_call(
        functools.partial(project_kernel, wide),
        grid=(PLANE,),
        in_specs=[
            by_slot(slot_len, inner),
            pl.BlockSpec((width, inner), lambda i: (0, block), pipeline_mode=pl.Buffered(1)),
        ],
        out_specs=split_specs(PLANE, rows, width),
        out_shape=split_shapes(PLANE, rows, width),
        compiler_params=params(),
        cost_estimate=cost(2 * total * inner * width, 20e6),
    )(left, right)


def back_kernel(left, first, second, near_ref, *far_refs):
    dv = second.shape[1]
    narrow = first.shape[1] - dv
    terms = dot_nt(left[:, :dv], first[:, narrow:]) + dot_nt(left[:, dv : 2 * dv], second[...])
    terms += dot_nt(left[:, 2 * dv :], first[:, :narrow])
    split_out(terms, near_ref, far_refs, slice(None))


def project_back(left, joined, dk, dv):
    total, inner = left.shape
    width = joined.shape[0]
    slot_len = total // PLANE
    rows = slot_len // 2
    return pl.pallas_call(
        back_kernel,
        grid=(PLANE,),
        in_specs=[
            by_slot(slot_len, inner),
            whole((width, 2 * dk + dv)),
            pl.BlockSpec((width, dv), lambda i: (0, 2), pipeline_mode=pl.Buffered(1)),
        ],
        out_specs=split_specs(PLANE, rows, width),
        out_shape=split_shapes(PLANE, rows, width),
        compiler_params=params(),
        cost_estimate=cost(2 * total * inner * width, 20e6),
    )(left, joined, joined)


def fold_kernel(*refs):
    nears, arriveds = refs[:3], refs[3:6]
    x1_ref, y2_ref, x3_ref, y3_ref, keep_x_ref, keep_y_ref = refs[6:]
    half = x1_ref.shape[0]
    targets = ((x1_ref, keep_x_ref), (keep_y_ref, y2_ref), (x3_ref, y3_ref))
    for near, arrived, (first, second) in zip(nears, arriveds, targets):
        first[...] = (near[0, :half] + arrived[:half].astype(f32)).astype(first.dtype)
        second[...] = (near[0, half:] + arrived[half:].astype(f32)).astype(second.dtype)


def fold_cut(slots):
    nears, arriveds, spots = zip(*slots)
    _, rows, width = nears[0].shape
    half = rows // 2
    part = width // 4
    kinds = (bf16, bf16, bf16, bf16, f32, f32)
    given = [pl.BlockSpec((1, rows, part), lambda i, spot=spot: (spot, 0, i)) for spot in spots]
    given += [pl.BlockSpec((rows, part), lambda i: (0, i))] * len(spots)
    return pl.pallas_call(
        fold_kernel,
        grid=(width // part,),
        in_specs=given,
        out_specs=[pl.BlockSpec((half, part), lambda i: (0, i))] * len(kinds),
        out_shape=[shaped((half, width), kind) for kind in kinds],
        compiler_params=params(),
        cost_estimate=cost(1e6, 12e6),
    )(*nears, *arriveds)


def hidden_kernel(first, wide, n, n_kept, *refs):
    pieces, (joined, back) = refs[: 2 * n], refs[2 * n : 2 * n + 2]
    act_ref, grad_ref, rows_ref, near_ref, *far_refs = refs[2 * n + 2 + n_kept : 3 * n + 6 + n_kept]
    held, sem, out_sem = refs[3 * n + 6 + n_kept :]
    rows = load_pieces(pieces, held, sem)
    step = pl.program_id(0)
    slot_len = rows.shape[0]
    inner = act_ref.shape[1]
    keep = pltpu.make_async_copy(
        held.at[step], rows_ref.at[pl.ds((step + first) * slot_len, slot_len)], out_sem
    )
    keep.start()
    weights, down_weights = joined[:, : 2 * inner], joined[:, 2 * inner :]
    up = dot(rows, weights[:, :inner])
    value = dot(rows, weights[:, inner:])
    slope = jnp.tanh(tanh_scale * (up + tanh_cubic * (up * up * up)))
    gelu = 0.5 * up * (1.0 + slope)
    act_ref[...] = (gelu * value).astype(bf16)
    rise = 0.5 * (1.0 + slope) + 0.5 * up * (1.0 - slope * slope) * (
        tanh_scale * (1.0 + 3.0 * tanh_cubic * (up * up))
    )
    grad = times_rows_back(back[...], down_weights, wide)
    grad_ref[:, :inner] = (grad * value * rise).astype(bf16)
    grad_ref[:, inner:] = (grad * gelu).astype(bf16)
    split_out(dot_nt(grad_ref[...], weights), near_ref, far_refs, slice(None))
    keep.wait()


def hidden_units(first, pieces, joined, back, kept, inner, wide):
    n = len(pieces) // 2
    rows, width = pieces[0].shape
    slot_len = 2 * rows
    total = back.shape[0]

    def at(cols):
        return pl.BlockSpec((slot_len, cols), lambda i: (i + first, 0))

    return pl.pallas_call(
        functools.partial(hidden_kernel, first, wide, n, len(kept)),
        grid=(n,),
        in_specs=[ANY] * (2 * n)
        + [
            pl.BlockSpec(memory_space=pltpu.VMEM),
            at(width),
        ]
        + [ANY] * len(kept),
        out_specs=[at(inner), at(2 * inner), ANY, *split_specs(n, rows, width)],
        out_shape=[
            pltpu.HBM((total, inner), bf16),
            pltpu.HBM((total, 2 * inner), bf16),
            pltpu.HBM((total, width), bf16),
            *split_shapes(n, rows, width, pltpu.HBM),
        ],
        scratch_shapes=[
            pltpu.VMEM((n, slot_len, width), bf16),
            pltpu.SemaphoreType.DMA((2 * n,)),
            pltpu.SemaphoreType.DMA,
        ],
        input_output_aliases={2 * n + 2 + i: i for i in range(len(kept))},
        compiler_params=params(44),
        cost_estimate=cost(10 * n * slot_len * width * inner, 15e6),
    )(*pieces, joined, back, *kept)


def retain_back_kernel(first, wide, n, n_kept, *refs):
    pieces = refs[: 2 * n]
    out_weights, decays, query, key, value, gate_ref, scores, retained_ref = refs[2 * n : 2 * n + 8]
    grad_ref, rows_ref = refs[2 * n + 8 + n_kept : 2 * n + 10 + n_kept]
    held, sem, out_sem = refs[2 * n + 10 + n_kept :]
    rows = load_pieces(pieces, held, sem)
    step = pl.program_id(0)
    slot_len = rows.shape[0]
    keep = pltpu.make_async_copy(
        held.at[step], rows_ref.at[pl.ds((step + first) * slot_len, slot_len)], out_sem
    )
    keep.start()
    dk, dv = query.shape[1], value.shape[1]
    grad = times_rows_back(rows, out_weights[...], wide)
    retained, gate = retained_ref[...], gate_ref[...]
    scale = lax.rsqrt(jnp.mean(retained * retained, axis=-1, keepdims=True) + group_floor)
    sigma = jax.nn.sigmoid(gate)
    normed = retained * scale
    grad_ref[:, dv : 2 * dv] = (grad * normed * (sigma * (1.0 + gate * (1.0 - sigma)))).astype(bf16)
    grad = grad * (gate * sigma)
    mean = jnp.mean(normed * grad, axis=-1, keepdims=True)
    grad_retained = (scale * (grad - normed * mean)).astype(bf16)
    grad_scores = (dot_nt(grad_retained, value[...]) * decays[...]).astype(bf16)
    grad_ref[:, :dv] = dot_tn(scores[0], grad_retained).astype(bf16)
    grad_ref[:, 2 * dv : 2 * dv + dk] = dot(grad_scores, key[...]).astype(bf16)
    grad_ref[:, 2 * dv + dk :] = dot_tn(grad_scores, query[...]).astype(bf16)
    keep.wait()


def retain_back(first, pieces, joined, decays, query, key, value, gate, scores, retained, kept, wide):
    n = len(pieces) // 2
    rows, width = pieces[0].shape
    slot_len = 2 * rows
    total, dk = query.shape
    dv = value.shape[1]

    def at(cols):
        return pl.BlockSpec((slot_len, cols), lambda i: (i + first, 0))

    return pl.pallas_call(
        functools.partial(retain_back_kernel, first, wide, n, len(kept)),
        grid=(n,),
        in_specs=[ANY] * (2 * n)
        + [
            pl.BlockSpec((width, dv), lambda i: (0, 3), pipeline_mode=pl.Buffered(1)),
            whole((slot_len, slot_len)),
            at(dk),
            at(dk),
            at(dv),
            at(dv),
            pl.BlockSpec((1, slot_len, slot_len), lambda i: (i + first, 0, 0)),
            at(dv),
        ]
        + [ANY] * len(kept),
        out_specs=[at(2 * dk + 2 * dv), ANY],
        out_shape=[shaped((total, 2 * dk + 2 * dv), bf16), shaped((total, width), bf16)],
        scratch_shapes=[
            pltpu.VMEM((n, slot_len, width), bf16),
            pltpu.SemaphoreType.DMA((2 * n,)),
            pltpu.SemaphoreType.DMA,
        ],
        input_output_aliases={2 * n + 8 + i: i for i in range(len(kept))},
        compiler_params=params(),
        cost_estimate=cost(4 * n * slot_len * width * dv, 15e6),
    )(*pieces, joined, decays, query, key, value, gate, scores, retained, *kept)


def grad_kernel(left, right, grad_ref):
    grad_ref[...] = dot_tn(left[...], right[...]).astype(bf16)


def columns_grad(left, right, block, cols):
    total, width = left.shape
    part = width // 4
    return pl.pallas_call(
        grad_kernel,
        grid=(width // part,),
        in_specs=[
            pl.BlockSpec((total, part), lambda i: (0, i)),
            pl.BlockSpec((total, cols), lambda i: (0, block), pipeline_mode=pl.Buffered(1)),
        ],
        out_specs=by_slot(part, cols),
        out_shape=shaped((width, cols), bf16),
        compiler_params=params(),
        cost_estimate=cost(2 * total * width * cols, 20e6),
    )(left, right)


def places_grad_kernel(me_ref, left, right, own, others, held, sem):
    step = pl.program_id(0)
    slot = step % 2
    held[slot] = dot_tn(left[...], right[...]).astype(bf16)
    shard = held.shape[1] // PLANE

    def each(step, slot, act):
        def copy(j, target):
            return pltpu.make_async_copy(held.at[slot, pl.ds(j * shard, shard)], target, sem.at[slot, j])

        for j in range(PLANE):
            k = me_ref[0] ^ j

            @pl.when(k == 0)
            def here(j=j):
                act(copy(j, own.at[pl.ds(pl.multiple_of(step * shard, shard), shard)]))

            @pl.when(k != 0)
            def there(j=j, k=k):
                at = pl.multiple_of((step * (PLANE - 1) + k - 1) * shard, shard)
                act(copy(j, others.at[pl.ds(at, shard)]))

    each(step, slot, lambda one: one.start())

    @pl.when(step > 0)
    def before():
        each(step - 1, 1 - slot, lambda one: one.wait())

    @pl.when(step == pl.num_programs(0) - 1)
    def last():
        each(step, slot, lambda one: one.wait())


def places_grad(me, left, right, depth):
    total, width = left.shape
    cols = right.shape[1]
    part = width // depth
    return pl.pallas_call(
        places_grad_kernel,
        grid=(depth,),
        in_specs=[
            pl.BlockSpec(memory_space=pltpu.SMEM),
            pl.BlockSpec((total, part), lambda i: (0, i)),
            whole((total, cols)),
        ],
        out_specs=[ANY, ANY],
        out_shape=[
            shaped((width // PLANE, cols), bf16),
            shaped((width // PLANE * (PLANE - 1), cols), bf16),
        ],
        scratch_shapes=[pltpu.VMEM((2, part, cols), bf16), pltpu.SemaphoreType.DMA((2, PLANE))],
        compiler_params=params(),
        cost_estimate=cost(2 * total * width * cols, 20e6),
    )(me, left, right)


def rows_grad(left, right, wide):
    total, inner = left.shape
    blocks = right.shape[1] // wide
    return pl.pallas_call(
        grad_kernel,
        grid=(blocks,),
        in_specs=[whole((total, inner)), pl.BlockSpec((total, wide), lambda i: (0, i))],
        out_specs=by_slot(inner, wide),
        out_shape=shaped((blocks * inner, wide), bf16),
        compiler_params=params(),
        cost_estimate=cost(2 * total * inner * wide * blocks, 20e6),
    )(left, right)


def place_grads_kernel(n, me_ref, *refs):
    ins, outs, held, sem = refs[:PLANE], refs[PLANE : PLANE + n], refs[-2], refs[-1]
    place = me_ref[0]
    copies = []
    for k in range(PLANE):
        held[k] = ins[k][...].astype(f32)
        at = 0
        for i, out in enumerate(outs):
            part = out.shape[1] // PLANE
            one = pltpu.make_async_copy(
                held.at[k, :, pl.ds(at, part)], out.at[:, lanes(place ^ k, part)], sem.at[k * n + i]
            )
            one.start()
            copies.append(one)
            at += part
    for one in copies:
        one.wait()


def place_columns(me, blocks, widths):
    rows = blocks[0].shape[0]
    n = len(widths)
    return pl.pallas_call(
        functools.partial(place_grads_kernel, n),
        in_specs=[pl.BlockSpec(memory_space=pltpu.SMEM)]
        + [pl.BlockSpec(memory_space=pltpu.VMEM)] * PLANE,
        out_specs=[ANY] * n,
        out_shape=[shaped((rows, PLANE * w), f32) for w in widths],
        scratch_shapes=[
            pltpu.VMEM((PLANE, *blocks[0].shape), f32),
            pltpu.SemaphoreType.DMA((PLANE * n,)),
        ],
        compiler_params=params(),
        cost_estimate=cost(0, 8e6),
    )(me, *blocks)


def place_rows_kernel(me_ref, *refs):
    ins, out, held, sem = refs[:PLANE], refs[PLANE], refs[-2], refs[-1]
    rows = ins[0].shape[0]
    copies = []
    for k in range(PLANE):
        held[k] = ins[k][...].astype(f32)
        one = pltpu.make_async_copy(held.at[k], out.at[lanes(me_ref[0] ^ k, rows), :], sem.at[k])
        one.start()
        copies.append(one)
    for one in copies:
        one.wait()


def place_rows(me, blocks):
    rows, cols = blocks[0].shape
    return pl.pallas_call(
        place_rows_kernel,
        in_specs=[pl.BlockSpec(memory_space=pltpu.SMEM)]
        + [pl.BlockSpec(memory_space=pltpu.VMEM)] * PLANE,
        out_specs=ANY,
        out_shape=shaped((PLANE * rows, cols), f32),
        scratch_shapes=[pltpu.VMEM((PLANE, rows, cols), f32), pltpu.SemaphoreType.DMA((PLANE,))],
        compiler_params=params(),
        cost_estimate=cost(0, 4e6),
    )(me, *blocks)


def cut_sums(me, columns, rows):
    width = columns.shape[1]
    shard = columns.shape[0] // PLANE
    blocks = [r.shape[0] // shard for r in rows]

    def plan(place, ins, outs):
        copies = []
        for k in range(PLANE):
            copies.append((ins[0].at[lanes(place ^ k, shard), :], outs[k].at[:, pl.ds(0, width)]))
            at = width
            for r, count in zip(ins[1:], blocks):
                for a in range(count):
                    source = r.at[pl.ds(a * shard, shard), lanes(place ^ k, shard)]
                    copies.append((source, outs[k].at[:, pl.ds(at, shard)]))
                    at += shard
        return copies

    shapes = [shaped((shard, width + shard * sum(blocks)), bf16)] * PLANE
    return place_copies(plan, PLANE * (1 + sum(blocks)), me, [columns, *rows], shapes)


def place_sums_kernel(parts, blocks, me_ref, *refs):
    ins, outs, held, sem = refs[:PLANE], refs[PLANE:-2], refs[-2], refs[-1]
    place = me_ref[0]
    shard = ins[0].shape[0]
    copies = []
    for k in range(PLANE):
        held[k] = ins[k][...].astype(f32)
        at = 0
        moves = []
        for out, part in zip(outs, parts):
            moves.append((held.at[k, :, pl.ds(at, part)], out.at[:, lanes(place ^ k, part)]))
            at += part
        for out, count in zip(outs[len(parts) :], blocks):
            for a in range(count):
                spot = pl.multiple_of((place ^ k) * count * shard + a * shard, shard)
                moves.append((held.at[k, :, pl.ds(at, shard)], out.at[pl.ds(spot, shard), :]))
                at += shard
        for n, move in enumerate(moves):
            copies.append(pltpu.make_async_copy(*move, sem.at[k, n]))
            copies[-1].start()
    for one in copies:
        one.wait()


def place_sums(me, pieces, parts, inners):
    shard, full = pieces[0].shape
    blocks = [inner // shard for inner in inners]
    return pl.pallas_call(
        functools.partial(place_sums_kernel, parts, blocks),
        in_specs=[pl.BlockSpec(memory_space=pltpu.SMEM)] + [pl.BlockSpec(memory_space=pltpu.VMEM)] * PLANE,
        out_specs=[ANY] * (len(parts) + len(blocks)),
        out_shape=[shaped((shard, PLANE * part), f32) for part in parts]
        + [shaped((PLANE * inner, shard), f32) for inner in inners],
        scratch_shapes=[
            pltpu.VMEM((PLANE, shard, full), f32),
            pltpu.SemaphoreType.DMA((PLANE, len(parts) + sum(blocks))),
        ],
        compiler_params=params(),
        cost_estimate=cost(0, 8e6),
    )(me, *pieces)


def hop(value, bits, count):
    return lax.ppermute(value, "dp", [(i, i ^ bits) for i in range(count)])


def swap(value):
    return lax.ppermute(value, "tensor", [(0, 1), (1, 0)])


def trade(blocks, count):
    return [blocks[0]] + [hop(blocks[k], k, count) for k in range(1, PLANE)]


def spread(mine, count, beside=None):
    half = mine.shape[0] // 2
    from_x = hop(mine, 1, count)
    from_y = hop(mine, 2, count)
    pieces = [mine, swap(mine)]
    if beside:
        from_x, from_y = after((from_x, from_y), beside(0, 1, pieces))
    far_a = hop(from_x[:half], 2, count)
    far_b = hop(from_y[half:], 1, count)
    nearer = [from_x, swap(from_x), from_y, swap(from_y)]
    if beside:
        far_a, far_b = after((far_a, far_b), beside(1, 3, nearer))
    far = jnp.concatenate([far_a, far_b])
    far = [far, swap(far)]
    if beside:
        return beside(3, 4, far)
    return pieces + nearer + far


def fold(groups, count, before=None, first=None, second=None):
    slots = {}

    def take(lo, near, *fars):
        for k, far in enumerate(fars):
            slots[lo + k] = near, swap(far), k

    for group in groups:
        take(*group)
    given = [(near, arrived) for near, arrived, _ in (slots[k] for k in (1, 2, 3))]
    made = []
    if before:
        made.append(before(slots[1][1]))
        given = after(given, made)
    cut = fold_cut([(*pair, slots[k][2]) for k, pair in zip((1, 2, 3), given)])
    to_x1, to_y2, to_x3, to_y3, keep_x, keep_y = cut
    half, width = to_x1.shape
    x1, y2 = hop(to_x1, 1, count), hop(to_y2, 2, count)
    x3, y3 = hop(to_x3, 1, count), hop(to_y3, 2, count)
    if first:
        made.append(first((to_x3, to_y3)))
        x3, y3 = after((x3, y3), made)
    if 0 not in slots:
        take(*made[-1][0])
    near_0, arrived_0, spot = slots[0]
    to_y, to_x = (keep_y + x3.astype(f32)).astype(bf16), (keep_x + y3.astype(f32)).astype(bf16)
    last_y, last_x = hop(to_y, 2, count), hop(to_x, 1, count)
    if second:
        made.append(second((to_x, to_y)))
        last_y, last_x = after((last_y, last_x), made[-1])
    near_0, arrived_0 = near_0[spot], arrived_0.astype(f32)
    summed = [
        near_0[:half] + arrived_0[:half] + (x1.astype(f32) + last_y.astype(f32)),
        near_0[half:] + arrived_0[half:] + (y2.astype(f32) + last_x.astype(f32)),
    ]
    return jnp.concatenate(summed), *made


def after(values, done):
    return lax.optimization_barrier((values, done))[0]


def on_device(
    tokens,
    lengths,
    w_query,
    w_key,
    w_value,
    w_gate,
    w_out,
    w_ffgate,
    w_ffup,
    w_ffdown,
    gain_attn,
    gain_mlp,
    cotangent,
):
    count = lax.axis_size("dp")
    depth = count // PLANE
    columns = [[q + PLANE * z for z in range(depth)] for q in range(PLANE)]
    place = lax.axis_index("dp")
    me = place % PLANE
    me_scalar = me.reshape(1).astype(jnp.int32)
    core = lax.axis_index("tensor")
    rows, width = tokens.shape
    wide = width // depth
    shard = w_query.shape[0]
    dk = w_query.shape[1] // PLANE
    dv = w_value.shape[1] // PLANE
    inner = w_ffgate.shape[1] // PLANE
    assert dk == DK and dv == DV

    def gather_depth(block):
        return lax.all_gather(block, "dp", axis=0, tiled=True, axis_index_groups=columns)

    def sum_depth(block):
        return lax.psum_scatter(block, "dp", scatter_dimension=0, tiled=True, axis_index_groups=columns)

    attn_cuts = cut_weights(me_scalar, (w_query, w_key, w_value, w_gate), w_out)
    attn_blocks = trade(attn_cuts, count)
    attn_width = 2 * dk + 2 * dv
    if depth == 4:
        own_gathered = gather_depth(attn_cuts[0])
        attn_own = jnp.concatenate(attn_blocks[1:])
        attn_weights = own_gathered, gather_depth(attn_own)
    else:
        attn_own = join_weights(me_scalar, attn_blocks, attn_width)
        attn_joined = gather_depth(attn_own)

    gains = jnp.stack([gain_attn, gain_mlp])[None]
    step = 1
    while step < count:
        gains = jnp.concatenate([gains, hop(gains, step, count)])
        step *= 2
    gains = jnp.take(gains, place ^ jnp.arange(count), axis=0).astype(f32)
    gain_first = gains[:, 0].reshape(1, width)
    gain_second = gains[:, 1].reshape(1, width)

    input_rows = tokens.astype(f32)
    first_scale = lax.rsqrt(jnp.mean(input_rows * input_rows, axis=-1, keepdims=True) + norm_eps)
    normed_attn = (input_rows * first_scale * gain_first).astype(bf16)
    attn_pieces = spread(after(normed_attn, attn_own), count)

    ff_cuts = after(cut_weights(me_scalar, (w_ffgate, w_ffup), w_ffdown), attn_pieces)
    ff_own = join_weights(me_scalar, trade(ff_cuts, count), 2 * inner)
    ff_joined = gather_depth(ff_own)

    local = jnp.arange(rows, dtype=jnp.int32)
    valid_rows = ((core * rows + local) < lengths[0]).astype(f32)[:, None]
    back_rows = valid_rows * cotangent.astype(f32)
    back_pieces = spread(after(back_rows.astype(bf16), ff_own), count)
    back_all = jnp.concatenate(back_pieces)

    positions = jnp.concatenate([core * rows + local, (1 - core) * rows + local])
    decays = decay_table(positions, core * PLANE + me)
    attn_pieces = after(attn_pieces, back_all)
    kept, groups = [], []
    if depth == 4:
        *kept, attn_joined = retain(1, attn_pieces[2:], attn_weights, decays, kept, dk, dv, wide, me_scalar)
    else:
        kept = retain(1, attn_pieces[2:], attn_joined, decays, kept, dk, dv, wide)
    kept, terms = kept[:8], kept[8:]
    groups.append((1, *terms))

    def retain_own(done):
        pieces = after(attn_pieces[:2], done)
        made = retain(0, pieces, attn_joined, decays, kept, dk, dv, wide)
        return (0, *made[8:]), made[:8]

    added, (_, made) = fold(groups, count, first=retain_own)
    query, key, value, gate, scores, retained, gated, attn_all = made
    hidden = input_rows + added

    second_scale = lax.rsqrt(jnp.mean(hidden * hidden, axis=-1, keepdims=True) + norm_eps)
    normed_mlp = (hidden * second_scale * gain_second).astype(bf16)

    state = {"kept": (), "groups": []}

    def units(lo, hi, pieces):
        if lo == 0:
            state["own"] = pieces
            return ()
        if lo == 1:
            lo, pieces = 0, state["own"] + pieces
        made = hidden_units(lo, pieces, ff_joined, back_all, state["kept"], inner, wide)
        state["kept"] = made[:3]
        state["groups"].append((lo, *made[3:]))
        return state["kept"]

    inner_act, grad_up, mlp_all = spread(normed_mlp, count, units)

    def down_grad(_):
        return rows_grad(inner_act, back_all, wide)

    def up_grad(done):
        return columns_grad(*after((mlp_all, grad_up), done), 0, 2 * inner)

    grad_normed, grad_down, grad_ff = fold(state["groups"], count, down_grad, up_grad)
    down_part = sum_depth(grad_down)
    ff_part = sum_depth(grad_ff)
    scaled = grad_normed * gain_second
    grad_hidden = back_rows + second_scale * (
        scaled
        - hidden * (second_scale * second_scale) * jnp.mean(hidden * scaled, axis=-1, keepdims=True)
    )
    gain_term_mlp = jnp.sum(grad_normed * hidden * second_scale, axis=0)

    state = {"kept": ()}

    def heads(lo, hi, pieces):
        if lo == 3:
            pieces = after(pieces, down_part)
        state["kept"] = retain_back(
            lo, pieces, attn_joined, decays, query, key, value, gate, scores, retained, state["kept"], wide
        )
        if lo > 0:
            return state["kept"]
        act = after(inner_act, pieces)
        state["mlp"] = project(act, ff_joined, 2, wide)
        return state["kept"], state["mlp"]

    grad_wide, attn_grad_all = spread(grad_hidden.astype(bf16), count, heads)
    grad_out = rows_grad(gated, attn_grad_all, wide)
    out_part = sum_depth(grad_out)

    own_grad, others_grad = places_grad(me_scalar, attn_all, after(grad_wide, grad_out), depth)

    def back_terms(done):
        return project_back(after(grad_wide, (done, ff_part)), attn_joined, dk, dv)

    mlp_added, _, attn_terms = fold([(0, *state["mlp"])], count, lambda _: others_grad, back_terms)
    others_part = sum_depth(others_grad)
    output = (valid_rows * (hidden + mlp_added)).astype(bf16)
    if shard % 128 == 0:
        sums = trade(cut_sums(me_scalar, ff_part, (down_part, out_part)), count)
    else:
        sums = out_part
    grad_normed_attn, *_ = fold([(0, *attn_terms)], count, lambda _: mlp_added, lambda _: sums)
    own_grad = after(own_grad, grad_normed_attn)
    own_part = sum_depth(own_grad)
    gain_term_attn = jnp.sum(grad_normed_attn * input_rows * first_scale, axis=0)
    scaled_first = grad_normed_attn * gain_first
    tokens_grad = grad_hidden + first_scale * (
        scaled_first
        - input_rows
        * (first_scale * first_scale)
        * jnp.mean(input_rows * scaled_first, axis=-1, keepdims=True)
    )
    tokens_grad = tokens_grad.astype(bf16)

    def back_columns(block, widths):
        cuts = [lax.dynamic_slice_in_dim(block, (me ^ k) * shard, shard, 0).astype(bf16) for k in range(PLANE)]
        return place_columns(me_scalar, trade(cuts, count), widths)

    def back_rows_of(block):
        cuts = [lax.dynamic_slice_in_dim(block, (me ^ k) * shard, shard, 1).astype(bf16) for k in range(PLANE)]
        return place_rows(me_scalar, trade(cuts, count))

    if shard % 128 == 0:
        ffgate_sum, ffup_sum, down_sum, out_sum = place_sums(me_scalar, sums, (inner, inner), (inner, dv))
    else:
        down_sum, out_sum = back_rows_of(down_part), back_rows_of(out_part)
        ffgate_sum, ffup_sum = back_columns(ff_part, (inner, inner))
    others_part = after(others_part, (tokens_grad, output))
    blocks = [hop(others_part[k * shard : (k + 1) * shard], k + 1, count) for k in range(PLANE - 1)]
    gain_terms = jnp.stack([gain_term_attn, gain_term_mlp])
    bit = count // 2
    while bit >= 1:
        side = (place // bit) % 2
        cut = gain_terms.reshape(2, 2, -1)
        kept = lax.dynamic_index_in_dim(cut, side, 1, keepdims=False)
        sent = lax.dynamic_index_in_dim(cut, 1 - side, 1, keepdims=False)
        gain_terms = kept + hop(sent, bit, count)
        bit //= 2
    cut = after(gain_terms, blocks).reshape(2, 2, -1)
    kept = lax.dynamic_index_in_dim(cut, core, 1, keepdims=False)
    sent = lax.dynamic_index_in_dim(cut, 1 - core, 1, keepdims=False)
    gain_terms = kept + swap(sent)
    early = output, tokens_grad, gain_terms, down_sum, ffgate_sum, ffup_sum, out_sum
    value_sum, gate_sum, query_sum, key_sum = place_columns(
        me_scalar, [after(own_part, (blocks, early)), *blocks], (dv, dv, dk, dk)
    )

    return (
        output,
        tokens_grad,
        query_sum,
        key_sum,
        value_sum,
        gate_sum,
        out_sum,
        ffgate_sum,
        ffup_sum,
        down_sum,
        gain_terms[0],
        gain_terms[1],
    )


def solution(mesh):
    return jax.shard_map(
        on_device,
        mesh=mesh,
        in_specs=(
            P(("dp", "tensor"), None),
            P("dp"),
            P("dp", "tensor"),
            P("dp", "tensor"),
            P("dp", "tensor"),
            P("dp", "tensor"),
            P("tensor", "dp"),
            P("dp", "tensor"),
            P("dp", "tensor"),
            P("tensor", "dp"),
            P("dp"),
            P("dp"),
            P(("dp", "tensor"), None),
        ),
        out_specs=(
            P(("dp", "tensor"), None),
            P(("dp", "tensor"), None),
            P("dp", "tensor"),
            P("dp", "tensor"),
            P("dp", "tensor"),
            P("dp", "tensor"),
            P("tensor", "dp"),
            P("dp", "tensor"),
            P("dp", "tensor"),
            P("tensor", "dp"),
            P(("dp", "tensor")),
            P(("dp", "tensor")),
        ),
        check_vma=False,
    )
```

```python
import functools

import jax
import jax.numpy as jnp
from jax import lax
from jax.experimental import pallas as pl
from jax.experimental.pallas import tpu as pltpu
from jax.sharding import PartitionSpec as P

DK = 256
DV = 512
PLANE = 4
SLOTS = ((0, 1), (1, 3), (3, 4))

norm_eps = 1e-06
group_floor = 1.0
tanh_scale = 0.7978845608028654
tanh_cubic = 0.044715

bf16 = jnp.bfloat16
f32 = jnp.float32


def shaped(shape, kind):
    return jax.ShapeDtypeStruct(shape, kind)


def cost(flops, bytes_accessed):
    return pl.CostEstimate(flops=int(flops), bytes_accessed=int(bytes_accessed), transcendentals=0)


def params(mib=62):
    return pltpu.CompilerParams(vmem_limit_bytes=mib * 1024 * 1024)


ANY = pl.BlockSpec(memory_space=pl.ANY)


def whole(shape):
    return pl.BlockSpec(shape, lambda i: (0,) * len(shape), pipeline_mode=pl.Buffered(1))


def by_slot(*shape):
    return pl.BlockSpec(shape, lambda i: (i,) + (0,) * (len(shape) - 1))


def dot(left, right):
    return jnp.dot(left, right, preferred_element_type=f32)


def dot_nt(left, right):
    return lax.dot_general(left, right, (((1,), (1,)), ((), ())), preferred_element_type=f32)


def dot_tn(left, right):
    return lax.dot_general(left, right, (((0,), (0,)), ((), ())), preferred_element_type=f32)


def decay_table(positions, head):
    spacing = positions[:, None] - positions[None, :]
    log_rate = jnp.log1p(-jnp.exp2(-5.0 - head.astype(f32)))
    kept_spacing = jnp.where(spacing >= 0, spacing, jnp.zeros_like(spacing)).astype(f32)
    powers = jnp.exp(kept_spacing * log_rate)
    return jnp.where(spacing >= 0, powers, jnp.zeros_like(powers))


def copy_kernel(plan, n_in, me_ref, *refs):
    ins, outs, sem = refs[:n_in], refs[n_in:-1], refs[-1]
    copies = [
        pltpu.make_async_copy(source, target, sem.at[i])
        for i, (source, target) in enumerate(plan(me_ref[0], ins, outs))
    ]
    for one in copies:
        one.start()
    for one in copies:
        one.wait()


def place_copies(plan, n_copies, me, ins, out_shapes):
    moved = 2 * sum(2 * s.size for s in out_shapes)
    return pl.pallas_call(
        functools.partial(copy_kernel, plan, len(ins)),
        in_specs=[pl.BlockSpec(memory_space=pltpu.SMEM)] + [pl.BlockSpec(memory_space=pltpu.VMEM)] * len(ins),
        out_specs=[ANY] * len(out_shapes),
        out_shape=out_shapes,
        scratch_shapes=[pltpu.SemaphoreType.DMA((n_copies,))],
        compiler_params=params(),
        cost_estimate=cost(0, moved),
    )(me, *ins)


def lanes(index, size):
    return pl.ds(pl.multiple_of(index * size, size), size)


def cut_weights(me, by_columns, by_rows):
    rows, cols = by_columns[0].shape[0], by_rows.shape[1]
    parts = [w.shape[1] // PLANE for w in by_columns]
    inner = by_rows.shape[0] // PLANE
    width = sum(parts)
    aligned = cols % 128 == 0
    if not aligned:
        by_rows = jnp.moveaxis(by_rows.reshape(PLANE, inner // rows, rows, cols), 1, 2)
        by_rows = jnp.moveaxis(by_rows.reshape(PLANE, rows, -1), 0, 1).reshape(rows, -1)

    def plan(place, ins, outs):
        copies = []
        for k in range(PLANE):
            at = 0
            for w, part in zip(ins, parts):
                copies.append((w.at[:, lanes(place ^ k, part)], outs[k].at[:, pl.ds(at, part)]))
                at += part
            if not aligned:
                copies.append((ins[-1].at[:, lanes(place ^ k, inner)], outs[k].at[:, pl.ds(width, inner)]))
                continue
            for block in range(inner // rows):
                source = pl.ds(pl.multiple_of((place ^ k) * inner + block * rows, rows), rows)
                copies.append((ins[-1].at[source, :], outs[k].at[:, pl.ds(width + block * cols, cols)]))
        return copies

    shapes = [shaped((rows, width + inner), bf16)] * PLANE
    n_copies = PLANE * (len(parts) + (inner // rows if aligned else 1))
    return place_copies(plan, n_copies, me, [*by_columns, by_rows], shapes)


def join_weights(me, blocks, width):
    rows, inner = blocks[0].shape[0], blocks[0].shape[1] - width
    tall = PLANE * rows
    aligned = rows % 128 == 0
    extra = []
    if not aligned:
        parts = jnp.stack([lax.dynamic_index_in_dim(jnp.stack(blocks), me[0] ^ j, 0, keepdims=False) for j in range(PLANE)])
        parts = parts[:, :, width:].reshape(PLANE, rows, inner // tall, PLANE, rows)
        extra = [jnp.transpose(parts, (3, 1, 2, 0, 4)).reshape(tall, inner)]

    def plan(place, ins, outs):
        copies = []
        for k in range(PLANE):
            copies.append((ins[k].at[:, pl.ds(0, width)], outs[0].at[lanes(place ^ k, rows), pl.ds(0, width)]))
            for block in range(inner // rows if aligned else 0):
                spot = pl.ds(pl.multiple_of(width + (place ^ k) * rows, rows), rows)
                if block >= PLANE:
                    spot = pl.ds(pl.multiple_of(width + (block // PLANE) * tall + (place ^ k) * rows, rows), rows)
                source = ins[k].at[:, pl.ds(width + block * rows, rows)]
                copies.append((source, outs[0].at[pl.ds((block % PLANE) * rows, rows), spot]))
        if not aligned:
            copies.append((ins[PLANE], outs[0].at[:, pl.ds(width, inner)]))
        return copies

    n_copies = PLANE * (1 + inner // rows) if aligned else PLANE + 1
    return place_copies(plan, n_copies, me, [*blocks, *extra], [shaped((tall, width + inner), bf16)])[0]


def load_pieces(pieces, held, sem):
    step = pl.program_id(0)
    rows = pieces[0].shape[0]
    copies = [
        pltpu.make_async_copy(piece, held.at[i // 2, pl.ds((i % 2) * rows, rows)], sem.at[i])
        for i, piece in enumerate(pieces)
    ]

    @pl.when(step == 0)
    def start():
        for one in copies:
            one.start()

    for s in range(len(pieces) // 2):

        @pl.when(step == s)
        def arrive(s=s):
            copies[2 * s].wait()
            copies[2 * s + 1].wait()

    return held[step]


def times_rows(left, right, wide):
    groups = right.shape[1] // wide
    for z in range(right.shape[0] // wide):
        terms = dot(left[:, :wide], right[z * wide : (z + 1) * wide, :wide])
        for g in range(1, groups):
            terms += dot(
                left[:, g * wide : (g + 1) * wide],
                right[z * wide : (z + 1) * wide, g * wide : (g + 1) * wide],
            )
        yield slice(z * wide, (z + 1) * wide), terms


def times_rows_back(left, right, wide):
    made = []
    for g in range(right.shape[1] // wide):
        group = slice(g * wide, (g + 1) * wide)
        terms = dot_nt(left[:, :wide], right[:wide, group])
        for z in range(1, right.shape[0] // wide):
            block = slice(z * wide, (z + 1) * wide)
            terms += dot_nt(left[:, block], right[block, group])
        made.append(terms)
    return made[0] if len(made) == 1 else jnp.concatenate(made, axis=1)


def split_out(terms, near_ref, far_refs, columns):
    rows = near_ref.shape[1]
    near_ref[0, :, columns] = terms[:rows]
    far = terms[rows:].astype(bf16)
    for slot, far_ref in enumerate(far_refs):

        @pl.when(pl.program_id(0) == slot)
        def put(far_ref=far_ref):
            far_ref[:, columns] = far


def split_specs(n, rows, width):
    fars = [pl.BlockSpec((rows, width), lambda i: (0, 0), pipeline_mode=pl.Buffered(1))] * n
    return [by_slot(1, rows, width), *fars]


def split_shapes(n, rows, width, place=shaped):
    return [place((n, rows, width), f32)] + [place((rows, width), bf16)] * n


def weave(place, own, others, target, width, sem):
    planes, full = 4, own.shape[1]
    shard = own.shape[0] // planes
    copies = []
    for plane in range(planes):
        top = plane * PLANE * shard
        for k in range(PLANE):
            if k == 0:
                source = own.at[pl.ds(plane * shard, shard)]
            else:
                source = others.at[pl.ds((plane * (PLANE - 1) + k - 1) * shard, shard)]
            spot = pl.ds(pl.multiple_of(top + (place ^ k) * shard, shard), shard)
            moves = [(source.at[:, pl.ds(0, width)], target.at[spot, pl.ds(0, width)])]
            spot = pl.ds(pl.multiple_of(width + (place ^ k) * shard, shard), shard)
            for a in range((full - width) // shard):
                piece = source.at[:, pl.ds(width + a * shard, shard)]
                moves.append((piece, target.at[pl.ds(top + a * shard, shard), spot]))
            copies += [pltpu.make_async_copy(*move, sem.at[plane, k, n]) for n, move in enumerate(moves)]
    return copies


def retain_kernel(first, wide, n, n_kept, woven, *refs):
    pieces, refs = refs[: 2 * n], refs[2 * n :]
    if woven:
        place_ref, own, others, decays = refs[:4]
        refs = refs[4:]
    else:
        weights, decays = refs[:2]
        refs = refs[2 + n_kept :]
    query_ref, key_ref, value_ref, gate_ref, scores_ref, retained_ref, gated_ref, rows_ref = refs[:8]
    near_ref, *far_refs = refs[8 : 9 + n]
    if woven:
        joined_ref, held, sem, out_sem, weights, weights_sem, joined_sem = refs[9 + n :]
    else:
        held, sem, out_sem = refs[9 + n :]
    step = pl.program_id(0)
    dk, dv = query_ref.shape[1], value_ref.shape[1]
    if woven:
        copies = weave(place_ref[0], own, others, weights, 2 * dk + 2 * dv, weights_sem)
        keep_weights = pltpu.make_async_copy(weights, joined_ref, joined_sem)

        @pl.when(step == 0)
        def bring():
            for one in copies:
                one.start()

    rows = load_pieces(pieces, held, sem)
    slot_len = rows.shape[0]
    keep = pltpu.make_async_copy(
        held.at[step], rows_ref.at[pl.ds((step + first) * slot_len, slot_len)], out_sem
    )
    keep.start()
    if woven:

        @pl.when(step == 0)
        def brought():
            for one in copies:
                one.wait()
            keep_weights.start()

    query_key = dot(rows, weights[:, : 2 * dk]).astype(bf16)
    query, key = query_key[:, :dk], query_key[:, dk:]
    query_ref[...] = query
    key_ref[...] = key
    scores = (dot_nt(query, key) * decays[...]).astype(bf16)
    scores_ref[...] = scores[None]
    value = dot(rows, weights[:, 2 * dk : 2 * dk + dv]).astype(bf16)
    value_ref[...] = value
    retained = dot(scores, value)
    retained_ref[...] = retained
    scale = lax.rsqrt(jnp.mean(retained * retained, axis=-1, keepdims=True) + group_floor)
    gate = dot(rows, weights[:, 2 * dk + dv : 2 * dk + 2 * dv])
    gate_ref[...] = gate
    gated_ref[...] = (gate * jax.nn.sigmoid(gate) * (retained * scale)).astype(bf16)
    for columns, terms in times_rows(gated_ref[...], weights[:, 2 * dk + 2 * dv :], wide):
        split_out(terms, near_ref, far_refs, columns)
    keep.wait()
    if woven:

        @pl.when(step == n - 1)
        def kept():
            keep_weights.wait()


def retain(first, pieces, weights, decays, kept, dk, dv, wide, place=None):
    n = len(pieces) // 2
    rows, width = pieces[0].shape
    slot_len = 2 * rows
    total = PLANE * slot_len

    def at(cols):
        return pl.BlockSpec((slot_len, cols), lambda i: (i + first, 0))

    kept_specs = [at(dk), at(dk), at(dv), at(dv), None, at(dv), at(dv), ANY]
    kept_specs[4] = pl.BlockSpec((1, slot_len, slot_len), lambda i: (i + first, 0, 0))
    out_specs = kept_specs + split_specs(n, rows, width)
    out_shape = [
        shaped((total, dk), bf16),
        shaped((total, dk), bf16),
        shaped((total, dv), bf16),
        shaped((total, dv), f32),
        shaped((PLANE, slot_len, slot_len), bf16),
        shaped((total, dv), f32),
        shaped((total, dv), bf16),
        shaped((total, width), bf16),
        *split_shapes(n, rows, width),
    ]
    scratch_shapes = [
        pltpu.VMEM((n, slot_len, width), bf16),
        pltpu.SemaphoreType.DMA((2 * n,)),
        pltpu.SemaphoreType.DMA,
    ]
    if place is None:
        given = [weights, decays]
        in_specs = [whole(weights.shape), whole((slot_len, slot_len))]
    else:
        assert not kept
        given = [place, *weights, decays]
        in_specs = [pl.BlockSpec(memory_space=pltpu.SMEM), ANY, ANY, whole((slot_len, slot_len))]
        full = weights[0].shape[1]
        shard = weights[0].shape[0] // 4
        out_specs.append(ANY)
        out_shape.append(shaped((width, full), bf16))
        scratch_shapes += [
            pltpu.VMEM((width, full), bf16),
            pltpu.SemaphoreType.DMA((4, PLANE, 1 + (full - 2 * dk - 2 * dv) // shard)),
            pltpu.SemaphoreType.DMA,
        ]
    return pl.pallas_call(
        functools.partial(retain_kernel, first, wide, n, len(kept), place is not None),
        grid=(n,),
        in_specs=[ANY] * (2 * n) + in_specs + [ANY] * len(kept),
        out_specs=out_specs,
        out_shape=out_shape,
        scratch_shapes=scratch_shapes,
        input_output_aliases={2 * n + len(given) + i: i for i in range(len(kept))},
        compiler_params=params(),
        cost_estimate=cost(2.2 * n * slot_len * width * (2 * dk + 3 * dv), 15e6),
    )(*pieces, *given, *kept)


def project_kernel(wide, left, right, near_ref, *far_refs):
    for columns, terms in times_rows(left[...], right[...], wide):
        split_out(terms, near_ref, far_refs, columns)


def project(left, right, block, wide):
    total, inner = left.shape
    width = right.shape[0]
    slot_len = total // PLANE
    rows = slot_len // 2
    return pl.pallas_call(
        functools.partial(project_kernel, wide),
        grid=(PLANE,),
        in_specs=[
            by_slot(slot_len, inner),
            pl.BlockSpec((width, inner), lambda i: (0, block), pipeline_mode=pl.Buffered(1)),
        ],
        out_specs=split_specs(PLANE, rows, width),
        out_shape=split_shapes(PLANE, rows, width),
        compiler_params=params(),
        cost_estimate=cost(2 * total * inner * width, 20e6),
    )(left, right)


def back_kernel(left, first, second, near_ref, *far_refs):
    dv = second.shape[1]
    narrow = first.shape[1] - dv
    terms = dot_nt(left[:, :dv], first[:, narrow:]) + dot_nt(left[:, dv : 2 * dv], second[...])
    terms += dot_nt(left[:, 2 * dv :], first[:, :narrow])
    split_out(terms, near_ref, far_refs, slice(None))


def project_back(left, joined, dk, dv):
    total, inner = left.shape
    width = joined.shape[0]
    slot_len = total // PLANE
    rows = slot_len // 2
    return pl.pallas_call(
        back_kernel,
        grid=(PLANE,),
        in_specs=[
            by_slot(slot_len, inner),
            whole((width, 2 * dk + dv)),
            pl.BlockSpec((width, dv), lambda i: (0, 2), pipeline_mode=pl.Buffered(1)),
        ],
        out_specs=split_specs(PLANE, rows, width),
        out_shape=split_shapes(PLANE, rows, width),
        compiler_params=params(),
        cost_estimate=cost(2 * total * inner * width, 20e6),
    )(left, joined, joined)


def fold_kernel(*refs):
    nears, arriveds = refs[:3], refs[3:6]
    x1_ref, y2_ref, x3_ref, y3_ref, keep_x_ref, keep_y_ref = refs[6:]
    half = x1_ref.shape[0]
    targets = ((x1_ref, keep_x_ref), (keep_y_ref, y2_ref), (x3_ref, y3_ref))
    for near, arrived, (first, second) in zip(nears, arriveds, targets):
        first[...] = (near[0, :half] + arrived[:half].astype(f32)).astype(first.dtype)
        second[...] = (near[0, half:] + arrived[half:].astype(f32)).astype(second.dtype)


def fold_cut(slots):
    nears, arriveds, spots = zip(*slots)
    _, rows, width = nears[0].shape
    half = rows // 2
    part = width // 4
    kinds = (bf16, bf16, bf16, bf16, f32, f32)
    given = [pl.BlockSpec((1, rows, part), lambda i, spot=spot: (spot, 0, i)) for spot in spots]
    given += [pl.BlockSpec((rows, part), lambda i: (0, i))] * len(spots)
    return pl.pallas_call(
        fold_kernel,
        grid=(width // part,),
        in_specs=given,
        out_specs=[pl.BlockSpec((half, part), lambda i: (0, i))] * len(kinds),
        out_shape=[shaped((half, width), kind) for kind in kinds],
        compiler_params=params(),
        cost_estimate=cost(1e6, 12e6),
    )(*nears, *arriveds)


def hidden_kernel(first, wide, n, n_kept, *refs):
    pieces, (joined, back) = refs[: 2 * n], refs[2 * n : 2 * n + 2]
    act_ref, grad_ref, rows_ref, near_ref, *far_refs = refs[2 * n + 2 + n_kept : 3 * n + 6 + n_kept]
    held, sem, out_sem = refs[3 * n + 6 + n_kept :]
    rows = load_pieces(pieces, held, sem)
    step = pl.program_id(0)
    slot_len = rows.shape[0]
    inner = act_ref.shape[1]
    keep = pltpu.make_async_copy(
        held.at[step], rows_ref.at[pl.ds((step + first) * slot_len, slot_len)], out_sem
    )
    keep.start()
    weights, down_weights = joined[:, : 2 * inner], joined[:, 2 * inner :]
    up = dot(rows, weights[:, :inner])
    value = dot(rows, weights[:, inner:])
    slope = jnp.tanh(tanh_scale * (up + tanh_cubic * (up * up * up)))
    gelu = 0.5 * up * (1.0 + slope)
    act_ref[...] = (gelu * value).astype(bf16)
    rise = 0.5 * (1.0 + slope) + 0.5 * up * (1.0 - slope * slope) * (
        tanh_scale * (1.0 + 3.0 * tanh_cubic * (up * up))
    )
    grad = times_rows_back(back[...], down_weights, wide)
    grad_ref[:, :inner] = (grad * value * rise).astype(bf16)
    grad_ref[:, inner:] = (grad * gelu).astype(bf16)
    split_out(dot_nt(grad_ref[...], weights), near_ref, far_refs, slice(None))
    keep.wait()


def hidden_units(first, pieces, joined, back, kept, inner, wide):
    n = len(pieces) // 2
    rows, width = pieces[0].shape
    slot_len = 2 * rows
    total = back.shape[0]

    def at(cols):
        return pl.BlockSpec((slot_len, cols), lambda i: (i + first, 0))

    return pl.pallas_call(
        functools.partial(hidden_kernel, first, wide, n, len(kept)),
        grid=(n,),
        in_specs=[ANY] * (2 * n)
        + [
            pl.BlockSpec(memory_space=pltpu.VMEM),
            at(width),
        ]
        + [ANY] * len(kept),
        out_specs=[at(inner), at(2 * inner), ANY, *split_specs(n, rows, width)],
        out_shape=[
            pltpu.HBM((total, inner), bf16),
            pltpu.HBM((total, 2 * inner), bf16),
            pltpu.HBM((total, width), bf16),
            *split_shapes(n, rows, width, pltpu.HBM),
        ],
        scratch_shapes=[
            pltpu.VMEM((n, slot_len, width), bf16),
            pltpu.SemaphoreType.DMA((2 * n,)),
            pltpu.SemaphoreType.DMA,
        ],
        input_output_aliases={2 * n + 2 + i: i for i in range(len(kept))},
        compiler_params=params(44),
        cost_estimate=cost(10 * n * slot_len * width * inner, 15e6 if n > 1 else 60e6),
    )(*pieces, joined, back, *kept)


def retain_back_kernel(first, wide, n, n_kept, *refs):
    pieces = refs[: 2 * n]
    out_weights, decays, query, key, value, gate_ref, scores, retained_ref = refs[2 * n : 2 * n + 8]
    grad_ref, rows_ref = refs[2 * n + 8 + n_kept : 2 * n + 10 + n_kept]
    held, sem, out_sem = refs[2 * n + 10 + n_kept :]
    rows = load_pieces(pieces, held, sem)
    step = pl.program_id(0)
    slot_len = rows.shape[0]
    keep = pltpu.make_async_copy(
        held.at[step], rows_ref.at[pl.ds((step + first) * slot_len, slot_len)], out_sem
    )
    keep.start()
    dk, dv = query.shape[1], value.shape[1]
    grad = times_rows_back(rows, out_weights[...], wide)
    retained, gate = retained_ref[...], gate_ref[...]
    scale = lax.rsqrt(jnp.mean(retained * retained, axis=-1, keepdims=True) + group_floor)
    sigma = jax.nn.sigmoid(gate)
    normed = retained * scale
    grad_ref[:, dv : 2 * dv] = (grad * normed * (sigma * (1.0 + gate * (1.0 - sigma)))).astype(bf16)
    grad = grad * (gate * sigma)
    mean = jnp.mean(normed * grad, axis=-1, keepdims=True)
    grad_retained = (scale * (grad - normed * mean)).astype(bf16)
    grad_scores = (dot_nt(grad_retained, value[...]) * decays[...]).astype(bf16)
    grad_ref[:, :dv] = dot_tn(scores[0], grad_retained).astype(bf16)
    grad_ref[:, 2 * dv : 2 * dv + dk] = dot(grad_scores, key[...]).astype(bf16)
    grad_ref[:, 2 * dv + dk :] = dot_tn(grad_scores, query[...]).astype(bf16)
    keep.wait()


def retain_back(first, pieces, joined, decays, query, key, value, gate, scores, retained, kept, wide):
    n = len(pieces) // 2
    rows, width = pieces[0].shape
    slot_len = 2 * rows
    total, dk = query.shape
    dv = value.shape[1]

    def at(cols):
        return pl.BlockSpec((slot_len, cols), lambda i: (i + first, 0))

    return pl.pallas_call(
        functools.partial(retain_back_kernel, first, wide, n, len(kept)),
        grid=(n,),
        in_specs=[ANY] * (2 * n)
        + [
            pl.BlockSpec((width, dv), lambda i: (0, 3), pipeline_mode=pl.Buffered(1)),
            whole((slot_len, slot_len)),
            at(dk),
            at(dk),
            at(dv),
            at(dv),
            pl.BlockSpec((1, slot_len, slot_len), lambda i: (i + first, 0, 0)),
            at(dv),
        ]
        + [ANY] * len(kept),
        out_specs=[at(2 * dk + 2 * dv), ANY],
        out_shape=[shaped((total, 2 * dk + 2 * dv), bf16), shaped((total, width), bf16)],
        scratch_shapes=[
            pltpu.VMEM((n, slot_len, width), bf16),
            pltpu.SemaphoreType.DMA((2 * n,)),
            pltpu.SemaphoreType.DMA,
        ],
        input_output_aliases={2 * n + 8 + i: i for i in range(len(kept))},
        compiler_params=params(),
        cost_estimate=cost(4 * n * slot_len * width * dv, 15e6),
    )(*pieces, joined, decays, query, key, value, gate, scores, retained, *kept)


def grad_kernel(left, right, grad_ref):
    grad_ref[...] = dot_tn(left[...], right[...]).astype(bf16)


def columns_grad(left, right, block, cols):
    total, width = left.shape
    part = width // 4
    return pl.pallas_call(
        grad_kernel,
        grid=(width // part,),
        in_specs=[
            pl.BlockSpec((total, part), lambda i: (0, i)),
            pl.BlockSpec((total, cols), lambda i: (0, block), pipeline_mode=pl.Buffered(1)),
        ],
        out_specs=by_slot(part, cols),
        out_shape=shaped((width, cols), bf16),
        compiler_params=params(),
        cost_estimate=cost(2 * total * width * cols, 20e6),
    )(left, right)


def places_grad_kernel(me_ref, left, right, own, others, held, sem):
    step = pl.program_id(0)
    slot = step % 2
    held[slot] = dot_tn(left[...], right[...]).astype(bf16)
    shard = held.shape[1] // PLANE

    def each(step, slot, act):
        def copy(j, target):
            return pltpu.make_async_copy(held.at[slot, pl.ds(j * shard, shard)], target, sem.at[slot, j])

        for j in range(PLANE):
            k = me_ref[0] ^ j

            @pl.when(k == 0)
            def here(j=j):
                act(copy(j, own.at[pl.ds(pl.multiple_of(step * shard, shard), shard)]))

            @pl.when(k != 0)
            def there(j=j, k=k):
                at = pl.multiple_of((step * (PLANE - 1) + k - 1) * shard, shard)
                act(copy(j, others.at[pl.ds(at, shard)]))

    each(step, slot, lambda one: one.start())

    @pl.when(step > 0)
    def before():
        each(step - 1, 1 - slot, lambda one: one.wait())

    @pl.when(step == pl.num_programs(0) - 1)
    def last():
        each(step, slot, lambda one: one.wait())


def places_grad(me, left, right, depth):
    total, width = left.shape
    cols = right.shape[1]
    part = width // depth
    return pl.pallas_call(
        places_grad_kernel,
        grid=(depth,),
        in_specs=[
            pl.BlockSpec(memory_space=pltpu.SMEM),
            pl.BlockSpec((total, part), lambda i: (0, i)),
            whole((total, cols)),
        ],
        out_specs=[ANY, ANY],
        out_shape=[
            shaped((width // PLANE, cols), bf16),
            shaped((width // PLANE * (PLANE - 1), cols), bf16),
        ],
        scratch_shapes=[pltpu.VMEM((2, part, cols), bf16), pltpu.SemaphoreType.DMA((2, PLANE))],
        compiler_params=params(),
        cost_estimate=cost(2 * total * width * cols, 20e6),
    )(me, left, right)


def rows_grad(left, right, wide):
    total, inner = left.shape
    blocks = right.shape[1] // wide
    return pl.pallas_call(
        grad_kernel,
        grid=(blocks,),
        in_specs=[whole((total, inner)), pl.BlockSpec((total, wide), lambda i: (0, i))],
        out_specs=by_slot(inner, wide),
        out_shape=shaped((blocks * inner, wide), bf16),
        compiler_params=params(),
        cost_estimate=cost(2 * total * inner * wide * blocks, 20e6),
    )(left, right)


def place_grads_kernel(n, ks, n_kept, me_ref, *refs):
    ins, outs, held, sem = refs[: len(ks)], refs[len(ks) + n_kept : -2], refs[-2], refs[-1]
    place = me_ref[0]
    copies = []
    for b, k in enumerate(ks):
        held[b] = ins[b][...].astype(f32)
        at = 0
        for i, out in enumerate(outs):
            part = out.shape[1] // PLANE
            one = pltpu.make_async_copy(
                held.at[b, :, pl.ds(at, part)], out.at[:, lanes(place ^ k, part)], sem.at[b * n + i]
            )
            one.start()
            copies.append(one)
            at += part
    for one in copies:
        one.wait()


def place_columns(me, blocks, widths, ks=tuple(range(PLANE)), kept=()):
    rows = blocks[0].shape[0]
    n = len(widths)
    return pl.pallas_call(
        functools.partial(place_grads_kernel, n, ks, len(kept)),
        in_specs=[pl.BlockSpec(memory_space=pltpu.SMEM)]
        + [pl.BlockSpec(memory_space=pltpu.VMEM)] * len(ks)
        + [ANY] * len(kept),
        out_specs=[ANY] * n,
        out_shape=[shaped((rows, PLANE * w), f32) for w in widths],
        scratch_shapes=[
            pltpu.VMEM((len(ks), *blocks[0].shape), f32),
            pltpu.SemaphoreType.DMA((len(ks) * n,)),
        ],
        input_output_aliases={1 + len(ks) + i: i for i in range(len(kept))},
        compiler_params=params(),
        cost_estimate=cost(0, 8e6),
    )(me, *blocks, *kept)


def place_rows_kernel(me_ref, *refs):
    ins, out, held, sem = refs[:PLANE], refs[PLANE], refs[-2], refs[-1]
    rows = ins[0].shape[0]
    copies = []
    for k in range(PLANE):
        held[k] = ins[k][...].astype(f32)
        one = pltpu.make_async_copy(held.at[k], out.at[lanes(me_ref[0] ^ k, rows), :], sem.at[k])
        one.start()
        copies.append(one)
    for one in copies:
        one.wait()


def place_rows(me, blocks):
    rows, cols = blocks[0].shape
    return pl.pallas_call(
        place_rows_kernel,
        in_specs=[pl.BlockSpec(memory_space=pltpu.SMEM)]
        + [pl.BlockSpec(memory_space=pltpu.VMEM)] * PLANE,
        out_specs=ANY,
        out_shape=shaped((PLANE * rows, cols), f32),
        scratch_shapes=[pltpu.VMEM((PLANE, rows, cols), f32), pltpu.SemaphoreType.DMA((PLANE,))],
        compiler_params=params(),
        cost_estimate=cost(0, 4e6),
    )(me, *blocks)


def cut_sums(me, columns, rows):
    width = columns.shape[1]
    shard = columns.shape[0] // PLANE
    blocks = [r.shape[0] // shard for r in rows]

    def plan(place, ins, outs):
        copies = []
        for k in range(PLANE):
            copies.append((ins[0].at[lanes(place ^ k, shard), :], outs[k].at[:, pl.ds(0, width)]))
            at = width
            for r, count in zip(ins[1:], blocks):
                for a in range(count):
                    source = r.at[pl.ds(a * shard, shard), lanes(place ^ k, shard)]
                    copies.append((source, outs[k].at[:, pl.ds(at, shard)]))
                    at += shard
        return copies

    shapes = [shaped((shard, width + shard * sum(blocks)), bf16)] * PLANE
    return place_copies(plan, PLANE * (1 + sum(blocks)), me, [columns, *rows], shapes)


def place_sums_kernel(parts, blocks, me_ref, *refs):
    ins, outs, held, sem = refs[:PLANE], refs[PLANE:-2], refs[-2], refs[-1]
    place = me_ref[0]
    shard = ins[0].shape[0]
    copies = []
    for k in range(PLANE):
        held[k] = ins[k][...].astype(f32)
        at = 0
        moves = []
        for out, part in zip(outs, parts):
            moves.append((held.at[k, :, pl.ds(at, part)], out.at[:, lanes(place ^ k, part)]))
            at += part
        for out, count in zip(outs[len(parts) :], blocks):
            for a in range(count):
                spot = pl.multiple_of((place ^ k) * count * shard + a * shard, shard)
                moves.append((held.at[k, :, pl.ds(at, shard)], out.at[pl.ds(spot, shard), :]))
                at += shard
        for n, move in enumerate(moves):
            copies.append(pltpu.make_async_copy(*move, sem.at[k, n]))
            copies[-1].start()
    for one in copies:
        one.wait()


def place_sums(me, pieces, parts, inners):
    shard, full = pieces[0].shape
    blocks = [inner // shard for inner in inners]
    return pl.pallas_call(
        functools.partial(place_sums_kernel, parts, blocks),
        in_specs=[pl.BlockSpec(memory_space=pltpu.SMEM)] + [pl.BlockSpec(memory_space=pltpu.VMEM)] * PLANE,
        out_specs=[ANY] * (len(parts) + len(blocks)),
        out_shape=[shaped((shard, PLANE * part), f32) for part in parts]
        + [shaped((PLANE * inner, shard), f32) for inner in inners],
        scratch_shapes=[
            pltpu.VMEM((PLANE, shard, full), f32),
            pltpu.SemaphoreType.DMA((PLANE, len(parts) + sum(blocks))),
        ],
        compiler_params=params(),
        cost_estimate=cost(0, 8e6),
    )(me, *pieces)


def hop(value, bits, count):
    return lax.ppermute(value, "dp", [(i, i ^ bits) for i in range(count)])


def swap(value):
    return lax.ppermute(value, "tensor", [(0, 1), (1, 0)])


def trade(blocks, count):
    return [blocks[0]] + [hop(blocks[k], k, count) for k in range(1, PLANE)]


def halves_kernel(first, second, top_ref, bottom_ref):
    top_ref[...] = first[...]
    bottom_ref[...] = second[...]


def halves(first, second):
    rows, width = first.shape
    half, part = rows // 2, width // 2
    out = pl.BlockSpec((half, part), lambda i: (0, i))
    return pl.pallas_call(
        halves_kernel,
        grid=(2,),
        in_specs=[out, pl.BlockSpec((half, part), lambda i: (1, i))],
        out_specs=[out, out],
        out_shape=[pltpu.HBM((half, width), bf16)] * 2,
        compiler_params=params(),
        cost_estimate=cost(0, 4e6),
    )(first, second)


def spread(mine, count, beside=None):
    from_x = hop(mine, 1, count)
    from_y = hop(mine, 2, count)
    pieces = [mine, swap(mine)]
    if beside:
        from_x, from_y = after((from_x, from_y), beside(0, 1, pieces))
    top, bottom = halves(from_x, from_y)
    far_a, far_b = hop(top, 2, count), hop(bottom, 1, count)
    nearer = [from_x, swap(from_x), from_y, swap(from_y)]
    if beside:
        far_a, far_b = after((far_a, far_b), beside(1, 3, nearer))
    far = jnp.concatenate([far_a, far_b])
    far = [far, swap(far)]
    if beside:
        return beside(3, 4, far)
    return pieces + nearer + far


def fold(groups, count, before=None, first=None, second=None):
    slots = {}

    def take(lo, near, *fars):
        for k, far in enumerate(fars):
            slots[lo + k] = near, swap(far), k

    for group in groups:
        take(*group)
    given = [(near, arrived) for near, arrived, _ in (slots[k] for k in (1, 2, 3))]
    made = []
    if before:
        made.append(before(slots[1][1]))
        given = after(given, made)
    cut = fold_cut([(*pair, slots[k][2]) for k, pair in zip((1, 2, 3), given)])
    to_x1, to_y2, to_x3, to_y3, keep_x, keep_y = cut
    half, width = to_x1.shape
    x1, y2 = hop(to_x1, 1, count), hop(to_y2, 2, count)
    x3, y3 = hop(to_x3, 1, count), hop(to_y3, 2, count)
    if first:
        made.append(first((to_x3, to_y3)))
        x3, y3 = after((x3, y3), made)
    if 0 not in slots:
        take(*made[-1][0])
    near_0, arrived_0, spot = slots[0]
    to_y, to_x = (keep_y + x3.astype(f32)).astype(bf16), (keep_x + y3.astype(f32)).astype(bf16)
    last_y, last_x = hop(to_y, 2, count), hop(to_x, 1, count)
    if second:
        made.append(second((to_x, to_y)))
        last_y, last_x = after((last_y, last_x), made[-1])
    near_0, arrived_0 = near_0[spot], arrived_0.astype(f32)
    summed = [
        near_0[:half] + arrived_0[:half] + (x1.astype(f32) + last_y.astype(f32)),
        near_0[half:] + arrived_0[half:] + (y2.astype(f32) + last_x.astype(f32)),
    ]
    return jnp.concatenate(summed), *made


def after(values, done):
    return lax.optimization_barrier((values, done))[0]


def on_device(
    tokens,
    lengths,
    w_query,
    w_key,
    w_value,
    w_gate,
    w_out,
    w_ffgate,
    w_ffup,
    w_ffdown,
    gain_attn,
    gain_mlp,
    cotangent,
):
    count = lax.axis_size("dp")
    depth = count // PLANE
    columns = [[q + PLANE * z for z in range(depth)] for q in range(PLANE)]
    place = lax.axis_index("dp")
    me = place % PLANE
    me_scalar = me.reshape(1).astype(jnp.int32)
    core = lax.axis_index("tensor")
    rows, width = tokens.shape
    wide = width // depth
    shard = w_query.shape[0]
    dk = w_query.shape[1] // PLANE
    dv = w_value.shape[1] // PLANE
    inner = w_ffgate.shape[1] // PLANE
    assert dk == DK and dv == DV

    def gather_depth(block):
        return lax.all_gather(block, "dp", axis=0, tiled=True, axis_index_groups=columns)

    def sum_depth(block):
        return lax.psum_scatter(block, "dp", scatter_dimension=0, tiled=True, axis_index_groups=columns)

    attn_cuts = cut_weights(me_scalar, (w_query, w_key, w_value, w_gate), w_out)
    attn_blocks = trade(attn_cuts, count)
    attn_width = 2 * dk + 2 * dv
    if depth == 4:
        own_gathered = gather_depth(attn_cuts[0])
        attn_own = jnp.concatenate(attn_blocks[1:])
        attn_weights = own_gathered, gather_depth(attn_own)
    else:
        attn_own = join_weights(me_scalar, attn_blocks, attn_width)
        attn_joined = gather_depth(attn_own)

    gains = jnp.stack([gain_attn, gain_mlp])[None]
    step = 1
    while step < count:
        gains = jnp.concatenate([gains, hop(gains, step, count)])
        step *= 2
    gains = jnp.take(gains, place ^ jnp.arange(count), axis=0).astype(f32)
    gain_first = gains[:, 0].reshape(1, width)
    gain_second = gains[:, 1].reshape(1, width)

    input_rows = tokens.astype(f32)
    first_scale = lax.rsqrt(jnp.mean(input_rows * input_rows, axis=-1, keepdims=True) + norm_eps)
    normed_attn = (input_rows * first_scale * gain_first).astype(bf16)
    attn_pieces = spread(after(normed_attn, attn_own), count)

    ff_cuts = after(cut_weights(me_scalar, (w_ffgate, w_ffup), w_ffdown), attn_pieces)
    ff_own = join_weights(me_scalar, trade(ff_cuts, count), 2 * inner)
    ff_joined = gather_depth(ff_own)

    local = jnp.arange(rows, dtype=jnp.int32)
    valid_rows = ((core * rows + local) < lengths[0]).astype(f32)[:, None]
    back_rows = valid_rows * cotangent.astype(f32)
    back_pieces = spread(after(back_rows.astype(bf16), ff_own), count)
    back_all = jnp.concatenate(back_pieces)

    positions = jnp.concatenate([core * rows + local, (1 - core) * rows + local])
    decays = decay_table(positions, core * PLANE + me)
    attn_pieces = after(attn_pieces, back_all)
    kept, groups = [], []
    if depth == 4:
        *kept, attn_joined = retain(1, attn_pieces[2:], attn_weights, decays, kept, dk, dv, wide, me_scalar)
    else:
        kept = retain(1, attn_pieces[2:], attn_joined, decays, kept, dk, dv, wide)
    kept, terms = kept[:8], kept[8:]
    groups.append((1, *terms))

    def retain_own(done):
        pieces = after(attn_pieces[:2], done)
        made = retain(0, pieces, attn_joined, decays, kept, dk, dv, wide)
        return (0, *made[8:]), made[:8]

    added, (_, made) = fold(groups, count, first=retain_own)
    query, key, value, gate, scores, retained, gated, attn_all = made
    hidden = input_rows + added

    second_scale = lax.rsqrt(jnp.mean(hidden * hidden, axis=-1, keepdims=True) + norm_eps)
    normed_mlp = (hidden * second_scale * gain_second).astype(bf16)

    state = {"kept": (), "groups": []}

    def units(lo, hi, pieces):
        if lo == 0:
            state["own"] = pieces
            return ()
        if lo == 1:
            lo, pieces = 0, state["own"] + pieces
        made = hidden_units(lo, pieces, ff_joined, back_all, state["kept"], inner, wide)
        state["kept"] = made[:3]
        state["groups"].append((lo, *made[3:]))
        return state["kept"]

    inner_act, grad_up, mlp_all = spread(normed_mlp, count, units)

    def down_grad(_):
        return rows_grad(inner_act, back_all, wide)

    def up_grad(done):
        return columns_grad(*after((mlp_all, grad_up), done), 0, 2 * inner)

    grad_normed, grad_down, grad_ff = fold(state["groups"], count, down_grad, up_grad)
    down_part = sum_depth(grad_down)
    ff_part = sum_depth(grad_ff)
    scaled = grad_normed * gain_second
    grad_hidden = back_rows + second_scale * (
        scaled
        - hidden * (second_scale * second_scale) * jnp.mean(hidden * scaled, axis=-1, keepdims=True)
    )
    gain_term_mlp = jnp.sum(grad_normed * hidden * second_scale, axis=0)

    state = {"kept": ()}

    def heads(lo, hi, pieces):
        if lo == 3:
            pieces = after(pieces, down_part)
        state["kept"] = retain_back(
            lo, pieces, attn_joined, decays, query, key, value, gate, scores, retained, state["kept"], wide
        )
        if lo > 0:
            return state["kept"]
        act = after(inner_act, pieces)
        state["mlp"] = project(act, ff_joined, 2, wide)
        return state["kept"], state["mlp"]

    grad_wide, attn_grad_all = spread(grad_hidden.astype(bf16), count, heads)
    grad_out = rows_grad(gated, attn_grad_all, wide)
    out_part = sum_depth(grad_out)

    own_grad, others_grad = places_grad(me_scalar, attn_all, after(grad_wide, grad_out), depth)

    def back_terms(done):
        return project_back(after(grad_wide, (done, ff_part)), attn_joined, dk, dv)

    mlp_added, _, attn_terms = fold([(0, *state["mlp"])], count, lambda _: others_grad, back_terms)
    others_part = sum_depth(others_grad)
    output = (valid_rows * (hidden + mlp_added)).astype(bf16)
    if shard % 128 == 0:
        sums = trade(cut_sums(me_scalar, ff_part, (down_part, out_part)), count)
    else:
        sums = out_part
    grad_normed_attn, *_ = fold([(0, *attn_terms)], count, lambda _: mlp_added, lambda _: sums)
    own_grad = after(own_grad, grad_normed_attn)
    own_part = sum_depth(own_grad)
    gain_term_attn = jnp.sum(grad_normed_attn * input_rows * first_scale, axis=0)
    scaled_first = grad_normed_attn * gain_first
    tokens_grad = grad_hidden + first_scale * (
        scaled_first
        - input_rows
        * (first_scale * first_scale)
        * jnp.mean(input_rows * scaled_first, axis=-1, keepdims=True)
    )
    tokens_grad = tokens_grad.astype(bf16)

    def back_columns(block, widths):
        cuts = [lax.dynamic_slice_in_dim(block, (me ^ k) * shard, shard, 0).astype(bf16) for k in range(PLANE)]
        return place_columns(me_scalar, trade(cuts, count), widths)

    def back_rows_of(block):
        cuts = [lax.dynamic_slice_in_dim(block, (me ^ k) * shard, shard, 1).astype(bf16) for k in range(PLANE)]
        return place_rows(me_scalar, trade(cuts, count))

    if shard % 128 == 0:
        ffgate_sum, ffup_sum, down_sum, out_sum = place_sums(me_scalar, sums, (inner, inner), (inner, dv))
    else:
        down_sum, out_sum = back_rows_of(down_part), back_rows_of(out_part)
        ffgate_sum, ffup_sum = back_columns(ff_part, (inner, inner))
    others_part = after(others_part, (tokens_grad, output))
    blocks = [hop(others_part[k * shard : (k + 1) * shard], k + 1, count) for k in range(PLANE - 1)]
    gain_terms = jnp.stack([gain_term_attn, gain_term_mlp])
    bit = count // 2
    while bit >= 1:
        side = (place // bit) % 2
        cut = gain_terms.reshape(2, 2, -1)
        kept = lax.dynamic_index_in_dim(cut, side, 1, keepdims=False)
        sent = lax.dynamic_index_in_dim(cut, 1 - side, 1, keepdims=False)
        gain_terms = kept + hop(sent, bit, count)
        bit //= 2
    cut = after(gain_terms, blocks).reshape(2, 2, -1)
    kept = lax.dynamic_index_in_dim(cut, core, 1, keepdims=False)
    sent = lax.dynamic_index_in_dim(cut, 1 - core, 1, keepdims=False)
    gain_terms = kept + swap(sent)
    early = output, tokens_grad, gain_terms, down_sum, ffgate_sum, ffup_sum, out_sum
    begun = place_columns(me_scalar, blocks, (dv, dv, dk, dk), (1, 2, 3))
    own_part = after(own_part, (begun, early))
    value_sum, gate_sum, query_sum, key_sum = place_columns(me_scalar, [own_part], (dv, dv, dk, dk), (0,), begun)

    return (
        output,
        tokens_grad,
        query_sum,
        key_sum,
        value_sum,
        gate_sum,
        out_sum,
        ffgate_sum,
        ffup_sum,
        down_sum,
        gain_terms[0],
        gain_terms[1],
    )


def solution(mesh):
    return jax.shard_map(
        on_device,
        mesh=mesh,
        in_specs=(
            P(("dp", "tensor"), None),
            P("dp"),
            P("dp", "tensor"),
            P("dp", "tensor"),
            P("dp", "tensor"),
            P("dp", "tensor"),
            P("tensor", "dp"),
            P("dp", "tensor"),
            P("dp", "tensor"),
            P("tensor", "dp"),
            P("dp"),
            P("dp"),
            P(("dp", "tensor"), None),
        ),
        out_specs=(
            P(("dp", "tensor"), None),
            P(("dp", "tensor"), None),
            P("dp", "tensor"),
            P("dp", "tensor"),
            P("dp", "tensor"),
            P("dp", "tensor"),
            P("tensor", "dp"),
            P("dp", "tensor"),
            P("dp", "tensor"),
            P("tensor", "dp"),
            P(("dp", "tensor")),
            P(("dp", "tensor")),
        ),
        check_vma=False,
    )
```

```python
import functools

import jax
import jax.numpy as jnp
from jax import lax
from jax.experimental import pallas as pl
from jax.experimental.pallas import tpu as pltpu
from jax.sharding import PartitionSpec as P

DK = 256
DV = 512
PLANE = 4
SLOTS = ((0, 1), (1, 3), (3, 4))

norm_eps = 1e-06
group_floor = 1.0
tanh_scale = 0.7978845608028654
tanh_cubic = 0.044715

bf16 = jnp.bfloat16
f32 = jnp.float32


def shaped(shape, kind):
    return jax.ShapeDtypeStruct(shape, kind)


def cost(flops, bytes_accessed):
    return pl.CostEstimate(flops=int(flops), bytes_accessed=int(bytes_accessed), transcendentals=0)


def params(mib=62):
    return pltpu.CompilerParams(vmem_limit_bytes=mib * 1024 * 1024)


ANY = pl.BlockSpec(memory_space=pl.ANY)


def whole(shape):
    return pl.BlockSpec(shape, lambda i: (0,) * len(shape), pipeline_mode=pl.Buffered(1))


def by_slot(*shape):
    return pl.BlockSpec(shape, lambda i: (i,) + (0,) * (len(shape) - 1))


def dot(left, right):
    return jnp.dot(left, right, preferred_element_type=f32)


def dot_nt(left, right):
    return lax.dot_general(left, right, (((1,), (1,)), ((), ())), preferred_element_type=f32)


def dot_tn(left, right):
    return lax.dot_general(left, right, (((0,), (0,)), ((), ())), preferred_element_type=f32)


def decay_table(positions, head):
    spacing = positions[:, None] - positions[None, :]
    log_rate = jnp.log1p(-jnp.exp2(-5.0 - head.astype(f32)))
    kept_spacing = jnp.where(spacing >= 0, spacing, jnp.zeros_like(spacing)).astype(f32)
    powers = jnp.exp(kept_spacing * log_rate)
    return jnp.where(spacing >= 0, powers, jnp.zeros_like(powers))


def copy_kernel(plan, n_in, me_ref, *refs):
    ins, outs, sem = refs[:n_in], refs[n_in:-1], refs[-1]
    copies = [
        pltpu.make_async_copy(source, target, sem.at[i])
        for i, (source, target) in enumerate(plan(me_ref[0], ins, outs))
    ]
    for one in copies:
        one.start()
    for one in copies:
        one.wait()


def place_copies(plan, n_copies, me, ins, out_shapes, any_in=False):
    moved = 2 * sum(2 * s.size for s in out_shapes)
    return pl.pallas_call(
        functools.partial(copy_kernel, plan, len(ins)),
        in_specs=[pl.BlockSpec(memory_space=pltpu.SMEM)]
        + [ANY if any_in else pl.BlockSpec(memory_space=pltpu.VMEM)] * len(ins),
        out_specs=[pl.BlockSpec(memory_space=pltpu.VMEM) if any_in else ANY] * len(out_shapes),
        out_shape=out_shapes,
        scratch_shapes=[pltpu.SemaphoreType.DMA((n_copies,))],
        compiler_params=params(),
        cost_estimate=cost(0, moved),
    )(me, *ins)


def lanes(index, size):
    return pl.ds(pl.multiple_of(index * size, size), size)


def cut_weights(me, by_columns, by_rows):
    rows, cols = by_columns[0].shape[0], by_rows.shape[1]
    parts = [w.shape[1] // PLANE for w in by_columns]
    inner = by_rows.shape[0] // PLANE
    width = sum(parts)
    aligned = cols % 128 == 0
    if not aligned:
        by_rows = jnp.moveaxis(by_rows.reshape(PLANE, inner // rows, rows, cols), 1, 2)
        by_rows = jnp.moveaxis(by_rows.reshape(PLANE, rows, -1), 0, 1).reshape(rows, -1)

    def plan(place, ins, outs):
        copies = []
        for k in range(PLANE):
            at = 0
            for w, part in zip(ins, parts):
                copies.append((w.at[:, lanes(place ^ k, part)], outs[k].at[:, pl.ds(at, part)]))
                at += part
            if not aligned:
                copies.append((ins[-1].at[:, lanes(place ^ k, inner)], outs[k].at[:, pl.ds(width, inner)]))
                continue
            for block in range(inner // rows):
                source = pl.ds(pl.multiple_of((place ^ k) * inner + block * rows, rows), rows)
                copies.append((ins[-1].at[source, :], outs[k].at[:, pl.ds(width + block * cols, cols)]))
        return copies

    shapes = [shaped((rows, width + inner), bf16)] * PLANE
    n_copies = PLANE * (len(parts) + (inner // rows if aligned else 1))
    return place_copies(plan, n_copies, me, [*by_columns, by_rows], shapes)


def own_weights(me, by_columns, by_rows):
    rows, cols = by_columns[0].shape[0], by_rows.shape[1]
    parts = [w.shape[1] // PLANE for w in by_columns]
    inner = by_rows.shape[0] // PLANE
    width = sum(parts)

    def plan(place, ins, outs):
        copies, at = [], 0
        for w, part in zip(ins, parts):
            copies.append((w.at[:, lanes(place, part)], outs[0].at[:, pl.ds(at, part)]))
            at += part
        for block in range(inner // rows):
            source = pl.ds(pl.multiple_of(place * inner + block * rows, rows), rows)
            copies.append((ins[-1].at[source, :], outs[0].at[:, pl.ds(width + block * cols, cols)]))
        return copies

    shape = shaped((rows, width + inner), bf16)
    return place_copies(plan, len(parts) + inner // rows, me, [*by_columns, by_rows], [shape], any_in=True)[0]


def join_weights(me, blocks, width):
    rows, inner = blocks[0].shape[0], blocks[0].shape[1] - width
    tall = PLANE * rows
    aligned = rows % 128 == 0
    extra = []
    if not aligned:
        parts = jnp.stack([lax.dynamic_index_in_dim(jnp.stack(blocks), me[0] ^ j, 0, keepdims=False) for j in range(PLANE)])
        parts = parts[:, :, width:].reshape(PLANE, rows, inner // tall, PLANE, rows)
        extra = [jnp.transpose(parts, (3, 1, 2, 0, 4)).reshape(tall, inner)]

    def plan(place, ins, outs):
        copies = []
        for k in range(PLANE):
            copies.append((ins[k].at[:, pl.ds(0, width)], outs[0].at[lanes(place ^ k, rows), pl.ds(0, width)]))
            for block in range(inner // rows if aligned else 0):
                spot = pl.ds(pl.multiple_of(width + (place ^ k) * rows, rows), rows)
                if block >= PLANE:
                    spot = pl.ds(pl.multiple_of(width + (block // PLANE) * tall + (place ^ k) * rows, rows), rows)
                source = ins[k].at[:, pl.ds(width + block * rows, rows)]
                copies.append((source, outs[0].at[pl.ds((block % PLANE) * rows, rows), spot]))
        if not aligned:
            copies.append((ins[PLANE], outs[0].at[:, pl.ds(width, inner)]))
        return copies

    n_copies = PLANE * (1 + inner // rows) if aligned else PLANE + 1
    return place_copies(plan, n_copies, me, [*blocks, *extra], [shaped((tall, width + inner), bf16)])[0]


def load_pieces(pieces, held, sem):
    step = pl.program_id(0)
    rows = pieces[0].shape[0]
    copies = [
        pltpu.make_async_copy(piece, held.at[i // 2, pl.ds((i % 2) * rows, rows)], sem.at[i])
        for i, piece in enumerate(pieces)
    ]

    @pl.when(step == 0)
    def start():
        for one in copies:
            one.start()

    for s in range(len(pieces) // 2):

        @pl.when(step == s)
        def arrive(s=s):
            copies[2 * s].wait()
            copies[2 * s + 1].wait()

    return held[step]


def times_rows(left, right, wide):
    groups = right.shape[1] // wide
    for z in range(right.shape[0] // wide):
        terms = dot(left[:, :wide], right[z * wide : (z + 1) * wide, :wide])
        for g in range(1, groups):
            terms += dot(
                left[:, g * wide : (g + 1) * wide],
                right[z * wide : (z + 1) * wide, g * wide : (g + 1) * wide],
            )
        yield slice(z * wide, (z + 1) * wide), terms


def times_rows_back(left, right, wide):
    made = []
    for g in range(right.shape[1] // wide):
        group = slice(g * wide, (g + 1) * wide)
        terms = dot_nt(left[:, :wide], right[:wide, group])
        for z in range(1, right.shape[0] // wide):
            block = slice(z * wide, (z + 1) * wide)
            terms += dot_nt(left[:, block], right[block, group])
        made.append(terms)
    return made[0] if len(made) == 1 else jnp.concatenate(made, axis=1)


def split_out(terms, near_ref, far_refs, columns):
    rows = near_ref.shape[1]
    near_ref[0, :, columns] = terms[:rows]
    far = terms[rows:].astype(bf16)
    for slot, far_ref in enumerate(far_refs):

        @pl.when(pl.program_id(0) == slot)
        def put(far_ref=far_ref):
            far_ref[:, columns] = far


def split_specs(n, rows, width):
    fars = [pl.BlockSpec((rows, width), lambda i: (0, 0), pipeline_mode=pl.Buffered(1))] * n
    return [by_slot(1, rows, width), *fars]


def split_shapes(n, rows, width, place=shaped):
    return [place((n, rows, width), f32)] + [place((rows, width), bf16)] * n


def weave(place, own, others, target, width, sem):
    planes, full = 4, own.shape[1]
    shard = own.shape[0] // planes
    copies = []
    for plane in range(planes):
        top = plane * PLANE * shard
        for k in range(PLANE):
            if k == 0:
                source = own.at[pl.ds(plane * shard, shard)]
            else:
                source = others.at[pl.ds((plane * (PLANE - 1) + k - 1) * shard, shard)]
            spot = pl.ds(pl.multiple_of(top + (place ^ k) * shard, shard), shard)
            moves = [(source.at[:, pl.ds(0, width)], target.at[spot, pl.ds(0, width)])]
            spot = pl.ds(pl.multiple_of(width + (place ^ k) * shard, shard), shard)
            for a in range((full - width) // shard):
                piece = source.at[:, pl.ds(width + a * shard, shard)]
                moves.append((piece, target.at[pl.ds(top + a * shard, shard), spot]))
            copies += [pltpu.make_async_copy(*move, sem.at[plane, k, n]) for n, move in enumerate(moves)]
    return copies


def retain_kernel(first, wide, n, n_kept, woven, *refs):
    pieces, refs = refs[: 2 * n], refs[2 * n :]
    if woven:
        place_ref, own, others, decays = refs[:4]
        refs = refs[4:]
    else:
        weights, decays = refs[:2]
        refs = refs[2 + n_kept :]
    query_ref, key_ref, value_ref, gate_ref, scores_ref, retained_ref, gated_ref, rows_ref = refs[:8]
    near_ref, *far_refs = refs[8 : 9 + n]
    if woven:
        joined_ref, held, sem, out_sem, weights, weights_sem, joined_sem = refs[9 + n :]
    else:
        held, sem, out_sem = refs[9 + n :]
    step = pl.program_id(0)
    dk, dv = query_ref.shape[1], value_ref.shape[1]
    if woven:
        copies = weave(place_ref[0], own, others, weights, 2 * dk + 2 * dv, weights_sem)
        keep_weights = pltpu.make_async_copy(weights, joined_ref, joined_sem)

        @pl.when(step == 0)
        def bring():
            for one in copies:
                one.start()

    rows = load_pieces(pieces, held, sem)
    slot_len = rows.shape[0]
    keep = pltpu.make_async_copy(
        held.at[step], rows_ref.at[pl.ds((step + first) * slot_len, slot_len)], out_sem
    )
    keep.start()
    if woven:

        @pl.when(step == 0)
        def brought():
            for one in copies:
                one.wait()
            keep_weights.start()

    query_key = dot(rows, weights[:, : 2 * dk]).astype(bf16)
    query, key = query_key[:, :dk], query_key[:, dk:]
    query_ref[...] = query
    key_ref[...] = key
    scores = (dot_nt(query, key) * decays[...]).astype(bf16)
    scores_ref[...] = scores[None]
    value = dot(rows, weights[:, 2 * dk : 2 * dk + dv]).astype(bf16)
    value_ref[...] = value
    retained = dot(scores, value)
    retained_ref[...] = retained
    scale = lax.rsqrt(jnp.mean(retained * retained, axis=-1, keepdims=True) + group_floor)
    gate = dot(rows, weights[:, 2 * dk + dv : 2 * dk + 2 * dv])
    gate_ref[...] = gate
    gated_ref[...] = (gate * jax.nn.sigmoid(gate) * (retained * scale)).astype(bf16)
    for columns, terms in times_rows(gated_ref[...], weights[:, 2 * dk + 2 * dv :], wide):
        split_out(terms, near_ref, far_refs, columns)
    keep.wait()
    if woven:

        @pl.when(step == n - 1)
        def kept():
            keep_weights.wait()


def retain(first, pieces, weights, decays, kept, dk, dv, wide, place=None):
    n = len(pieces) // 2
    rows, width = pieces[0].shape
    slot_len = 2 * rows
    total = PLANE * slot_len

    def at(cols):
        return pl.BlockSpec((slot_len, cols), lambda i: (i + first, 0))

    kept_specs = [at(dk), at(dk), at(dv), at(dv), None, at(dv), at(dv), ANY]
    kept_specs[4] = pl.BlockSpec((1, slot_len, slot_len), lambda i: (i + first, 0, 0))
    out_specs = kept_specs + split_specs(n, rows, width)
    out_shape = [
        shaped((total, dk), bf16),
        shaped((total, dk), bf16),
        shaped((total, dv), bf16),
        shaped((total, dv), f32),
        shaped((PLANE, slot_len, slot_len), bf16),
        shaped((total, dv), f32),
        shaped((total, dv), bf16),
        shaped((total, width), bf16),
        *split_shapes(n, rows, width),
    ]
    scratch_shapes = [
        pltpu.VMEM((n, slot_len, width), bf16),
        pltpu.SemaphoreType.DMA((2 * n,)),
        pltpu.SemaphoreType.DMA,
    ]
    if place is None:
        given = [weights, decays]
        in_specs = [whole(weights.shape), whole((slot_len, slot_len))]
    else:
        assert not kept
        given = [place, *weights, decays]
        in_specs = [pl.BlockSpec(memory_space=pltpu.SMEM), ANY, ANY, whole((slot_len, slot_len))]
        full = weights[0].shape[1]
        shard = weights[0].shape[0] // 4
        out_specs.append(ANY)
        out_shape.append(shaped((width, full), bf16))
        scratch_shapes += [
            pltpu.VMEM((width, full), bf16),
            pltpu.SemaphoreType.DMA((4, PLANE, 1 + (full - 2 * dk - 2 * dv) // shard)),
            pltpu.SemaphoreType.DMA,
        ]
    return pl.pallas_call(
        functools.partial(retain_kernel, first, wide, n, len(kept), place is not None),
        grid=(n,),
        in_specs=[ANY] * (2 * n) + in_specs + [ANY] * len(kept),
        out_specs=out_specs,
        out_shape=out_shape,
        scratch_shapes=scratch_shapes,
        input_output_aliases={2 * n + len(given) + i: i for i in range(len(kept))},
        compiler_params=params(),
        cost_estimate=cost(2.2 * n * slot_len * width * (2 * dk + 3 * dv), 15e6),
    )(*pieces, *given, *kept)


def project_kernel(wide, left, right, near_ref, *far_refs):
    for columns, terms in times_rows(left[...], right[...], wide):
        split_out(terms, near_ref, far_refs, columns)


def project(left, right, block, wide):
    total, inner = left.shape
    width = right.shape[0]
    slot_len = total // PLANE
    rows = slot_len // 2
    return pl.pallas_call(
        functools.partial(project_kernel, wide),
        grid=(PLANE,),
        in_specs=[
            by_slot(slot_len, inner),
            pl.BlockSpec((width, inner), lambda i: (0, block), pipeline_mode=pl.Buffered(1)),
        ],
        out_specs=split_specs(PLANE, rows, width),
        out_shape=split_shapes(PLANE, rows, width),
        compiler_params=params(),
        cost_estimate=cost(2 * total * inner * width, 20e6),
    )(left, right)


def back_kernel(left, first, second, near_ref, *far_refs):
    dv = second.shape[1]
    narrow = first.shape[1] - dv
    terms = dot_nt(left[:, :dv], first[:, narrow:]) + dot_nt(left[:, dv : 2 * dv], second[...])
    terms += dot_nt(left[:, 2 * dv :], first[:, :narrow])
    split_out(terms, near_ref, far_refs, slice(None))


def project_back(left, joined, dk, dv):
    total, inner = left.shape
    width = joined.shape[0]
    slot_len = total // PLANE
    rows = slot_len // 2
    return pl.pallas_call(
        back_kernel,
        grid=(PLANE,),
        in_specs=[
            by_slot(slot_len, inner),
            whole((width, 2 * dk + dv)),
            pl.BlockSpec((width, dv), lambda i: (0, 2), pipeline_mode=pl.Buffered(1)),
        ],
        out_specs=split_specs(PLANE, rows, width),
        out_shape=split_shapes(PLANE, rows, width),
        compiler_params=params(),
        cost_estimate=cost(2 * total * inner * width, 20e6),
    )(left, joined, joined)


def fold_kernel(*refs):
    nears, arriveds = refs[:3], refs[3:6]
    x1_ref, y2_ref, x3_ref, y3_ref, keep_x_ref, keep_y_ref = refs[6:]
    half = x1_ref.shape[0]
    targets = ((x1_ref, keep_x_ref), (keep_y_ref, y2_ref), (x3_ref, y3_ref))
    for near, arrived, (first, second) in zip(nears, arriveds, targets):
        first[...] = (near[0, :half] + arrived[:half].astype(f32)).astype(first.dtype)
        second[...] = (near[0, half:] + arrived[half:].astype(f32)).astype(second.dtype)


def fold_cut(slots):
    nears, arriveds, spots = zip(*slots)
    _, rows, width = nears[0].shape
    half = rows // 2
    part = width // 4
    kinds = (bf16, bf16, bf16, bf16, f32, f32)
    given = [pl.BlockSpec((1, rows, part), lambda i, spot=spot: (spot, 0, i)) for spot in spots]
    given += [pl.BlockSpec((rows, part), lambda i: (0, i))] * len(spots)
    return pl.pallas_call(
        fold_kernel,
        grid=(width // part,),
        in_specs=given,
        out_specs=[pl.BlockSpec((half, part), lambda i: (0, i))] * len(kinds),
        out_shape=[shaped((half, width), kind) for kind in kinds],
        compiler_params=params(),
        cost_estimate=cost(1e6, 12e6),
    )(*nears, *arriveds)


def hidden_kernel(first, wide, n, n_kept, *refs):
    pieces, (joined, back) = refs[: 2 * n], refs[2 * n : 2 * n + 2]
    act_ref, grad_ref, rows_ref, near_ref, *far_refs = refs[2 * n + 2 + n_kept : 3 * n + 6 + n_kept]
    held, sem, out_sem = refs[3 * n + 6 + n_kept :]
    rows = load_pieces(pieces, held, sem)
    step = pl.program_id(0)
    slot_len = rows.shape[0]
    inner = act_ref.shape[1]
    keep = pltpu.make_async_copy(
        held.at[step], rows_ref.at[pl.ds((step + first) * slot_len, slot_len)], out_sem
    )
    keep.start()
    weights, down_weights = joined[:, : 2 * inner], joined[:, 2 * inner :]
    up = dot(rows, weights[:, :inner])
    value = dot(rows, weights[:, inner:])
    slope = jnp.tanh(tanh_scale * (up + tanh_cubic * (up * up * up)))
    gelu = 0.5 * up * (1.0 + slope)
    act_ref[...] = (gelu * value).astype(bf16)
    rise = 0.5 * (1.0 + slope) + 0.5 * up * (1.0 - slope * slope) * (
        tanh_scale * (1.0 + 3.0 * tanh_cubic * (up * up))
    )
    grad = times_rows_back(back[...], down_weights, wide)
    grad_ref[:, :inner] = (grad * value * rise).astype(bf16)
    grad_ref[:, inner:] = (grad * gelu).astype(bf16)
    split_out(dot_nt(grad_ref[...], weights), near_ref, far_refs, slice(None))
    keep.wait()


def hidden_units(first, pieces, joined, back, kept, inner, wide):
    n = len(pieces) // 2
    rows, width = pieces[0].shape
    slot_len = 2 * rows
    total = back.shape[0]

    def at(cols):
        return pl.BlockSpec((slot_len, cols), lambda i: (i + first, 0))

    return pl.pallas_call(
        functools.partial(hidden_kernel, first, wide, n, len(kept)),
        grid=(n,),
        in_specs=[ANY] * (2 * n)
        + [
            pl.BlockSpec(memory_space=pltpu.VMEM),
            at(width),
        ]
        + [ANY] * len(kept),
        out_specs=[at(inner), at(2 * inner), ANY, *split_specs(n, rows, width)],
        out_shape=[
            pltpu.HBM((total, inner), bf16),
            pltpu.HBM((total, 2 * inner), bf16),
            pltpu.HBM((total, width), bf16),
            *split_shapes(n, rows, width, pltpu.HBM),
        ],
        scratch_shapes=[
            pltpu.VMEM((n, slot_len, width), bf16),
            pltpu.SemaphoreType.DMA((2 * n,)),
            pltpu.SemaphoreType.DMA,
        ],
        input_output_aliases={2 * n + 2 + i: i for i in range(len(kept))},
        compiler_params=params(44),
        cost_estimate=cost(10 * n * slot_len * width * inner, 15e6 if n > 1 else 60e6),
    )(*pieces, joined, back, *kept)


def retain_back_kernel(first, wide, n, n_kept, *refs):
    pieces = refs[: 2 * n]
    out_weights, decays, query, key, value, gate_ref, scores, retained_ref = refs[2 * n : 2 * n + 8]
    grad_ref, rows_ref = refs[2 * n + 8 + n_kept : 2 * n + 10 + n_kept]
    held, sem, out_sem = refs[2 * n + 10 + n_kept :]
    rows = load_pieces(pieces, held, sem)
    step = pl.program_id(0)
    slot_len = rows.shape[0]
    keep = pltpu.make_async_copy(
        held.at[step], rows_ref.at[pl.ds((step + first) * slot_len, slot_len)], out_sem
    )
    keep.start()
    dk, dv = query.shape[1], value.shape[1]
    grad = times_rows_back(rows, out_weights[...], wide)
    retained, gate = retained_ref[...], gate_ref[...]
    scale = lax.rsqrt(jnp.mean(retained * retained, axis=-1, keepdims=True) + group_floor)
    sigma = jax.nn.sigmoid(gate)
    normed = retained * scale
    grad_ref[:, dv : 2 * dv] = (grad * normed * (sigma * (1.0 + gate * (1.0 - sigma)))).astype(bf16)
    grad = grad * (gate * sigma)
    mean = jnp.mean(normed * grad, axis=-1, keepdims=True)
    grad_retained = (scale * (grad - normed * mean)).astype(bf16)
    grad_scores = (dot_nt(grad_retained, value[...]) * decays[...]).astype(bf16)
    grad_ref[:, :dv] = dot_tn(scores[0], grad_retained).astype(bf16)
    grad_ref[:, 2 * dv : 2 * dv + dk] = dot(grad_scores, key[...]).astype(bf16)
    grad_ref[:, 2 * dv + dk :] = dot_tn(grad_scores, query[...]).astype(bf16)
    keep.wait()


def retain_back(first, pieces, joined, decays, query, key, value, gate, scores, retained, kept, wide):
    n = len(pieces) // 2
    rows, width = pieces[0].shape
    slot_len = 2 * rows
    total, dk = query.shape
    dv = value.shape[1]

    def at(cols):
        return pl.BlockSpec((slot_len, cols), lambda i: (i + first, 0))

    return pl.pallas_call(
        functools.partial(retain_back_kernel, first, wide, n, len(kept)),
        grid=(n,),
        in_specs=[ANY] * (2 * n)
        + [
            pl.BlockSpec((width, dv), lambda i: (0, 3), pipeline_mode=pl.Buffered(1)),
            whole((slot_len, slot_len)),
            at(dk),
            at(dk),
            at(dv),
            at(dv),
            pl.BlockSpec((1, slot_len, slot_len), lambda i: (i + first, 0, 0)),
            at(dv),
        ]
        + [ANY] * len(kept),
        out_specs=[at(2 * dk + 2 * dv), ANY],
        out_shape=[shaped((total, 2 * dk + 2 * dv), bf16), shaped((total, width), bf16)],
        scratch_shapes=[
            pltpu.VMEM((n, slot_len, width), bf16),
            pltpu.SemaphoreType.DMA((2 * n,)),
            pltpu.SemaphoreType.DMA,
        ],
        input_output_aliases={2 * n + 8 + i: i for i in range(len(kept))},
        compiler_params=params(),
        cost_estimate=cost(4 * n * slot_len * width * dv, 15e6),
    )(*pieces, joined, decays, query, key, value, gate, scores, retained, *kept)


def grad_kernel(left, right, grad_ref):
    grad_ref[...] = dot_tn(left[...], right[...]).astype(bf16)


def columns_grad(left, right, block, cols):
    total, width = left.shape
    part = width // 4
    return pl.pallas_call(
        grad_kernel,
        grid=(width // part,),
        in_specs=[
            pl.BlockSpec((total, part), lambda i: (0, i)),
            pl.BlockSpec((total, cols), lambda i: (0, block), pipeline_mode=pl.Buffered(1)),
        ],
        out_specs=by_slot(part, cols),
        out_shape=shaped((width, cols), bf16),
        compiler_params=params(),
        cost_estimate=cost(2 * total * width * cols, 20e6),
    )(left, right)


def places_grad_kernel(me_ref, left, right, own, others, held, sem):
    step = pl.program_id(0)
    slot = step % 2
    held[slot] = dot_tn(left[...], right[...]).astype(bf16)
    shard = held.shape[1] // PLANE

    def each(step, slot, act):
        def copy(j, target):
            return pltpu.make_async_copy(held.at[slot, pl.ds(j * shard, shard)], target, sem.at[slot, j])

        for j in range(PLANE):
            k = me_ref[0] ^ j

            @pl.when(k == 0)
            def here(j=j):
                act(copy(j, own.at[pl.ds(pl.multiple_of(step * shard, shard), shard)]))

            @pl.when(k != 0)
            def there(j=j, k=k):
                at = pl.multiple_of((step * (PLANE - 1) + k - 1) * shard, shard)
                act(copy(j, others.at[pl.ds(at, shard)]))

    each(step, slot, lambda one: one.start())

    @pl.when(step > 0)
    def before():
        each(step - 1, 1 - slot, lambda one: one.wait())

    @pl.when(step == pl.num_programs(0) - 1)
    def last():
        each(step, slot, lambda one: one.wait())


def places_grad(me, left, right, depth):
    total, width = left.shape
    cols = right.shape[1]
    part = width // depth
    return pl.pallas_call(
        places_grad_kernel,
        grid=(depth,),
        in_specs=[
            pl.BlockSpec(memory_space=pltpu.SMEM),
            pl.BlockSpec((total, part), lambda i: (0, i)),
            whole((total, cols)),
        ],
        out_specs=[ANY, ANY],
        out_shape=[
            shaped((width // PLANE, cols), bf16),
            shaped((width // PLANE * (PLANE - 1), cols), bf16),
        ],
        scratch_shapes=[pltpu.VMEM((2, part, cols), bf16), pltpu.SemaphoreType.DMA((2, PLANE))],
        compiler_params=params(),
        cost_estimate=cost(2 * total * width * cols, 20e6),
    )(me, left, right)


def rows_grad(left, right, wide):
    total, inner = left.shape
    blocks = right.shape[1] // wide
    return pl.pallas_call(
        grad_kernel,
        grid=(blocks,),
        in_specs=[whole((total, inner)), pl.BlockSpec((total, wide), lambda i: (0, i))],
        out_specs=by_slot(inner, wide),
        out_shape=shaped((blocks * inner, wide), bf16),
        compiler_params=params(),
        cost_estimate=cost(2 * total * inner * wide * blocks, 20e6),
    )(left, right)


def place_grads_kernel(n, ks, n_kept, me_ref, *refs):
    ins, outs, held, sem = refs[: len(ks)], refs[len(ks) + n_kept : -2], refs[-2], refs[-1]
    place = me_ref[0]
    copies = []
    for b, k in enumerate(ks):
        held[b] = ins[b][...].astype(f32)
        at = 0
        for i, out in enumerate(outs):
            part = out.shape[1] // PLANE
            one = pltpu.make_async_copy(
                held.at[b, :, pl.ds(at, part)], out.at[:, lanes(place ^ k, part)], sem.at[b * n + i]
            )
            one.start()
            copies.append(one)
            at += part
    for one in copies:
        one.wait()


def place_columns(me, blocks, widths, ks=tuple(range(PLANE)), kept=()):
    rows = blocks[0].shape[0]
    n = len(widths)
    return pl.pallas_call(
        functools.partial(place_grads_kernel, n, ks, len(kept)),
        in_specs=[pl.BlockSpec(memory_space=pltpu.SMEM)]
        + [pl.BlockSpec(memory_space=pltpu.VMEM)] * len(ks)
        + [ANY] * len(kept),
        out_specs=[ANY] * n,
        out_shape=[shaped((rows, PLANE * w), f32) for w in widths],
        scratch_shapes=[
            pltpu.VMEM((len(ks), *blocks[0].shape), f32),
            pltpu.SemaphoreType.DMA((len(ks) * n,)),
        ],
        input_output_aliases={1 + len(ks) + i: i for i in range(len(kept))},
        compiler_params=params(),
        cost_estimate=cost(0, 8e6),
    )(me, *blocks, *kept)


def place_rows_kernel(me_ref, *refs):
    ins, out, held, sem = refs[:PLANE], refs[PLANE], refs[-2], refs[-1]
    rows = ins[0].shape[0]
    copies = []
    for k in range(PLANE):
        held[k] = ins[k][...].astype(f32)
        one = pltpu.make_async_copy(held.at[k], out.at[lanes(me_ref[0] ^ k, rows), :], sem.at[k])
        one.start()
        copies.append(one)
    for one in copies:
        one.wait()


def place_rows(me, blocks):
    rows, cols = blocks[0].shape
    return pl.pallas_call(
        place_rows_kernel,
        in_specs=[pl.BlockSpec(memory_space=pltpu.SMEM)]
        + [pl.BlockSpec(memory_space=pltpu.VMEM)] * PLANE,
        out_specs=ANY,
        out_shape=shaped((PLANE * rows, cols), f32),
        scratch_shapes=[pltpu.VMEM((PLANE, rows, cols), f32), pltpu.SemaphoreType.DMA((PLANE,))],
        compiler_params=params(),
        cost_estimate=cost(0, 4e6),
    )(me, *blocks)


def cut_sums(me, columns, rows):
    width = columns.shape[1]
    shard = columns.shape[0] // PLANE
    blocks = [r.shape[0] // shard for r in rows]

    def plan(place, ins, outs):
        copies = []
        for k in range(PLANE):
            copies.append((ins[0].at[lanes(place ^ k, shard), :], outs[k].at[:, pl.ds(0, width)]))
            at = width
            for r, count in zip(ins[1:], blocks):
                for a in range(count):
                    source = r.at[pl.ds(a * shard, shard), lanes(place ^ k, shard)]
                    copies.append((source, outs[k].at[:, pl.ds(at, shard)]))
                    at += shard
        return copies

    shapes = [shaped((shard, width + shard * sum(blocks)), bf16)] * PLANE
    return place_copies(plan, PLANE * (1 + sum(blocks)), me, [columns, *rows], shapes)


def place_sums_kernel(parts, blocks, me_ref, *refs):
    ins, outs, held, sem = refs[:PLANE], refs[PLANE:-2], refs[-2], refs[-1]
    place = me_ref[0]
    shard = ins[0].shape[0]
    copies = []
    for k in range(PLANE):
        held[k] = ins[k][...].astype(f32)
        at = 0
        moves = []
        for out, part in zip(outs, parts):
            moves.append((held.at[k, :, pl.ds(at, part)], out.at[:, lanes(place ^ k, part)]))
            at += part
        for out, count in zip(outs[len(parts) :], blocks):
            for a in range(count):
                spot = pl.multiple_of((place ^ k) * count * shard + a * shard, shard)
                moves.append((held.at[k, :, pl.ds(at, shard)], out.at[pl.ds(spot, shard), :]))
                at += shard
        for n, move in enumerate(moves):
            copies.append(pltpu.make_async_copy(*move, sem.at[k, n]))
            copies[-1].start()
    for one in copies:
        one.wait()


def place_sums(me, pieces, parts, inners):
    shard, full = pieces[0].shape
    blocks = [inner // shard for inner in inners]
    return pl.pallas_call(
        functools.partial(place_sums_kernel, parts, blocks),
        in_specs=[pl.BlockSpec(memory_space=pltpu.SMEM)] + [pl.BlockSpec(memory_space=pltpu.VMEM)] * PLANE,
        out_specs=[ANY] * (len(parts) + len(blocks)),
        out_shape=[shaped((shard, PLANE * part), f32) for part in parts]
        + [shaped((PLANE * inner, shard), f32) for inner in inners],
        scratch_shapes=[
            pltpu.VMEM((PLANE, shard, full), f32),
            pltpu.SemaphoreType.DMA((PLANE, len(parts) + sum(blocks))),
        ],
        compiler_params=params(),
        cost_estimate=cost(0, 8e6),
    )(me, *pieces)


def hop(value, bits, count):
    return lax.ppermute(value, "dp", [(i, i ^ bits) for i in range(count)])


def swap(value):
    return lax.ppermute(value, "tensor", [(0, 1), (1, 0)])


def trade(blocks, count):
    return [blocks[0]] + [hop(blocks[k], k, count) for k in range(1, PLANE)]


def halves_kernel(first, second, top_ref, bottom_ref):
    top_ref[...] = first[...]
    bottom_ref[...] = second[...]


def halves(first, second):
    rows, width = first.shape
    half, part = rows // 2, width // 2
    out = pl.BlockSpec((half, part), lambda i: (0, i))
    return pl.pallas_call(
        halves_kernel,
        grid=(2,),
        in_specs=[out, pl.BlockSpec((half, part), lambda i: (1, i))],
        out_specs=[out, out],
        out_shape=[pltpu.HBM((half, width), bf16)] * 2,
        compiler_params=params(),
        cost_estimate=cost(0, 4e6),
    )(first, second)


def spread(mine, count, beside=None):
    from_x = hop(mine, 1, count)
    from_y = hop(mine, 2, count)
    pieces = [mine, swap(mine)]
    if beside:
        from_x, from_y = after((from_x, from_y), beside(0, 1, pieces))
    top, bottom = halves(from_x, from_y)
    far_a, far_b = hop(top, 2, count), hop(bottom, 1, count)
    nearer = [from_x, swap(from_x), from_y, swap(from_y)]
    if beside:
        far_a, far_b = after((far_a, far_b), beside(1, 3, nearer))
    far = jnp.concatenate([far_a, far_b])
    far = [far, swap(far)]
    if beside:
        return beside(3, 4, far)
    return pieces + nearer + far


def fold(groups, count, before=None, first=None, second=None):
    slots = {}

    def take(lo, near, *fars):
        for k, far in enumerate(fars):
            slots[lo + k] = near, swap(far), k

    for group in groups:
        take(*group)
    given = [(near, arrived) for near, arrived, _ in (slots[k] for k in (1, 2, 3))]
    made = []
    if before:
        made.append(before(slots[1][1]))
        given = after(given, made)
    cut = fold_cut([(*pair, slots[k][2]) for k, pair in zip((1, 2, 3), given)])
    to_x1, to_y2, to_x3, to_y3, keep_x, keep_y = cut
    half, width = to_x1.shape
    x1, y2 = hop(to_x1, 1, count), hop(to_y2, 2, count)
    x3, y3 = hop(to_x3, 1, count), hop(to_y3, 2, count)
    if first:
        made.append(first((to_x3, to_y3)))
        x3, y3 = after((x3, y3), made)
    if 0 not in slots:
        take(*made[-1][0])
    near_0, arrived_0, spot = slots[0]
    to_y, to_x = (keep_y + x3.astype(f32)).astype(bf16), (keep_x + y3.astype(f32)).astype(bf16)
    last_y, last_x = hop(to_y, 2, count), hop(to_x, 1, count)
    if second:
        made.append(second((to_x, to_y)))
        last_y, last_x = after((last_y, last_x), made[-1])
    near_0, arrived_0 = near_0[spot], arrived_0.astype(f32)
    summed = [
        near_0[:half] + arrived_0[:half] + (x1.astype(f32) + last_y.astype(f32)),
        near_0[half:] + arrived_0[half:] + (y2.astype(f32) + last_x.astype(f32)),
    ]
    return jnp.concatenate(summed), *made


def after(values, done):
    return lax.optimization_barrier((values, done))[0]


def on_device(
    tokens,
    lengths,
    w_query,
    w_key,
    w_value,
    w_gate,
    w_out,
    w_ffgate,
    w_ffup,
    w_ffdown,
    gain_attn,
    gain_mlp,
    cotangent,
):
    count = lax.axis_size("dp")
    depth = count // PLANE
    columns = [[q + PLANE * z for z in range(depth)] for q in range(PLANE)]
    place = lax.axis_index("dp")
    me = place % PLANE
    me_scalar = me.reshape(1).astype(jnp.int32)
    core = lax.axis_index("tensor")
    rows, width = tokens.shape
    wide = width // depth
    shard = w_query.shape[0]
    dk = w_query.shape[1] // PLANE
    dv = w_value.shape[1] // PLANE
    inner = w_ffgate.shape[1] // PLANE
    assert dk == DK and dv == DV

    def gather_depth(block):
        return lax.all_gather(block, "dp", axis=0, tiled=True, axis_index_groups=columns)

    def sum_depth(block):
        return lax.psum_scatter(block, "dp", scatter_dimension=0, tiled=True, axis_index_groups=columns)

    attn_cuts = cut_weights(me_scalar, (w_query, w_key, w_value, w_gate), w_out)
    attn_blocks = trade(attn_cuts, count)
    attn_width = 2 * dk + 2 * dv
    if depth == 4:
        own_gathered = gather_depth(own_weights(me_scalar, (w_query, w_key, w_value, w_gate), w_out))
        attn_own = jnp.concatenate(attn_blocks[1:])
        attn_weights = own_gathered, gather_depth(attn_own)
    else:
        attn_own = join_weights(me_scalar, attn_blocks, attn_width)
        attn_joined = gather_depth(attn_own)

    gains = jnp.stack([gain_attn, gain_mlp])[None]
    step = 1
    while step < count:
        gains = jnp.concatenate([gains, hop(gains, step, count)])
        step *= 2
    gains = jnp.take(gains, place ^ jnp.arange(count), axis=0).astype(f32)
    gain_first = gains[:, 0].reshape(1, width)
    gain_second = gains[:, 1].reshape(1, width)

    input_rows = tokens.astype(f32)
    first_scale = lax.rsqrt(jnp.mean(input_rows * input_rows, axis=-1, keepdims=True) + norm_eps)
    normed_attn = (input_rows * first_scale * gain_first).astype(bf16)
    attn_pieces = spread(after(normed_attn, attn_own), count)

    ff_cuts = after(cut_weights(me_scalar, (w_ffgate, w_ffup), w_ffdown), attn_pieces)
    ff_own = join_weights(me_scalar, trade(ff_cuts, count), 2 * inner)
    ff_joined = gather_depth(ff_own)

    local = jnp.arange(rows, dtype=jnp.int32)
    valid_rows = ((core * rows + local) < lengths[0]).astype(f32)[:, None]
    back_rows = valid_rows * cotangent.astype(f32)
    back_pieces = spread(after(back_rows.astype(bf16), ff_own), count)
    back_all = jnp.concatenate(back_pieces)

    positions = jnp.concatenate([core * rows + local, (1 - core) * rows + local])
    decays = decay_table(positions, core * PLANE + me)
    attn_pieces = after(attn_pieces, back_all)
    kept, groups = [], []
    if depth == 4:
        *kept, attn_joined = retain(1, attn_pieces[2:], attn_weights, decays, kept, dk, dv, wide, me_scalar)
    else:
        kept = retain(1, attn_pieces[2:], attn_joined, decays, kept, dk, dv, wide)
    kept, terms = kept[:8], kept[8:]
    groups.append((1, *terms))

    def retain_own(done):
        pieces = after(attn_pieces[:2], done)
        made = retain(0, pieces, attn_joined, decays, kept, dk, dv, wide)
        return (0, *made[8:]), made[:8]

    added, (_, made) = fold(groups, count, first=retain_own)
    query, key, value, gate, scores, retained, gated, attn_all = made
    hidden = input_rows + added

    second_scale = lax.rsqrt(jnp.mean(hidden * hidden, axis=-1, keepdims=True) + norm_eps)
    normed_mlp = (hidden * second_scale * gain_second).astype(bf16)

    state = {"kept": (), "groups": []}

    def units(lo, hi, pieces):
        if lo == 0:
            state["own"] = pieces
            return ()
        if lo == 1:
            lo, pieces = 0, state["own"] + pieces
        made = hidden_units(lo, pieces, ff_joined, back_all, state["kept"], inner, wide)
        state["kept"] = made[:3]
        state["groups"].append((lo, *made[3:]))
        return state["kept"]

    inner_act, grad_up, mlp_all = spread(normed_mlp, count, units)

    def down_grad(_):
        return rows_grad(inner_act, back_all, wide)

    def up_grad(done):
        return columns_grad(*after((mlp_all, grad_up), done), 0, 2 * inner)

    grad_normed, grad_down, grad_ff = fold(state["groups"], count, down_grad, up_grad)
    down_part = sum_depth(grad_down)
    ff_part = sum_depth(grad_ff)
    scaled = grad_normed * gain_second
    grad_hidden = back_rows + second_scale * (
        scaled
        - hidden * (second_scale * second_scale) * jnp.mean(hidden * scaled, axis=-1, keepdims=True)
    )
    gain_term_mlp = jnp.sum(grad_normed * hidden * second_scale, axis=0)

    state = {"kept": ()}

    def heads(lo, hi, pieces):
        if lo == 3:
            pieces = after(pieces, down_part)
        state["kept"] = retain_back(
            lo, pieces, attn_joined, decays, query, key, value, gate, scores, retained, state["kept"], wide
        )
        if lo > 0:
            return state["kept"]
        act = after(inner_act, pieces)
        state["mlp"] = project(act, ff_joined, 2, wide)
        return state["kept"], state["mlp"]

    grad_wide, attn_grad_all = spread(grad_hidden.astype(bf16), count, heads)
    grad_out = rows_grad(gated, attn_grad_all, wide)
    out_part = sum_depth(grad_out)

    own_grad, others_grad = places_grad(me_scalar, attn_all, after(grad_wide, grad_out), depth)

    def back_terms(done):
        return project_back(after(grad_wide, (done, ff_part)), attn_joined, dk, dv)

    mlp_added, _, attn_terms = fold([(0, *state["mlp"])], count, lambda _: others_grad, back_terms)
    others_part = sum_depth(others_grad)
    output = (valid_rows * (hidden + mlp_added)).astype(bf16)
    if shard % 128 == 0:
        sums = trade(cut_sums(me_scalar, ff_part, (down_part, out_part)), count)
    else:
        sums = out_part
    grad_normed_attn, *_ = fold([(0, *attn_terms)], count, lambda _: mlp_added, lambda _: sums)
    own_grad = after(own_grad, grad_normed_attn)
    own_part = sum_depth(own_grad)
    gain_term_attn = jnp.sum(grad_normed_attn * input_rows * first_scale, axis=0)
    scaled_first = grad_normed_attn * gain_first
    tokens_grad = grad_hidden + first_scale * (
        scaled_first
        - input_rows
        * (first_scale * first_scale)
        * jnp.mean(input_rows * scaled_first, axis=-1, keepdims=True)
    )
    tokens_grad = tokens_grad.astype(bf16)

    def back_columns(block, widths):
        cuts = [lax.dynamic_slice_in_dim(block, (me ^ k) * shard, shard, 0).astype(bf16) for k in range(PLANE)]
        return place_columns(me_scalar, trade(cuts, count), widths)

    def back_rows_of(block):
        cuts = [lax.dynamic_slice_in_dim(block, (me ^ k) * shard, shard, 1).astype(bf16) for k in range(PLANE)]
        return place_rows(me_scalar, trade(cuts, count))

    if shard % 128 == 0:
        ffgate_sum, ffup_sum, down_sum, out_sum = place_sums(me_scalar, sums, (inner, inner), (inner, dv))
    else:
        down_sum, out_sum = back_rows_of(down_part), back_rows_of(out_part)
        ffgate_sum, ffup_sum = back_columns(ff_part, (inner, inner))
    others_part = after(others_part, (tokens_grad, output))
    blocks = [hop(others_part[k * shard : (k + 1) * shard], k + 1, count) for k in range(PLANE - 1)]
    gain_terms = jnp.stack([gain_term_attn, gain_term_mlp])
    bit = count // 2
    while bit >= 1:
        side = (place // bit) % 2
        cut = gain_terms.reshape(2, 2, -1)
        kept = lax.dynamic_index_in_dim(cut, side, 1, keepdims=False)
        sent = lax.dynamic_index_in_dim(cut, 1 - side, 1, keepdims=False)
        gain_terms = kept + hop(sent, bit, count)
        bit //= 2
    cut = after(gain_terms, blocks).reshape(2, 2, -1)
    kept = lax.dynamic_index_in_dim(cut, core, 1, keepdims=False)
    sent = lax.dynamic_index_in_dim(cut, 1 - core, 1, keepdims=False)
    gain_terms = kept + swap(sent)
    early = output, tokens_grad, gain_terms, down_sum, ffgate_sum, ffup_sum, out_sum
    begun = place_columns(me_scalar, blocks, (dv, dv, dk, dk), (1, 2, 3))
    own_part = after(own_part, (begun, early))
    value_sum, gate_sum, query_sum, key_sum = place_columns(me_scalar, [own_part], (dv, dv, dk, dk), (0,), begun)

    return (
        output,
        tokens_grad,
        query_sum,
        key_sum,
        value_sum,
        gate_sum,
        out_sum,
        ffgate_sum,
        ffup_sum,
        down_sum,
        gain_terms[0],
        gain_terms[1],
    )


def solution(mesh):
    return jax.shard_map(
        on_device,
        mesh=mesh,
        in_specs=(
            P(("dp", "tensor"), None),
            P("dp"),
            P("dp", "tensor"),
            P("dp", "tensor"),
            P("dp", "tensor"),
            P("dp", "tensor"),
            P("tensor", "dp"),
            P("dp", "tensor"),
            P("dp", "tensor"),
            P("tensor", "dp"),
            P("dp"),
            P("dp"),
            P(("dp", "tensor"), None),
        ),
        out_specs=(
            P(("dp", "tensor"), None),
            P(("dp", "tensor"), None),
            P("dp", "tensor"),
            P("dp", "tensor"),
            P("dp", "tensor"),
            P("dp", "tensor"),
            P("tensor", "dp"),
            P("dp", "tensor"),
            P("dp", "tensor"),
            P("tensor", "dp"),
            P(("dp", "tensor")),
            P(("dp", "tensor")),
        ),
        check_vma=False,
    )
```
